32 devices in a mesh: bx: 4 (over z), by: 8 (over y, x, core).
Axes of the slice: x: 2, y: 2, z: 4, core: 2. Of those that a mesh axis runs over, the one named last changes fastest.
Arguments:
- positions: float32 [3, 4096], P(None, ('bx', 'by')), may hold values from 0 to 8, as said below
- tangent: float32 [3, 4096], P(None, ('bx', 'by')), may hold values from -6 to 6
- embedding: float32 [4096, 256], P(('bx', 'by')), may hold values from -6 to 6
- counts: int32 [32], P(('bx', 'by')), may hold values from 64 to 128, as said below
- neighbours: int32 [32, 4096], P(None, ('bx', 'by')), may hold values from 0 to 191, as said below
- send_rows: int32 [32, 64], P(('bx', 'by')), may hold values from 0 to 127
- w_one_in: float32 [256, 256], replicated, may hold values from -0.375 to 0.375
- w_one_out: float32 [256, 512], replicated, may hold values from -0.375 to 0.375
- filter_one: float32 [20, 512], replicated, may hold values from -0.3125 to 0.3125
- w_left: float32 [256, 256], replicated, may hold values from -0.375 to 0.375
- w_right: float32 [256, 256], replicated, may hold values from -0.375 to 0.375
- w_two_in: float32 [256, 256], replicated, may hold values from -0.375 to 0.375
- w_two_out: float32 [256, 256], replicated, may hold values from -0.375 to 0.375
- filter_two: float32 [20, 256], replicated, may hold values from -0.3125 to 0.3125
- w_hidden: float32 [256, 256], replicated, may hold values from -0.375 to 0.375
- w_energy: float32 [256], replicated, may hold values from -0.375 to 0.375
Outputs:
- forces: float32 [3, 4096], P(None, ('bx', 'by'))
- hessian_tangent: float32 [3, 4096], P(None, ('bx', 'by'))
The draws below stay inside these ranges and needn't reach their ends.
Inputs may be any that keep to these rules, and one draw needn't show every extreme that they name: The live atoms of a brick are its first counts rows; every count is a multiple of 32; some brick holds 128 live atoms and some 128 // 2. `neighbours`: the 32 slots of an atom are distinct; each is a live row of its own brick other than the atom's own row, or a slot of a neighbouring brick that exists in the sheet. `positions`: atom n lies within one unit of its brick's indices along x and y, with the third coordinate in [0, 0.3).
All inputs are finite; a program needn't handle non-finite values.
Results may differ from the reference program's by a relative error of at most 0.0003.
Values sent between devices are 32-bit elements; how exact they have to be, the bound alone decides.
No kernel may reach another device: no remote copies, remote signals or barrier semaphores. Data moves between devices by JAX's collectives and lax.ppermute only.
A program may use at most 192 MiB of HBM per device.

```python
import math
import jax
import jax.numpy as jnp
from jax import lax

F = 256
NR = 20
K = 32
ROWS = 128
GH = 8
BRICKS_X = 4
BRICKS_Y = 8
BRICKS = 32
ATOMS = 4096


offsets = ((-1, -1), (-1, 0), (-1, 1), (0, -1), (0, 1), (1, -1), (1, 0), (1, 1))


def shared_counts(key):
    levels = jax.random.randint(jax.random.fold_in(key, 11), (BRICKS,), 2, 5)
    chosen = jax.random.randint(jax.random.fold_in(key, 12), (), 0, BRICKS)
    second = (chosen + 1 + jax.random.randint(jax.random.fold_in(key, 13), (), 0, BRICKS - 1)) % BRICKS
    brick_order = jnp.arange(BRICKS)
    levels = jnp.where(brick_order == chosen, 4, levels)
    levels = jnp.where(brick_order == second, 2, levels)
    return (levels * (ROWS // 4)).astype(jnp.int32)


def draw_counts(key, part):
    return shared_counts(key)


def draw_send_rows(key, part):
    counts = shared_counts(key)
    raw_scores = jax.random.randint(jax.random.fold_in(key, 21), (BRICKS, 8, ROWS), 0, 2 ** 19)
    row_order = jnp.arange(ROWS)
    scores = raw_scores * ROWS + row_order[None, None, :] + jnp.where(row_order[None, None, :] < counts[:, None, None], 0, 2 ** 30)
    picked = jnp.argsort(scores, axis=-1)[:, :, :GH]
    return picked.reshape(BRICKS, 8 * GH).astype(jnp.int32)


def draw_neighbours(key, part):
    counts = shared_counts(key)
    table = ROWS + 8 * GH
    slot_order = jnp.arange(table)
    row_order = jnp.arange(ROWS)
    brick_order = jnp.arange(BRICKS)
    along_x = brick_order // BRICKS_Y
    along_y = brick_order % BRICKS_Y
    shift_x = jnp.array([target[0] for target in offsets])
    shift_y = jnp.array([target[1] for target in offsets])
    source_x = along_x[:, None] + shift_x[None, :]
    source_y = along_y[:, None] + shift_y[None, :]
    exists = (source_x >= 0) & (source_x < BRICKS_X) & (source_y >= 0) & (source_y < BRICKS_Y)
    ghost_group = jnp.clip((slot_order - ROWS) // GH, 0, 7)
    ghost_valid = (slot_order[None, :] >= ROWS) & exists[:, ghost_group]
    own_valid = (slot_order[None, None, :] < counts[:, None, None]) & (slot_order[None, None, :] != row_order[None, :, None])
    valid = own_valid | ghost_valid[:, None, :]
    raw_scores = jax.random.randint(jax.random.fold_in(key, 31), (BRICKS, ROWS, table), 0, 2 ** 17)
    ghost_penalty = jnp.where(slot_order >= ROWS, 2 ** 15, 0)
    scores = (raw_scores + ghost_penalty[None, None, :]) * table + slot_order[None, None, :] + jnp.where(valid, 0, 2 ** 30)
    picked = jnp.argsort(scores, axis=-1)[:, :, :K]
    return jnp.transpose(picked, (2, 0, 1)).reshape(K, BRICKS * ROWS).astype(jnp.int32)


def draw_positions(key, part):
    atom_order = jnp.arange(ATOMS)
    brick_of = atom_order // ROWS
    base_x = (brick_of // BRICKS_Y).astype(jnp.float32)
    base_y = (brick_of % BRICKS_Y).astype(jnp.float32)
    within = jax.random.uniform(key, (3, ATOMS), jnp.float32)
    return jnp.stack([base_x + within[0], base_y + within[1], 0.3 * within[2]])


def shard_levels(own_key, dims, cuts, least, high):
    loudness = 1.0
    for position, shards_of in cuts:
        steps = jax.random.uniform(jax.random.fold_in(jax.random.fold_in(own_key, 6), position), (shards_of,), jnp.float32, least / len(cuts), high / len(cuts))
        loudness = loudness * jnp.repeat(jnp.exp(steps), dims[position] // shards_of).reshape((-1,) + (1,) * (len(dims) - 1 - position))
    return loudness


def scatter_about(own_key, shape, deviation, reach, shards=(), kind=jnp.bfloat16):
    values = deviation * jax.random.normal(own_key, shape, jnp.float32)
    if shards:
        values = values * shard_levels(own_key, shape, shards, -0.22, 0.18)
    return jnp.clip(values, -reach, reach).astype(kind)


def setup_inputs(seed: int = 0) -> dict:
    streams_of = jax.random.split(jax.random.key(seed), 17)
    return {
        "positions": draw_positions(jax.random.fold_in(streams_of[16], 71), 0),
        "tangent": scatter_about(streams_of[1], (3, ATOMS), 1.0, 6.0, ((1, 32),), jnp.float32),
        "embedding": scatter_about(streams_of[2], (ATOMS, F), 1.0, 6.0, ((0, 32),), jnp.float32),
        "counts": draw_counts(jax.random.fold_in(streams_of[16], 71), 0),
        "neighbours": draw_neighbours(jax.random.fold_in(streams_of[16], 71), 0),
        "send_rows": draw_send_rows(jax.random.fold_in(streams_of[16], 71), 0),
        "w_one_in": scatter_about(streams_of[6], (F, F), F ** -0.5, 0.375, (), jnp.float32),
        "w_one_out": scatter_about(streams_of[7], (F, 2 * F), F ** -0.5, 0.375, (), jnp.float32),
        "filter_one": scatter_about(streams_of[8], (NR, 2 * F), (NR * NR) ** -0.5, 0.3125, (), jnp.float32),
        "w_left": scatter_about(streams_of[9], (F, F), F ** -0.5, 0.375, (), jnp.float32),
        "w_right": scatter_about(streams_of[10], (F, F), F ** -0.5, 0.375, (), jnp.float32),
        "w_two_in": scatter_about(streams_of[11], (F, F), F ** -0.5, 0.375, (), jnp.float32),
        "w_two_out": scatter_about(streams_of[12], (F, F), F ** -0.5, 0.375, (), jnp.float32),
        "filter_two": scatter_about(streams_of[13], (NR, F), (NR * NR) ** -0.5, 0.3125, (), jnp.float32),
        "w_hidden": scatter_about(streams_of[14], (F, F), F ** -0.5, 0.375, (), jnp.float32),
        "w_energy": scatter_about(streams_of[15], (F,), F ** -0.5, 0.375, (), jnp.float32),
    }


highest = lax.Precision.HIGHEST
cutoff_radius = 3.0
softening = 0.01
offsets = ((-1, -1), (-1, 0), (-1, 1), (0, -1), (0, 1), (1, -1), (1, 0), (1, 1))

def project_rows(features, w_inner, w_outer):
    inner = jax.nn.silu(jnp.dot(features, w_inner, precision=highest))
    return jnp.dot(inner, w_outer, precision=highest)

def geometry(pos_table, own_lists, basis_count):
    own_rows = own_lists.shape[1]
    centre = pos_table[:, :own_rows]
    others = jnp.take(pos_table, own_lists, axis=1)
    offset = others - centre[:, None, :]
    distance = jnp.sqrt(lax.optimization_barrier(jnp.sum(offset * offset, axis=0)) + softening)
    direction = offset / distance[None]
    orders = jnp.arange(1, basis_count + 1).astype(distance.dtype)
    radial = jnp.sin(orders[:, None, None] * (math.pi / cutoff_radius) * distance[None]) / distance[None]
    envelope = 0.5 * (jnp.cos(math.pi / cutoff_radius * distance) + 1.0)
    return (radial, envelope, direction)

def edge_weights(radial, envelope, filter_table):
    mixed = jnp.einsum('qkr,qc->krc', radial, filter_table, precision=highest)
    return mixed * envelope[:, :, None]

def first_layer(pos_table, phi_table, embed_own, own_lists, filter_one, w_left, w_right):
    radial, envelope, direction = geometry(pos_table, own_lists, filter_one.shape[0])
    scale_edges = 1.0 / math.sqrt(own_lists.shape[0])
    message = jnp.take(phi_table, own_lists, axis=0) * edge_weights(radial, envelope, filter_one)
    channels = embed_own.shape[1]
    scalar_part = scale_edges * lax.optimization_barrier(jnp.sum(message[:, :, :channels], axis=0))
    vector_part = scale_edges * jnp.einsum('ckr,krf->crf', direction, message[:, :, channels:], precision=highest)
    left_map = jnp.einsum('crf,fg->crg', vector_part, w_left, precision=highest)
    right_map = jnp.einsum('crf,fg->crg', vector_part, w_right, precision=highest)
    return embed_own + scalar_part + lax.optimization_barrier(jnp.sum(left_map * right_map, axis=0))

def second_layer(pos_table, phi_table, state_own, own_lists, live_rows, filter_two, w_hidden, w_energy):
    geometry_parts = geometry(pos_table, own_lists, filter_two.shape[0])
    scale_edges = 1.0 / math.sqrt(own_lists.shape[0])
    weighted = jnp.take(phi_table, own_lists, axis=0) * edge_weights(geometry_parts[0], geometry_parts[1], filter_two)
    message = scale_edges * lax.optimization_barrier(jnp.sum(weighted, axis=0))
    hidden_rows = jax.nn.silu(jnp.dot(state_own + message, w_hidden, precision=highest))
    return jnp.sum(live_rows * jnp.dot(hidden_rows, w_energy, precision=highest))

def reference(positions, tangent, embedding, counts, neighbours, send_rows, w_one_in, w_one_out, filter_one, w_left, w_right, w_two_in, w_two_out, filter_two, w_hidden, w_energy):
    bricks = BRICKS_X * BRICKS_Y
    float_type = positions.dtype
    brick_ids = jnp.arange(bricks, dtype=jnp.int32)
    along_x = brick_ids // BRICKS_Y
    along_y = brick_ids % BRICKS_Y
    ghost_ids = []
    ghost_inside = []
    for number, target in enumerate(offsets):
        source_x = along_x + target[0]
        source_y = along_y + target[1]
        inside = (source_x >= 0) & (source_x < BRICKS_X) & (source_y >= 0) & (source_y < BRICKS_Y)
        source = jnp.clip(source_x, 0, BRICKS_X - 1) * BRICKS_Y + jnp.clip(source_y, 0, BRICKS_Y - 1)
        rows_sent = send_rows[source][:, (7 - number) * GH:(8 - number) * GH]
        ghost_ids.append((source[:, None] * ROWS + rows_sent).astype(jnp.int32))
        ghost_inside.append(jnp.broadcast_to(inside[:, None], (bricks, GH)))
    own_ids = (brick_ids[:, None] * ROWS + jnp.arange(ROWS, dtype=jnp.int32)[None, :]).astype(jnp.int32)
    table_ids = jnp.concatenate([own_ids] + ghost_ids, 1).astype(jnp.int32)
    table_inside = jnp.concatenate([jnp.ones((bricks, ROWS), dtype=bool)] + ghost_inside, 1).astype(float_type)

    def brick_tables(brick_index):
        slot_atoms = table_ids[brick_index]
        inside_mask = table_inside[brick_index]
        pos_table = positions[:, slot_atoms] * inside_mask[None]
        tan_table = tangent[:, slot_atoms] * inside_mask[None]
        own_lists = lax.dynamic_slice_in_dim(neighbours, (brick_index * ROWS).astype(jnp.int32), ROWS, 1)
        return (slot_atoms, inside_mask, pos_table, tan_table, own_lists)

    def first_inputs(brick_index):
        slot_atoms, inside_mask, pos_table, tan_table, own_lists = brick_tables(brick_index)
        phi_table = project_rows(embedding[slot_atoms], w_one_in, w_one_out) * inside_mask[:, None]
        embed_own = lax.dynamic_slice_in_dim(embedding, (brick_index * ROWS).astype(jnp.int32), ROWS, 0)

        def first_section(pos_arg):
            return first_layer(pos_arg, phi_table, embed_own, own_lists, filter_one, w_left, w_right)
        return (first_section, pos_table, tan_table)

    def first_pass(brick_index):
        first_section, pos_table, tan_table = first_inputs(brick_index)
        return jax.jvp(first_section, (pos_table,), (tan_table,))
    node_state, state_tangent = lax.map(first_pass, brick_ids)
    node_state = node_state.reshape(bricks * ROWS, -1)
    state_tangent = state_tangent.reshape(bricks * ROWS, -1)

    def second_pass(brick_index):
        slot_atoms, inside_mask, pos_table, tan_table, own_lists = brick_tables(brick_index)
        state_table = node_state[slot_atoms] * inside_mask[:, None]
        tangent_table = state_tangent[slot_atoms] * inside_mask[:, None]
        live_rows = (jnp.arange(ROWS) < counts[brick_index]).astype(float_type)

        def second_section(pos_arg, table_arg):
            phi_table = project_rows(table_arg, w_two_in, w_two_out)
            return second_layer(pos_arg, phi_table, table_arg[:ROWS], own_lists, live_rows, filter_two, w_hidden, w_energy)
        return jax.jvp(jax.grad(second_section, argnums=(0, 1)), (pos_table, state_table), (tan_table, tangent_table))
    grads_second, tangents_second = lax.map(second_pass, brick_ids)
    flat_ids = table_ids.reshape(-1)
    inside_flat = table_inside.reshape(-1)
    channels = node_state.shape[1]

    def scatter_positions(per_brick):
        moved = jnp.transpose(per_brick, (1, 0, 2)).reshape(3, -1) * inside_flat[None]
        return jnp.zeros((3, bricks * ROWS), float_type).at[:, flat_ids].add(moved)

    def scatter_states(per_brick):
        moved = per_brick.reshape(-1, channels) * inside_flat[:, None]
        return jnp.zeros((bricks * ROWS, channels), float_type).at[flat_ids].add(moved)
    pos_grad = scatter_positions(grads_second[0])
    pos_grad_tangent = scatter_positions(tangents_second[0])
    state_cot = scatter_states(grads_second[1])
    state_cot_tangent = scatter_states(tangents_second[1])

    def third_pass(brick_index):
        first_section, pos_table, tan_table = first_inputs(brick_index)
        start = (brick_index * ROWS).astype(jnp.int32)
        own_cot = lax.dynamic_slice_in_dim(state_cot, start, ROWS, 0)
        own_cot_tangent = lax.dynamic_slice_in_dim(state_cot_tangent, start, ROWS, 0)

        def pull_first(pos_arg, cot_arg):
            pullback = jax.vjp(first_section, pos_arg)[1]
            return pullback(cot_arg)[0]
        return jax.jvp(pull_first, (pos_table, own_cot), (tan_table, own_cot_tangent))
    grads_first, tangents_first = lax.map(third_pass, brick_ids)
    pos_grad = pos_grad + scatter_positions(grads_first)
    pos_grad_tangent = pos_grad_tangent + scatter_positions(tangents_first)
    return (-pos_grad, -pos_grad_tangent)
```

```python
import functools
import math

import jax
import jax.numpy as jnp
from jax import lax
from jax.experimental import pallas as pl
from jax.experimental.pallas import tpu as pltpu
from jax.sharding import PartitionSpec as P

f32 = jnp.float32
bf16 = jnp.bfloat16
cutoff_radius = 3.0
softening = 0.01
wave = math.pi / cutoff_radius
offsets = ((-1, -1), (-1, 0), (-1, 1), (0, -1), (0, 1), (1, -1), (1, 0), (1, 1))
lanes = 128
wide = 256
row_block = 32
nn_dims = (((1,), (0,)), ((), ()))
nt_dims = (((1,), (1,)), ((), ()))

U, UD, DD, P0, P1, P2, SN, CS, RS, RC, RI = 0, 3, 6, 7, 8, 9, 10, 11, 12, 13, 14
geo_slots = 15


def split(value):
    high = value.astype(bf16)
    return high, (value - high.astype(f32)).astype(bf16)


def mxu(left, right, dims=nn_dims):
    return lax.dot_general(left, right, dims, preferred_element_type=f32)


def dot3(left, right, dims=nn_dims):
    lh, ll = split(left)
    rh, rl = split(right)
    return mxu(lh, rh, dims) + mxu(ll, rh, dims) + mxu(lh, rl, dims)


def sigmoid(value):
    return 1.0 / (1.0 + jnp.exp(-jnp.maximum(value, -80.0)))


def silu_parts(value):
    gate = sigmoid(value)
    first = gate * (1.0 + value * (1.0 - gate))
    second = gate * (1.0 - gate) * (2.0 + value * (1.0 - 2.0 * gate))
    return value * gate, first, second


def sin_cos(theta):
    t = jnp.minimum(theta, 6.0) * 0.25
    x = t * t
    s = -1.0 / 39916800.0 + x * (1.0 / 6227020800.0)
    s = 1.0 / 362880.0 + x * s
    s = -1.0 / 5040.0 + x * s
    s = 1.0 / 120.0 + x * s
    s = -1.0 / 6.0 + x * s
    s = t + t * x * s
    c = 1.0 / 479001600.0 - x * (1.0 / 87178291200.0)
    c = -1.0 / 3628800.0 + x * c
    c = 1.0 / 40320.0 + x * c
    c = -1.0 / 720.0 + x * c
    c = 1.0 / 24.0 + x * c
    c = -0.5 + x * c
    c = 1.0 + x * c
    s, c = 2.0 * s * c, 1.0 - 2.0 * s * s
    return 2.0 * s * c, 1.0 - 2.0 * s * s


def fill_geometry(geo, first, second, mask_at, height, members):
    repeats = wide // members
    group = lax.broadcasted_iota(jnp.int32, (1, wide), 1) // members
    for start in range(0, height, row_block):
        rows = pl.ds(start, row_block)
        off = [first(i, start) - second(i, start) for i in range(3)]
        move = [first(i + 3, start) - second(i + 3, start) for i in range(3)]
        square = off[0] * off[0] + off[1] * off[1] + off[2] * off[2] + softening
        inverse = lax.rsqrt(square)
        inverse = inverse * (1.5 - 0.5 * square * inverse * inverse)
        theta = wave * (square * inverse)
        unit = [o * inverse for o in off]
        speed = unit[0] * move[0] + unit[1] * move[1] + unit[2] * move[2]
        for i in range(3):
            geo[U + i, rows, :] = unit[i]
            geo[UD + i, rows, :] = (move[i] - unit[i] * speed) * inverse
        sn, cs = sin_cos(theta)
        g0 = (0.5 * cs + 0.5) * inverse
        g1 = ((-0.5 * wave) * sn - g0) * inverse
        g2 = ((-0.5 * wave * wave) * cs - 2.0 * g1) * inverse
        mask = mask_at(start)
        geo[DD, rows, :] = speed
        geo[P0, rows, :] = mask * g0
        geo[P1, rows, :] = mask * g1
        geo[P2, rows, :] = mask * g2
        geo[RI, rows, :] = inverse
        turn_s, turn_c = sn, cs
        state_s, state_c = sn, cs
        for i in range(1, repeats):
            turn_s, turn_c = turn_s * cs + turn_c * sn, turn_c * cs - turn_s * sn
            state_s = jnp.where(group >= i, turn_s, state_s)
            state_c = jnp.where(group >= i, turn_c, state_c)
        geo[SN, rows, :] = state_s
        geo[CS, rows, :] = state_c
        geo[RS, rows, :] = turn_s
        geo[RC, rows, :] = turn_c


def order_factor(step, members):
    repeats = wide // members
    group = lax.broadcasted_iota(jnp.int32, (1, wide), 1) // members
    return (group + (step * repeats + 1)).astype(f32) * wave


def rotate(geo, rows, s, c):
    rs = geo[RS, rows, :]
    rc = geo[RC, rows, :]
    geo[SN, rows, :] = s * rc + c * rs
    geo[CS, rows, :] = c * rc - s * rs


def listed(nbr_ref, start, members):
    slot = lax.broadcasted_iota(jnp.int32, (members, lanes), 0) + start
    found = nbr_ref[0:1, :] == slot
    for k in range(1, nbr_ref.shape[0]):
        found = found | (nbr_ref[k : k + 1, :] == slot)
    return jnp.where(found, 1.0, 0.0).astype(f32)


def stack_coords(box, pos_ref, tan_ref):
    box[...] = jnp.zeros_like(box)
    box[0:3, :] = pos_ref[...]
    box[3:6, :] = tan_ref[...]


def geometry_by_atom(geo, box, wbox, ghost_ref, nbr_ref, own_rows, ghost):
    columns = box[...].T
    if ghost:
        members = ghost_ref.shape[0]
        repeats = wide // members
        table = jnp.concatenate([ghost_ref[...]] * repeats, 0).T
        mask = listed(nbr_ref, own_rows, members)
    else:
        members = own_rows
        repeats = wide // members
        table = jnp.concatenate([box[...]] * repeats, 1)
        mask = listed(nbr_ref, 0, members)
    wbox[...] = jnp.concatenate([mask] * repeats, 0).T
    fill_geometry(
        geo,
        lambda i, start: table[i : i + 1, :],
        lambda i, start: columns[start : start + row_block, i : i + 1],
        lambda start: wbox[start : start + row_block, :],
        own_rows,
        members,
    )
    return members


def geometry_by_slot(geo, box, wbox, ghost_ref, nbr_ref, own_rows, ghost):
    repeats = wide // own_rows
    centre = jnp.concatenate([box[...]] * repeats, 1)
    if ghost:
        height = ghost_ref.shape[0]
        columns = ghost_ref[...]
        mask = listed(nbr_ref, own_rows, height)
    else:
        height = own_rows
        columns = box[...].T
        mask = listed(nbr_ref, 0, height)
    wbox[0:height, :] = jnp.concatenate([mask] * repeats, 1)
    fill_geometry(
        geo,
        lambda i, start: columns[start : start + row_block, i : i + 1],
        lambda i, start: centre[i : i + 1, :],
        lambda start: wbox[start : start + row_block, :],
        height,
        own_rows,
    )
    return height


def scaled_rows(high, low, filter_ref, value, step, columns, scale):
    members = value.shape[0]
    for i in range(wide // members):
        row = filter_ref[pl.ds(step * (wide // members) + i, 1), columns] * scale
        h, l = split(row * value)
        high[i * members : (i + 1) * members, :] = h
        low[i * members : (i + 1) * members, :] = l


def put_split(high, low, start, value):
    h, l = split(value)
    high[start : start + value.shape[0], :] = h
    low[start : start + value.shape[0], :] = l


def first_messages(acc, geo, ah, al, gh, gl, vh, vl, phi_ref, filter_ref, members, scale, fresh):
    height = geo.shape[1]
    channels = phi_ref.shape[1] // 2
    if fresh:
        acc[...] = jnp.zeros_like(acc)

    def chunk(step, _):
        factor = order_factor(step, members)
        scaled_rows(gh, gl, filter_ref, phi_ref[:, :channels], step, slice(0, channels), scale)
        scaled_rows(
            vh, vl, filter_ref, phi_ref[:, channels:], step, slice(channels, 2 * channels), scale
        )
        for start in range(0, height, row_block):
            rows = pl.ds(start, row_block)
            s, c = geo[SN, rows, :], geo[CS, rows, :]
            p0 = geo[P0, rows, :]
            b = p0 * s
            bd = (geo[P1, rows, :] * s + factor * (p0 * c)) * geo[DD, rows, :]
            put_split(ah, al, start, b)
            put_split(ah, al, height + start, bd)
            for i in range(3):
                unit = geo[U + i, rows, :]
                put_split(ah, al, (2 + i) * height + start, unit * b)
                put_split(ah, al, (5 + i) * height + start, geo[UD + i, rows, :] * b + unit * bd)
            rotate(geo, rows, s, c)
        top = 2 * height
        acc[:top, :] += (
            mxu(ah[:top, :], gh[...]) + mxu(al[:top, :], gh[...]) + mxu(ah[:top, :], gl[...])
        )
        acc[top:, :] += (
            mxu(ah[top:, :], vh[...]) + mxu(al[top:, :], vh[...]) + mxu(ah[top:, :], vl[...])
        )
        return 0

    lax.fori_loop(0, filter_ref.shape[0] * members // wide, chunk, 0)


def second_messages(acc, geo, ah, al, gh, gl, vh, vl, value, dots, filter_ref, members, scale):
    height = acc.shape[0] // 2

    def chunk(step, _):
        factor = order_factor(step, members)
        scaled_rows(gh, gl, filter_ref, value(), step, slice(None), scale)
        scaled_rows(vh, vl, filter_ref, dots(), step, slice(None), scale)
        for start in range(0, height, row_block):
            rows = pl.ds(start, row_block)
            s, c = geo[SN, rows, :], geo[CS, rows, :]
            p0 = geo[P0, rows, :]
            put_split(ah, al, start, p0 * s)
            put_split(
                ah,
                al,
                height + start,
                (geo[P1, rows, :] * s + factor * (p0 * c)) * geo[DD, rows, :],
            )
            rotate(geo, rows, s, c)
        top = 2 * height
        acc[...] += (
            mxu(ah[:top, :], gh[...]) + mxu(al[:top, :], gh[...]) + mxu(ah[:top, :], gl[...])
        )
        acc[height:, :] += (
            mxu(ah[:height, :], vh[...])
            + mxu(al[:height, :], vh[...])
            + mxu(ah[:height, :], vl[...])
        )
        return 0

    lax.fori_loop(0, filter_ref.shape[0] * members // wide, chunk, 0)


def neighbour_id(target, sizes):
    along = lax.axis_index("bx") + target[0]
    across = lax.axis_index("by") + target[1]
    inside = (along >= 0) & (along < sizes[0]) & (across >= 0) & (across < sizes[1])
    device = jnp.clip(along, 0, sizes[0] - 1) * sizes[1] + jnp.clip(across, 0, sizes[1] - 1)
    return device, inside


def send_gathered(out_ref, table, send_ref, sizes):
    count = out_ref.shape[1]
    for number, target in enumerate(offsets):
        device, inside = neighbour_id(target, sizes)

        @pl.when(inside)
        def _():
            for p in range(count):
                index = send_ref[0, number * count + p]
                out_ref[device, p : p + 1, :] = table[pl.ds(index, 1), :]


def send_groups(out_ref, table, sizes):
    count = out_ref.shape[1]
    for number, target in enumerate(offsets):
        device, inside = neighbour_id(target, sizes)

        @pl.when(inside)
        def _():
            out_ref[device] = table[number * count : (number + 1) * count, :]


def receive_groups(table, in_ref, sizes):
    count = in_ref.shape[1]
    table[...] = jnp.zeros_like(table)
    for number, target in enumerate(offsets):
        device, inside = neighbour_id(target, sizes)

        @pl.when(inside)
        def _():
            table[number * count : (number + 1) * count, :] = in_ref[device]


def add_returned(table, in_ref, send_ref, sizes):
    count = in_ref.shape[1]
    for number, target in enumerate(offsets):
        device, inside = neighbour_id(target, sizes)

        @pl.when(inside)
        def _():
            for p in range(count):
                index = send_ref[0, number * count + p]
                table[pl.ds(index, 1), :] += in_ref[device, p : p + 1, :]


def pack_kernel(sizes, pos, tan, emb, send, out, box, table):
    channels = emb.shape[1]
    stack_coords(box, pos, tan)
    table[:, :channels] = emb[...]
    table[:, channels:] = box[...].T
    send_gathered(out, table, send, sizes)


def first_own_kernel(
    scale, pos, tan, emb, nbr, w_in, w_out, filt, acc, phi, box, wbox, geo, ah, al, gh, gl, vh, vl
):
    stack_coords(box, pos, tan)
    phi[...] = dot3(silu_parts(dot3(emb[...], w_in[...]))[0], w_out[...])
    members = geometry_by_atom(geo, box, wbox, None, nbr, pos.shape[1], False)
    first_messages(acc, geo, ah, al, gh, gl, vh, vl, phi, filt, members, scale, True)


def first_ghost_kernel(
    sizes,
    scale,
    pos,
    tan,
    emb,
    nbr,
    send,
    w_in,
    w_out,
    filt,
    w_left,
    w_right,
    w_two_in,
    w_two_out,
    partial,
    arrived,
    out,
    state,
    inner,
    maps,
    phi_two,
    phi_ghost,
    coords_ghost,
    box,
    wbox,
    geo,
    ah,
    al,
    gh,
    gl,
    vh,
    vl,
    acc,
    table,
):
    own_rows = pos.shape[1]
    channels = emb.shape[1]
    stack_coords(box, pos, tan)
    receive_groups(table, arrived, sizes)
    coords_ghost[...] = table[:, channels:]
    phi_ghost[...] = dot3(silu_parts(dot3(table[:, :channels], w_in[...]))[0], w_out[...])
    members = geometry_by_atom(geo, box, wbox, coords_ghost, nbr, own_rows, True)
    acc[...] = partial[...]
    first_messages(acc, geo, ah, al, gh, gl, vh, vl, phi_ghost, filt, members, scale, False)
    top = 2 * own_rows
    half = 3 * own_rows
    maps[0 : 2 * half, :] = dot3(acc[top:, :], w_left[...])
    maps[2 * half :, :] = dot3(acc[top:, :], w_right[...])
    total = emb[...] + acc[0:own_rows, :]
    moved = acc[own_rows:top, :]
    for i in range(3):
        a, b = i * own_rows, (i + 1) * own_rows
        left, left_dot = maps[a:b, :], maps[half + a : half + b, :]
        right = maps[2 * half + a : 2 * half + b, :]
        right_dot = maps[3 * half + a : 3 * half + b, :]
        total = total + left * right
        moved = moved + left_dot * right + left * right_dot
    state[0:own_rows, :] = total
    state[own_rows:, :] = moved
    inner[...] = dot3(state[...], w_two_in[...])
    value, slope, _ = silu_parts(inner[0:own_rows, :])
    state_two = jnp.concatenate([value, slope * inner[own_rows:, :]], 0)
    outer = dot3(state_two, w_two_out[...])
    phi_two[:, :channels] = outer[:own_rows]
    phi_two[:, channels:] = outer[own_rows:]
    send_gathered(out, phi_two, send, sizes)


def second_own_kernel(
    scale, pos, tan, nbr, filt, phi_two, acc, box, wbox, geo, ah, al, gh, gl, vh, vl
):
    channels = filt.shape[1]
    stack_coords(box, pos, tan)
    members = geometry_by_atom(geo, box, wbox, None, nbr, pos.shape[1], False)
    acc[...] = jnp.zeros_like(acc)
    second_messages(
        acc,
        geo,
        ah,
        al,
        gh,
        gl,
        vh,
        vl,
        lambda: phi_two[:, :channels],
        lambda: phi_two[:, channels:],
        filt,
        members,
        scale,
    )


def second_ghost_kernel(
    sizes,
    scale,
    pos,
    tan,
    nbr,
    counts,
    filt,
    coords_ghost,
    state,
    partial,
    w_hidden,
    w_energy,
    arrived,
    out,
    table,
    cot,
    box,
    wbox,
    geo,
    ah,
    al,
    gh,
    gl,
    vh,
    vl,
    acc,
    back,
):
    own_rows = pos.shape[1]
    channels = filt.shape[1]
    stack_coords(box, pos, tan)
    receive_groups(table, arrived, sizes)
    members = geometry_by_atom(geo, box, wbox, coords_ghost, nbr, own_rows, True)
    acc[...] = partial[...]
    second_messages(
        acc,
        geo,
        ah,
        al,
        gh,
        gl,
        vh,
        vl,
        lambda: table[:, :channels],
        lambda: table[:, channels:],
        filt,
        members,
        scale,
    )
    hidden = dot3(state[...] + acc[...], w_hidden[...])
    _, slope, bend = silu_parts(hidden[:own_rows])
    live = lax.broadcasted_iota(jnp.int32, (own_rows, 1), 0) < counts[0]
    weight = jnp.where(live, w_energy[...], 0.0)
    bars = jnp.concatenate([weight * slope, weight * bend * hidden[own_rows:]], 0)
    cot[...] = dot3(bars, w_hidden[...], nt_dims)
    height = geometry_by_slot(geo, box, wbox, coords_ghost, nbr, own_rows, True)
    table_cotangents(back, geo, ah, al, gh, gl, vh, vl, cot, filt, height, own_rows, scale)
    send_groups(out, back, sizes)


def table_cotangents(back, geo, ah, al, gh, gl, vh, vl, cot, filt, height, own_rows, scale):
    channels = filt.shape[1]
    back[...] = jnp.zeros_like(back)

    def chunk(step, _):
        factor = order_factor(step, own_rows)
        scaled_rows(gh, gl, filt, cot[0:own_rows, :], step, slice(None), scale)
        scaled_rows(vh, vl, filt, cot[own_rows:, :], step, slice(None), scale)
        for start in range(0, height, row_block):
            rows = pl.ds(start, row_block)
            s, c = geo[SN, rows, :], geo[CS, rows, :]
            p0 = geo[P0, rows, :]
            put_split(ah, al, start, p0 * s)
            put_split(
                ah,
                al,
                height + start,
                (geo[P1, rows, :] * s + factor * (p0 * c)) * geo[DD, rows, :],
            )
            rotate(geo, rows, s, c)
        top = 2 * height
        both = mxu(ah[:top, :], gh[...]) + mxu(al[:top, :], gh[...]) + mxu(ah[:top, :], gl[...])
        back[:, :channels] += both[:height]
        back[:, channels:] += (
            both[height:]
            + mxu(ah[:height, :], vh[...])
            + mxu(al[:height, :], vh[...])
            + mxu(ah[:height, :], vl[...])
        )
        return 0

    lax.fori_loop(0, filt.shape[0] * own_rows // wide, chunk, 0)


def folded(value, members):
    total = value[:, :lanes] + value[:, lanes:]
    if members < lanes:
        total = total + pltpu.roll(total, members, 1)
    return total


def second_pairs(geo, ah, al, gh, gl, vh, vl, value, dots, filt, members, scale, pair):
    height = geo.shape[1]
    pair[...] = jnp.zeros_like(pair)

    def chunk(step, _):
        factor = order_factor(step, members)
        scaled_rows(gh, gl, filt, value(), step, slice(None), scale)
        scaled_rows(vh, vl, filt, dots(), step, slice(None), scale)
        top = 2 * height
        both = (
            mxu(ah[:top, :], gh[...], nt_dims)
            + mxu(al[:top, :], gh[...], nt_dims)
            + mxu(ah[:top, :], gl[...], nt_dims)
        )
        plain = both[:height]
        dot = (
            both[height:]
            + mxu(ah[:height, :], vh[...], nt_dims)
            + mxu(al[:height, :], vh[...], nt_dims)
            + mxu(ah[:height, :], vl[...], nt_dims)
        )
        for start in range(0, height, row_block):
            rows = pl.ds(start, row_block)
            s, c = geo[SN, rows, :], geo[CS, rows, :]
            p0, p1 = geo[P0, rows, :], geo[P1, rows, :]
            b1 = p1 * s + factor * (p0 * c)
            b2 = geo[P2, rows, :] * s + factor * (2.0 * p1 * c - factor * (p0 * s))
            g = plain[start : start + row_block]
            pair[0, rows, :] += b1 * g
            pair[1, rows, :] += (b2 * geo[DD, rows, :]) * g + b1 * dot[start : start + row_block]
            rotate(geo, rows, s, c)
        return 0

    lax.fori_loop(0, filt.shape[0] * members // wide, chunk, 0)


def second_back_kernel(
    scale,
    pos,
    tan,
    nbr,
    filt,
    coords_ghost,
    phi_two,
    table,
    cot,
    back,
    pair_own,
    pair_ghost,
    box,
    wbox,
    geo,
    ah,
    al,
    gh,
    gl,
    vh,
    vl,
    pair,
):
    own_rows = pos.shape[1]
    channels = filt.shape[1]
    stack_coords(box, pos, tan)
    height = geometry_by_slot(geo, box, wbox, None, nbr, own_rows, False)
    table_cotangents(back, geo, ah, al, gh, gl, vh, vl, cot, filt, height, own_rows, scale)
    put_split(ah, al, 0, cot[...])
    for source, result, ghost in ((phi_two, pair_own, False), (table, pair_ghost, True)):
        members = geometry_by_atom(geo, box, wbox, coords_ghost, nbr, own_rows, ghost)
        second_pairs(
            geo,
            ah,
            al,
            gh,
            gl,
            vh,
            vl,
            lambda: source[:, :channels],
            lambda: source[:, channels:],
            filt,
            members,
            scale,
            pair,
        )
        result[0] = folded(pair[0], members)
        result[1] = folded(pair[1], members)


def first_pairs(geo, ch, cl, gh, gl, vh, vl, phi_ref, filt, members, scale, pair, cots):
    height = geo.shape[1]
    channels = phi_ref.shape[1] // 2
    pair[...] = jnp.zeros_like(pair)

    def chunk(step, _):
        factor = order_factor(step, members)
        scaled_rows(gh, gl, filt, phi_ref[:, :channels], step, slice(0, channels), scale)
        scaled_rows(vh, vl, filt, phi_ref[:, channels:], step, slice(channels, 2 * channels), scale)
        top = 2 * height
        cots[:top, :] = (
            mxu(ch[:top, :], gh[...], nt_dims)
            + mxu(cl[:top, :], gh[...], nt_dims)
            + mxu(ch[:top, :], gl[...], nt_dims)
        )
        cots[top:, :] = (
            mxu(ch[top:, :], vh[...], nt_dims)
            + mxu(cl[top:, :], vh[...], nt_dims)
            + mxu(ch[top:, :], vl[...], nt_dims)
        )
        for start in range(0, height, row_block):
            rows = pl.ds(start, row_block)
            s, c = geo[SN, rows, :], geo[CS, rows, :]
            p0, p1, dd = geo[P0, rows, :], geo[P1, rows, :], geo[DD, rows, :]
            b = p0 * s
            b1 = p1 * s + factor * (p0 * c)
            b2d = (geo[P2, rows, :] * s + factor * (2.0 * p1 * c - factor * b)) * dd
            b1d = b1 * dd
            along = cots[start : start + row_block, :]
            along_dot = cots[height + start : height + start + row_block, :]
            for i in range(3):
                at = (2 + i) * height + start
                g = cots[at : at + row_block, :]
                at = (5 + i) * height + start
                gd = cots[at : at + row_block, :]
                unit = geo[U + i, rows, :]
                along = along + unit * g
                along_dot = along_dot + unit * gd + geo[UD + i, rows, :] * g
                pair[2 + i, rows, :] += b * g
                pair[5 + i, rows, :] += b * gd + b1d * g
            pair[0, rows, :] += b1 * along
            pair[1, rows, :] += b2d * along + b1 * along_dot
            rotate(geo, rows, s, c)
        return 0

    lax.fori_loop(0, filt.shape[0] * members // wide, chunk, 0)


def offset_gradients(geo, pair, second, members, by_slot, by_atom):
    near = [folded(pair[i], members) for i in range(8)]
    height = geo.shape[1]
    units = [geo[U + i, :, :lanes] for i in range(3)]
    moves = [geo[UD + i, :, :lanes] for i in range(3)]
    inverse = geo[RI, :, :lanes]
    speed = geo[DD, :, :lanes]
    along = near[0] + second[0]
    along_dot = near[1] + second[1]
    turn, turn_dot = near[2:5], near[5:8]
    inner = units[0] * turn[0] + units[1] * turn[1] + units[2] * turn[2]
    inner_dot = sum(units[i] * turn_dot[i] + moves[i] * turn[i] for i in range(3))
    rate = speed * inverse
    lane = lax.broadcasted_iota(jnp.int32, (1, lanes), 1)
    sums = jnp.zeros((height, lanes), f32)
    for i in range(3):
        part = (turn[i] - units[i] * inner) * inverse
        grad = along * units[i] + part
        grad_dot = (
            along_dot * units[i]
            + along * moves[i]
            + (turn_dot[i] - moves[i] * inner - units[i] * inner_dot) * inverse
            - rate * part
        )
        for row, value in ((i, grad), (3 + i, grad_dot)):
            by_slot[row : row + 1, :] = jnp.sum(value, 0, keepdims=True)
            if members < lanes:
                value = jnp.where(lane < members, value, 0.0)
            sums = jnp.where(lane == row, -jnp.sum(value, 1, keepdims=True), sums)
    by_atom[...] = sums


def first_back_ghost_kernel(
    sizes,
    scale,
    pos,
    tan,
    nbr,
    send,
    filt,
    coords_ghost,
    phi_ghost,
    cot,
    inner,
    maps,
    back,
    pair_ghost,
    w_two_in,
    w_two_out,
    w_left,
    w_right,
    arrived,
    out,
    bars,
    by_atom,
    box,
    wbox,
    geo,
    ch,
    cl,
    gh,
    gl,
    vh,
    vl,
    pair,
    cots,
    total,
    by_slot,
):
    own_rows = pos.shape[1]
    channels = filt.shape[1] // 2
    stack_coords(box, pos, tan)
    total[...] = back[...]
    add_returned(total, arrived, send, sizes)
    outer = dot3(
        jnp.concatenate([total[:, :channels], total[:, channels:]], 0), w_two_out[...], nt_dims
    )
    _, slope, bend = silu_parts(inner[:own_rows, :])
    pulled = jnp.concatenate(
        [
            outer[:own_rows] * slope,
            outer[own_rows:] * slope + outer[:own_rows] * bend * inner[own_rows:, :],
        ],
        0,
    )
    bars[0 : 2 * own_rows, :] = cot[...] + dot3(pulled, w_two_in[...], nt_dims)
    half = 3 * own_rows
    bar, bar_dot = bars[0:own_rows, :], bars[own_rows : 2 * own_rows, :]
    for i in range(3):
        a, b = i * own_rows, (i + 1) * own_rows
        left, left_dot = maps[a:b, :], maps[half + a : half + b, :]
        right = maps[2 * half + a : 2 * half + b, :]
        right_dot = maps[3 * half + a : 3 * half + b, :]
        for_left = jnp.concatenate([bar * right, bar_dot * right + bar * right_dot], 0)
        for_right = jnp.concatenate([bar * left, bar_dot * left + bar * left_dot], 0)
        both = dot3(for_left, w_left[...], nt_dims) + dot3(for_right, w_right[...], nt_dims)
        at = (2 + i) * own_rows
        bars[at : at + own_rows, :] = both[:own_rows]
        at = (5 + i) * own_rows
        bars[at : at + own_rows, :] = both[own_rows:]
    put_split(ch, cl, 0, bars[...])
    members = geometry_by_atom(geo, box, wbox, coords_ghost, nbr, own_rows, True)
    first_pairs(geo, ch, cl, gh, gl, vh, vl, phi_ghost, filt, members, scale, pair, cots)
    by_slot[...] = jnp.zeros_like(by_slot)
    offset_gradients(geo, pair, pair_ghost, members, by_slot, by_atom)
    for target in offsets:
        device, inside = neighbour_id(target, sizes)

        @pl.when(inside)
        def _():
            out[device] = by_slot[...]


def first_back_own_kernel(
    scale,
    pos,
    tan,
    nbr,
    filt,
    phi_own,
    bars,
    pair_own,
    ghost_sums,
    result,
    box,
    wbox,
    geo,
    ch,
    cl,
    gh,
    gl,
    vh,
    vl,
    pair,
    cots,
    by_atom,
):
    own_rows = pos.shape[1]
    stack_coords(box, pos, tan)
    put_split(ch, cl, 0, bars[...])
    members = geometry_by_atom(geo, box, wbox, None, nbr, own_rows, False)
    first_pairs(geo, ch, cl, gh, gl, vh, vl, phi_own, filt, members, scale, pair, cots)
    result[...] = jnp.zeros_like(result)
    offset_gradients(geo, pair, pair_own, members, result, by_atom)
    result[...] += (by_atom[...] + ghost_sums[...]).T[0:8, :]


def finish_kernel(sizes, send, partial, arrived, forces, product, rows):
    count = send.shape[1] // 8
    own_rows = partial.shape[1]
    rows[...] = jnp.zeros_like(rows)
    lane = lax.broadcasted_iota(jnp.int32, (1, lanes), 1)
    for number, target in enumerate(offsets):
        device, inside = neighbour_id(target, sizes)

        @pl.when(inside)
        def _():
            shift = ((2 * number - 7) * count) % lanes
            moved = arrived[device]
            if shift:
                moved = pltpu.roll(moved, shift, 1)
            mine = (lane >= number * count) & (lane < (number + 1) * count)
            rows[...] += jnp.where(mine, moved, 0.0)

    atom = lax.broadcasted_iota(jnp.int32, (own_rows, 8 * count), 0)
    place = jnp.where(atom == send[...], 1.0, 0.0).astype(bf16)
    value = rows[:, : 8 * count]
    high, low = split(value)
    rest = (value - high.astype(f32) - low.astype(f32)).astype(bf16)
    total = partial[...] + mxu(high, place, nt_dims) + mxu(low, place, nt_dims)
    total = total + mxu(rest, place, nt_dims)
    forces[...] = -total[0:3, :]
    product[...] = -total[3:6, :]


def call(kernel, outs, scratch, name, args, smem=()):
    specs = [
        pl.BlockSpec(memory_space=pltpu.SMEM if i in smem else pltpu.VMEM)
        for i in range(len(args))
    ]
    single = len(outs) == 1
    shapes = [jax.ShapeDtypeStruct(shape, f32) for shape in outs]
    out_specs = [pl.BlockSpec(memory_space=pltpu.VMEM) for _ in outs]
    return pl.pallas_call(
        kernel,
        out_shape=shapes[0] if single else shapes,
        in_specs=specs,
        out_specs=out_specs[0] if single else out_specs,
        scratch_shapes=[pltpu.VMEM(shape, kind) for shape, kind in scratch],
        compiler_params=pltpu.CompilerParams(vmem_limit_bytes=40 * 1024 * 1024),
        name=name,
    )(*args)


def exchanged(buffer):
    return lax.all_to_all(buffer, ("bx", "by"), 0, 0)


def per_device(
    positions,
    tangent,
    embedding,
    counts,
    neighbours,
    send_rows,
    w_one_in,
    w_one_out,
    filter_one,
    w_left,
    w_right,
    w_two_in,
    w_two_out,
    filter_two,
    w_hidden,
    w_energy,
):
    sizes = (lax.axis_size("bx"), lax.axis_size("by"))
    devices = sizes[0] * sizes[1]
    n = positions.shape[1]
    channels = embedding.shape[1]
    ghosts = send_rows.shape[1]
    count = ghosts // 8
    scale = 1.0 / math.sqrt(neighbours.shape[0])
    part = functools.partial
    base = [((n, n), f32), ((n, wide), f32), ((geo_slots, n, wide), f32)]

    def halves(rows):
        return [((rows, wide), bf16)] * 2

    factors = halves(wide) + halves(wide)

    buffer = call(
        part(pack_kernel, sizes),
        [(devices, count, channels + lanes)],
        [((n, n), f32), ((n, channels + lanes), f32)],
        "pack",
        (positions, tangent, embedding, send_rows),
        (3,),
    )
    arrived = exchanged(buffer)
    partial, phi_own = call(
        part(first_own_kernel, scale),
        [(8 * n, channels), (n, 2 * channels)],
        base + halves(8 * n) + factors,
        "first_own",
        (positions, tangent, embedding, neighbours, w_one_in, w_one_out, filter_one),
    )
    buffer, state, inner, maps, phi_two, phi_ghost, coords_ghost = call(
        part(first_ghost_kernel, sizes, scale),
        [
            (devices, count, 2 * channels),
            (2 * n, channels),
            (2 * n, channels),
            (12 * n, channels),
            (n, 2 * channels),
            (ghosts, 2 * channels),
            (ghosts, lanes),
        ],
        base
        + halves(8 * n)
        + factors
        + [((8 * n, channels), f32), ((ghosts, channels + lanes), f32)],
        "first_ghost",
        (
            positions,
            tangent,
            embedding,
            neighbours,
            send_rows,
            w_one_in,
            w_one_out,
            filter_one,
            w_left,
            w_right,
            w_two_in,
            w_two_out,
            partial,
            arrived,
        ),
        (4,),
    )
    arrived = exchanged(buffer)
    partial = call(
        part(second_own_kernel, scale),
        [(2 * n, channels)],
        base + halves(2 * n) + factors,
        "second_own",
        (positions, tangent, neighbours, filter_two, phi_two),
    )
    buffer, table, cot = call(
        part(second_ghost_kernel, sizes, scale),
        [(devices, count, 2 * channels), (ghosts, 2 * channels), (2 * n, channels)],
        base
        + halves(2 * n)
        + factors
        + [((2 * n, channels), f32), ((ghosts, 2 * channels), f32)],
        "second_ghost",
        (
            positions,
            tangent,
            neighbours,
            counts,
            filter_two,
            coords_ghost,
            state,
            partial,
            w_hidden,
            w_energy.reshape(1, channels),
            arrived,
        ),
        (3,),
    )
    arrived = exchanged(buffer)
    back, pair_own, pair_ghost = call(
        part(second_back_kernel, scale),
        [(n, 2 * channels), (2, n, lanes), (2, n, lanes)],
        base + halves(2 * n) + factors + [((2, n, wide), f32)],
        "second_back",
        (positions, tangent, neighbours, filter_two, coords_ghost, phi_two, table, cot),
    )
    pairs = [((8, n, wide), f32), ((8 * n, wide), f32)]
    buffer, bars, ghost_sums = call(
        part(first_back_ghost_kernel, sizes, scale),
        [(devices, 8, lanes), (8 * n, channels), (n, lanes)],
        base
        + halves(8 * n)
        + factors
        + pairs
        + [((n, 2 * channels), f32), ((8, lanes), f32)],
        "first_back_ghost",
        (
            positions,
            tangent,
            neighbours,
            send_rows,
            filter_one,
            coords_ghost,
            phi_ghost,
            cot,
            inner,
            maps,
            back,
            pair_ghost,
            w_two_in,
            w_two_out,
            w_left,
            w_right,
            arrived,
        ),
        (3,),
    )
    arrived = exchanged(buffer)
    partial = call(
        part(first_back_own_kernel, scale),
        [(8, lanes)],
        base + halves(8 * n) + factors + pairs + [((n, lanes), f32)],
        "first_back_own",
        (
            positions,
            tangent,
            neighbours,
            filter_one,
            phi_own,
            bars,
            pair_own,
            ghost_sums,
        ),
    )
    return call(
        part(finish_kernel, sizes),
        [(3, n), (3, n)],
        [((8, lanes), f32)],
        "finish",
        (send_rows, partial, arrived),
    )


def solution(mesh):
    placed = (
        P(None, ("bx", "by")),
        P(None, ("bx", "by")),
        P(("bx", "by"), None),
        P(("bx", "by")),
        P(None, ("bx", "by")),
        P(("bx", "by"), None),
        P(),
        P(),
        P(),
        P(),
        P(),
        P(),
        P(),
        P(),
        P(),
        P(),
    )

    def run(*arrays):
        return tuple(per_device(*arrays))

    return jax.shard_map(
        run,
        mesh=mesh,
        in_specs=placed,
        out_specs=(P(None, ("bx", "by")), P(None, ("bx", "by"))),
        check_vma=False,
    )
```

```python
import functools
import math

import jax
import jax.numpy as jnp
from jax import lax
from jax.experimental import pallas as pl
from jax.experimental.pallas import tpu as pltpu
from jax.sharding import PartitionSpec as P

f32 = jnp.float32
bf16 = jnp.bfloat16
cutoff_radius = 3.0
softening = 0.01
wave = math.pi / cutoff_radius
offsets = ((-1, -1), (-1, 0), (-1, 1), (0, -1), (0, 1), (1, -1), (1, 0), (1, 1))
lanes = 128
wide = 256
row_block = 32
nn_dims = (((1,), (0,)), ((), ()))
nt_dims = (((1,), (1,)), ((), ()))

U, UD, DD, RI = 0, 3, 6, 7
geo_slots = 8
P0, P1, P2, SN, CS, RS, RC = 0, 1, 2, 3, 4, 5, 6
osc_slots = 7


def split(value):
    high = value.astype(bf16)
    return high, (value - high.astype(f32)).astype(bf16)


def mxu(left, right, dims=nn_dims):
    return lax.dot_general(left, right, dims, preferred_element_type=f32)


def three(lh, ll, rh, rl, dims=nn_dims):
    return mxu(lh, rh, dims) + mxu(ll, rh, dims) + mxu(lh, rl, dims)


def dot3(left, right, dims=nn_dims):
    return three(*split(left), *split(right[...]), dims)


def sigmoid(value):
    return 1.0 / (1.0 + jnp.exp(-jnp.maximum(value, -80.0)))


def silu_parts(value):
    gate = sigmoid(value)
    first = gate * (1.0 + value * (1.0 - gate))
    second = gate * (1.0 - gate) * (2.0 + value * (1.0 - 2.0 * gate))
    return value * gate, first, second


def sin_cos(theta):
    t = jnp.minimum(theta, 6.0) * 0.25
    x = t * t
    s = -1.0 / 39916800.0 + x * (1.0 / 6227020800.0)
    s = 1.0 / 362880.0 + x * s
    s = -1.0 / 5040.0 + x * s
    s = 1.0 / 120.0 + x * s
    s = -1.0 / 6.0 + x * s
    s = t + t * x * s
    c = 1.0 / 479001600.0 - x * (1.0 / 87178291200.0)
    c = -1.0 / 3628800.0 + x * c
    c = 1.0 / 40320.0 + x * c
    c = -1.0 / 720.0 + x * c
    c = 1.0 / 24.0 + x * c
    c = -0.5 + x * c
    c = 1.0 + x * c
    s, c = 2.0 * s * c, 1.0 - 2.0 * s * s
    return 2.0 * s * c, 1.0 - 2.0 * s * s


def fill_geometry(geo, osc, first, second, mask_at, height, members):
    repeats = wide // members
    group = lax.broadcasted_iota(jnp.int32, (1, wide), 1) // members
    for start in range(0, height, row_block):
        rows = pl.ds(start, row_block)
        off = [first(i, start) - second(i, start) for i in range(3)]
        move = [first(i + 3, start) - second(i + 3, start) for i in range(3)]
        square = off[0] * off[0] + off[1] * off[1] + off[2] * off[2] + softening
        inverse = lax.rsqrt(square)
        inverse = inverse * (1.5 - 0.5 * square * inverse * inverse)
        theta = wave * (square * inverse)
        unit = [o * inverse for o in off]
        speed = unit[0] * move[0] + unit[1] * move[1] + unit[2] * move[2]
        for i in range(3):
            geo[U + i, rows, :] = unit[i]
            geo[UD + i, rows, :] = (move[i] - unit[i] * speed) * inverse
        sn, cs = sin_cos(theta)
        g0 = (0.5 * cs + 0.5) * inverse
        g1 = ((-0.5 * wave) * sn - g0) * inverse
        g2 = ((-0.5 * wave * wave) * cs - 2.0 * g1) * inverse
        mask = mask_at(start)
        geo[DD, rows, :] = speed
        osc[P0, rows, :] = mask * g0
        osc[P1, rows, :] = mask * g1
        osc[P2, rows, :] = mask * g2
        geo[RI, rows, :] = inverse
        turn_s, turn_c = sn, cs
        state_s, state_c = sn, cs
        for i in range(1, repeats):
            turn_s, turn_c = turn_s * cs + turn_c * sn, turn_c * cs - turn_s * sn
            state_s = jnp.where(group >= i, turn_s, state_s)
            state_c = jnp.where(group >= i, turn_c, state_c)
        osc[SN, rows, :] = state_s
        osc[CS, rows, :] = state_c
        osc[RS, rows, :] = turn_s
        osc[RC, rows, :] = turn_c


def order_factor(step, members):
    repeats = wide // members
    group = lax.broadcasted_iota(jnp.int32, (1, wide), 1) // members
    return (group + (step * repeats + 1)).astype(f32) * wave


def rotate(wave_state, osc, rows, s, c):
    rs = osc[RS, rows, :]
    rc = osc[RC, rows, :]
    wave_state[0, rows, :] = s * rc + c * rs
    wave_state[1, rows, :] = c * rc - s * rs


def listed(nbr_ref, start, members):
    slot = lax.broadcasted_iota(jnp.int32, (members, lanes), 0) + start
    found = nbr_ref[0:1, :] == slot
    for k in range(1, nbr_ref.shape[0]):
        found = found | (nbr_ref[k : k + 1, :] == slot)
    return jnp.where(found, 1.0, 0.0).astype(f32)


def geometry_by_atom(geo, osc, columns, table, mask, wbox):
    members = mask.shape[0]
    repeats = wide // members
    table = jnp.concatenate([table] * repeats, 1)
    wbox[...] = jnp.concatenate([mask] * repeats, 0).T
    fill_geometry(
        geo,
        osc,
        lambda i, start: table[i : i + 1, :],
        lambda i, start: columns[start : start + row_block, i : i + 1],
        lambda start: wbox[start : start + row_block, :],
        geo.shape[1],
        members,
    )


def geometry_by_slot(geo, osc, columns, centre, mask, wbox):
    height, own_rows = mask.shape
    repeats = wide // own_rows
    centre = jnp.concatenate([centre] * repeats, 1)
    wbox[0:height, :] = jnp.concatenate([mask] * repeats, 1)
    fill_geometry(
        geo,
        osc,
        lambda i, start: columns[start : start + row_block, i : i + 1],
        lambda i, start: centre[i : i + 1, :],
        lambda start: wbox[start : start + row_block, :],
        height,
        own_rows,
    )


def scaled_rows(pair, slot, step, filter_ref, columns, value):
    members = value.shape[0]
    for i in range(wide // members):
        row = filter_ref[pl.ds(step * (wide // members) + i, 1), columns]
        h, l = split(row * value)
        pair[0][slot, i * members : (i + 1) * members, :] = h
        pair[1][slot, i * members : (i + 1) * members, :] = l


def put_split(pair, start, value):
    h, l = split(value)
    pair[0][start : start + value.shape[0], :] = h
    pair[1][start : start + value.shape[0], :] = l


def at(pair, index):
    return pair[0].at[index], pair[1].at[index]


def basis_rows(kept, state, geo, osc, step, factor, start, height):
    rows = pl.ds(start, row_block)
    if step == 0:
        s, c = osc[SN, rows, :], osc[CS, rows, :]
    else:
        s, c = state[0, rows, :], state[1, rows, :]
    p0 = osc[P0, rows, :]
    b = p0 * s
    bd = (osc[P1, rows, :] * s + factor * (p0 * c)) * geo[DD, rows, :]
    put_split(kept, start, b)
    put_split(kept, height + start, bd)
    rotate(state, osc, rows, s, c)
    return b, bd


def first_messages(acc, geo, osc, state, work, scalars, vectors, phi, filt, members, chunks):
    height = geo.shape[1]
    channels = phi.shape[1] // 2
    top = 2 * height
    for step in range(chunks):
        factor = order_factor(step, members)
        slot = step % scalars[0].shape[0]
        scaled_rows(scalars, slot, step, filt, slice(0, channels), phi[:, :channels])
        scaled_rows(vectors, slot, step, filt, slice(channels, 2 * channels), phi[:, channels:])
        now = at(work, step % 2)
        for start in range(0, height, row_block):
            rows = pl.ds(start, row_block)
            b, bd = basis_rows(now, state, geo, osc, step, factor, start, height)
            for i in range(3):
                unit = geo[U + i, rows, :]
                put_split(now, (2 + i) * height + start, unit * b)
                put_split(
                    now, (5 + i) * height + start, geo[UD + i, rows, :] * b + unit * bd
                )
        ah, al = now
        acc[:top, :] += three(ah[:top, :], al[:top, :], scalars[0][slot], scalars[1][slot])
        acc[top:, :] += three(ah[top:, :], al[top:, :], vectors[0][slot], vectors[1][slot])


def second_messages(acc, basis_at, plain, dotted, filt, value, chunks):
    height = acc.shape[0] // 2
    channels = acc.shape[1]
    for step in range(chunks):
        slot = step % 2
        scaled_rows(plain, slot, step, filt, slice(None), value[:, :channels])
        scaled_rows(dotted, slot, step, filt, slice(None), value[:, channels:])
        ah, al = basis_at(step)
        acc[...] += three(ah[...], al[...], plain[0][slot], plain[1][slot])
        acc[height:, :] += three(
            ah[:height, :], al[:height, :], dotted[0][slot], dotted[1][slot]
        )


def plain_basis(kept, geo, osc, state, members, step, height):
    factor = order_factor(step, members)
    for start in range(0, height, row_block):
        basis_rows(kept, state, geo, osc, step, factor, start, height)


def full_basis(kept, geo, osc, state, members, step):
    height = geo.shape[1]
    factor = order_factor(step, members)
    for start in range(0, height, row_block):
        rows = pl.ds(start, row_block)
        if step == 0:
            s, c = osc[SN, rows, :], osc[CS, rows, :]
        else:
            s, c = state[0, rows, :], state[1, rows, :]
        p0, p1 = osc[P0, rows, :], osc[P1, rows, :]
        b = p0 * s
        kept[0, rows, :] = b
        kept[1, rows, :] = p1 * s + factor * (p0 * c)
        kept[2, rows, :] = (
            osc[P2, rows, :] * s + factor * (2.0 * p1 * c - factor * b)
        ) * geo[DD, rows, :]
        rotate(state, osc, rows, s, c)


def table_cotangents(back, basis_at, plain, dotted, filt, cot, chunks):
    channels = filt.shape[1]
    own_rows = cot.shape[0] // 2
    height = back.shape[0]
    back[...] = jnp.zeros_like(back)
    for step in range(chunks):
        slot = step % 2
        scaled_rows(plain, slot, step, filt, slice(None), cot[0:own_rows, :])
        scaled_rows(dotted, slot, step, filt, slice(None), cot[own_rows:, :])
        ah, al = basis_at(step)
        both = three(ah[...], al[...], plain[0][slot], plain[1][slot])
        back[:, :channels] += both[:height]
        back[:, channels:] += both[height:] + three(
            ah[:height, :], al[:height, :], dotted[0][slot], dotted[1][slot]
        )


def folded(value, members):
    total = value[:, :lanes] + value[:, lanes:]
    if members < lanes:
        total = total + pltpu.roll(total, members, 1)
    return total


def second_pairs(pair, result, split_cot, basis_at, plain, dotted, filt, value, chunks):
    height = pair.shape[1]
    channels = filt.shape[1]
    pair[...] = jnp.zeros_like(pair)
    ah, al = split_cot
    for step in range(chunks):
        slot = step % 2
        scaled_rows(plain, slot, step, filt, slice(None), value[:, :channels])
        scaled_rows(dotted, slot, step, filt, slice(None), value[:, channels:])
        both = three(ah[...], al[...], plain[0][slot], plain[1][slot], nt_dims)
        dot = both[height:] + three(
            ah[:height, :], al[:height, :], dotted[0][slot], dotted[1][slot], nt_dims
        )
        basis = basis_at(step)
        for start in range(0, height, row_block):
            rows = pl.ds(start, row_block)
            b1 = basis[1, rows, :]
            g = both[start : start + row_block]
            pair[0, rows, :] += b1 * g
            pair[1, rows, :] += basis[2, rows, :] * g + b1 * dot[start : start + row_block]
    members = value.shape[0]
    result[0] = folded(pair[0], members)
    result[1] = folded(pair[1], members)


def first_pairs(pair, spaces, split_cot, geo, basis_at, factors_at, chunks):
    height = geo.shape[1]
    pair[...] = jnp.zeros_like(pair)
    ch, cl = split_cot
    top = 2 * height
    for step in range(chunks):
        cots = spaces.at[step % 2]
        scalars, vectors = factors_at(step)
        cots[:top, :] = three(
            ch[:top, :], cl[:top, :], scalars[0][...], scalars[1][...], nt_dims
        )
        cots[top:, :] = three(
            ch[top:, :], cl[top:, :], vectors[0][...], vectors[1][...], nt_dims
        )
        basis = basis_at(step)
        for start in range(0, height, row_block):
            rows = pl.ds(start, row_block)
            b, b1, b2d = [basis[i, rows, :] for i in range(3)]
            b1d = b1 * geo[DD, rows, :]
            along = cots[start : start + row_block, :]
            along_dot = cots[height + start : height + start + row_block, :]
            for i in range(3):
                place = (2 + i) * height + start
                g = cots[place : place + row_block, :]
                place = (5 + i) * height + start
                gd = cots[place : place + row_block, :]
                unit = geo[U + i, rows, :]
                along = along + unit * g
                along_dot = along_dot + unit * gd + geo[UD + i, rows, :] * g
                pair[2 + i, rows, :] += b * g
                pair[5 + i, rows, :] += b * gd + b1d * g
            pair[0, rows, :] += b1 * along
            pair[1, rows, :] += b2d * along + b1 * along_dot


def neighbour_id(target, sizes):
    along = lax.axis_index("bx") + target[0]
    across = lax.axis_index("by") + target[1]
    inside = (along >= 0) & (along < sizes[0]) & (across >= 0) & (across < sizes[1])
    device = jnp.clip(along, 0, sizes[0] - 1) * sizes[1] + jnp.clip(across, 0, sizes[1] - 1)
    return device, inside


def send_chunks(r, chunk_at, sizes):
    for number, target in enumerate(offsets):
        device, inside = neighbour_id(target, sizes)
        copy = pltpu.make_async_copy(chunk_at(number), r.out.at[device], r.moves.at[number])

        @pl.when(inside)
        def _():
            copy.start()

    for number, target in enumerate(offsets):
        device, inside = neighbour_id(target, sizes)
        copy = pltpu.make_async_copy(chunk_at(number), r.out.at[device], r.moves.at[number])

        @pl.when(inside)
        def _():
            copy.wait()


def send_groups(r, table, sizes):
    count = r.out.shape[1]
    send_chunks(r, lambda number: table.at[number * count : (number + 1) * count, :], sizes)


def send_gathered(r, table, stage, send_ref, sizes):
    for slot in range(stage.shape[0]):
        stage[slot : slot + 1, :] = table[pl.ds(send_ref[0, slot], 1), :]
    send_groups(r, stage, sizes)


def receive(r, table, sizes):
    count = r.arrived.shape[1]

    def each(act):
        for number, target in enumerate(offsets):
            device, inside = neighbour_id(target, sizes)
            copy = pltpu.make_async_copy(
                r.arrived.at[device],
                table.at[number * count : (number + 1) * count, :],
                r.moves.at[number],
            )

            @pl.when(inside)
            def _():
                act(copy)

    each(lambda copy: copy.start())
    return lambda: each(lambda copy: copy.wait())


def add_returned(total, table, send_ref, sizes):
    count = table.shape[0] // 8
    for number, target in enumerate(offsets):
        device, inside = neighbour_id(target, sizes)

        @pl.when(inside)
        def _():
            for slot in range(number * count, (number + 1) * count):
                total[pl.ds(send_ref[0, slot], 1), :] += table[slot : slot + 1, :]


def offset_gradients(geo, pair, second, members, by_slot, by_atom):
    near = [folded(pair[i], members) for i in range(8)]
    height = geo.shape[1]
    units = [geo[U + i, :, :lanes] for i in range(3)]
    moves = [geo[UD + i, :, :lanes] for i in range(3)]
    inverse = geo[RI, :, :lanes]
    speed = geo[DD, :, :lanes]
    along = near[0] + second[0]
    along_dot = near[1] + second[1]
    turn, turn_dot = near[2:5], near[5:8]
    inner = units[0] * turn[0] + units[1] * turn[1] + units[2] * turn[2]
    inner_dot = sum(units[i] * turn_dot[i] + moves[i] * turn[i] for i in range(3))
    rate = speed * inverse
    lane = lax.broadcasted_iota(jnp.int32, (1, lanes), 1)
    sums = jnp.zeros((height, lanes), f32)
    for i in range(3):
        part = (turn[i] - units[i] * inner) * inverse
        grad = along * units[i] + part
        grad_dot = (
            along_dot * units[i]
            + along * moves[i]
            + (turn_dot[i] - moves[i] * inner - units[i] * inner_dot) * inverse
            - rate * part
        )
        for row, value in ((i, grad), (3 + i, grad_dot)):
            by_slot[row : row + 1, :] = jnp.sum(value, 0, keepdims=True)
            if members < lanes:
                value = jnp.where(lane < members, value, 0.0)
            sums = jnp.where(lane == row, -jnp.sum(value, 1, keepdims=True), sums)
    by_atom[...] = sums


def pack_kernel(sizes, r):
    channels = r.embedding.shape[1]
    r.box[...] = jnp.zeros_like(r.box)
    r.need("positions", "tangent")
    r.box[0:3, :] = r.positions[...]
    r.box[3:6, :] = r.tangent[...]
    r.table[:, channels:] = r.box[...].T
    r.need("embedding")
    r.table[:, :channels] = r.embedding[...]
    r.need("send_rows")
    send_gathered(r, r.table, r.stage, r.send_rows, sizes)


def first_own_kernel(scale, chunks, r):
    own_rows = r.positions.shape[1]
    r.box[...] = jnp.zeros_like(r.box)
    r.need("positions", "tangent", "neighbours")
    r.box[0:3, :] = r.positions[...]
    r.box[3:6, :] = r.tangent[...]
    r.cols[...] = r.box[...].T
    r.mask_own[...] = listed(r.neighbours, 0, own_rows)
    r.mask_ghost[...] = listed(r.neighbours, own_rows, r.mask_ghost.shape[0])
    r.put("box", "cols", "mask_own", "mask_ghost")
    geometry_by_atom(r.geo_own, r.osc_own, r.cols[...], r.box[...], r.mask_own[...], r.wbox)
    r.put("geo_own", "osc_own")
    r.need("w_one_in", "w_one_out", "embedding", "filter_one", "filter_two")
    r.filt_one[...] = r.filter_one[...] * scale
    r.filt_two[...] = r.filter_two[...] * scale
    r.put("filt_one", "filt_two")
    r.phi_own[...] = dot3(silu_parts(dot3(r.embedding[...], r.w_one_in))[0], r.w_one_out)
    r.put("phi_own")
    r.acc[...] = jnp.zeros_like(r.acc)
    first_messages(
        r.acc,
        r.geo_own,
        r.osc_own,
        r.state,
        r.work,
        r.gs,
        r.gv,
        r.phi_own,
        r.filt_one,
        own_rows,
        chunks,
    )
    r.put("acc")


def first_ghost_kernel(sizes, chunks, r):
    own_rows = r.embedding.shape[0]
    channels = r.embedding.shape[1]
    r.table[...] = jnp.zeros_like(r.table)
    arrival = receive(r, r.table, sizes)
    r.need("w_one_in", "w_one_out", "cols", "mask_ghost")
    arrival()
    r.coords_ghost[...] = r.table[:, channels:]
    r.put("coords_ghost")
    r.phi_ghost[...] = dot3(
        silu_parts(dot3(r.table[:, :channels], r.w_one_in))[0], r.w_one_out
    )
    r.put("phi_ghost")
    members = r.mask_ghost.shape[0]
    geometry_by_atom(
        r.geo, r.osc, r.cols[...], ghost_lanes(r.coords_ghost), r.mask_ghost[...], r.wbox
    )
    r.need("acc", "filt_one")
    first_messages(
        r.acc,
        r.geo,
        r.osc,
        r.state,
        r.work,
        r.gs,
        r.gv,
        r.phi_ghost,
        r.filt_one,
        members,
        chunks,
    )
    r.need("w_left", "w_right", "embedding", "w_two_in", "w_two_out", "send_rows")
    top = 2 * own_rows
    half = 3 * own_rows
    acc, maps = r.acc, r.maps
    ah, al = split(acc[top:, :])
    maps[0 : 2 * half, :] = three(ah, al, *split(r.w_left[...]))
    maps[2 * half :, :] = three(ah, al, *split(r.w_right[...]))
    r.put("maps")
    total = r.embedding[...] + acc[0:own_rows, :]
    moved = acc[own_rows:top, :]
    for i in range(3):
        a, b = i * own_rows, (i + 1) * own_rows
        left, left_dot = maps[a:b, :], maps[half + a : half + b, :]
        right = maps[2 * half + a : 2 * half + b, :]
        right_dot = maps[3 * half + a : 3 * half + b, :]
        total = total + left * right
        moved = moved + left_dot * right + left * right_dot
    r.node[0:own_rows, :] = total
    r.node[own_rows:, :] = moved
    r.put("node")
    r.inner[...] = dot3(r.node[...], r.w_two_in)
    r.put("inner")
    value, slope, _ = silu_parts(r.inner[0:own_rows, :])
    outer = dot3(jnp.concatenate([value, slope * r.inner[own_rows:, :]], 0), r.w_two_out)
    r.phi_two[:, :channels] = outer[:own_rows]
    r.phi_two[:, channels:] = outer[own_rows:]
    r.put("phi_two")
    send_gathered(r, r.phi_two, r.stage, r.send_rows, sizes)


def ghost_lanes(coords):
    members = coords.shape[0]
    return jnp.concatenate([coords[...]] * (lanes // members), 0).T[:, :members]


def second_own_kernel(chunks, ghost_chunks, r):
    own_rows = r.mask_own.shape[0]
    ghosts = r.mask_ghost.shape[0]
    channels = r.filt_two.shape[1]
    r.acc_two[...] = jnp.zeros_like(r.acc_two)
    r.need("geo_own", "osc_own", "filt_two", "phi_two")

    def own_basis(step):
        kept = at(r.work, step % 2)
        plain_basis(kept, r.geo_own, r.osc_own, r.state, own_rows, step, own_rows)
        return kept

    second_messages(r.acc_two, own_basis, r.plain, r.dotted, r.filt_two, r.phi_two, chunks)
    r.put("acc_two")
    r.need("box", "cols", "mask_own", "mask_ghost", "coords_ghost")
    geometry_by_slot(
        r.geo, r.osc, r.coords_ghost[...], r.box[...], r.mask_ghost[...], r.wbox
    )
    for step in range(chunks):
        plain_basis(at(r.at_ghost, step), r.geo, r.osc, r.state, own_rows, step, ghosts)
    r.put("at_ghost")
    geometry_by_atom(
        r.geo_ghost,
        r.osc,
        r.cols[...],
        ghost_lanes(r.coords_ghost),
        r.mask_ghost[...],
        r.wbox,
    )
    r.put("geo_ghost")
    for step in range(ghost_chunks):
        plain_basis(at(r.a_ghost, step), r.geo_ghost, r.osc, r.state, ghosts, step, own_rows)
    r.put("a_ghost")
    r.need("phi_ghost", "filt_one")
    for step in range(ghost_chunks):
        full_basis(r.basis_ghost.at[step], r.geo_ghost, r.osc, r.state, ghosts, step)
    r.put("basis_ghost")
    for step in range(ghost_chunks):
        phi = r.phi_ghost
        scaled_rows(r.gs_ghost, step, step, r.filt_one, slice(0, channels), phi[:, :channels])
        scaled_rows(
            r.gv_ghost, step, step, r.filt_one, slice(channels, None), phi[:, channels:]
        )
    r.put("gs_ghost", "gv_ghost")


def second_ghost_kernel(sizes, chunks, ghost_chunks, r):
    own_rows = r.node.shape[0] // 2
    r.table[...] = jnp.zeros_like(r.table)
    arrival = receive(r, r.table, sizes)
    r.need("filt_two", "acc_two")
    arrival()
    r.put("table")

    r.need("a_ghost")
    second_messages(
        r.acc_two,
        lambda step: at(r.a_ghost, step),
        r.plain,
        r.dotted,
        r.filt_two,
        r.table,
        ghost_chunks,
    )
    r.need("node", "w_hidden", "w_energy")
    hidden = dot3(r.node[...] + r.acc_two[...], r.w_hidden)
    _, slope, bend = silu_parts(hidden[:own_rows])
    live = lax.broadcasted_iota(jnp.int32, (own_rows, 1), 0) < r.counts[0]
    weight = jnp.where(live, r.w_energy[...], 0.0)
    bars = jnp.concatenate([weight * slope, weight * bend * hidden[own_rows:]], 0)
    r.cot[...] = dot3(bars, r.w_hidden, nt_dims)
    r.put("cot")
    r.need("at_ghost")
    table_cotangents(
        r.back_ghost,
        lambda step: at(r.at_ghost, step),
        r.plain,
        r.dotted,
        r.filt_two,
        r.cot,
        chunks,
    )
    send_groups(r, r.back_ghost, sizes)


def second_back_kernel(chunks, ghost_chunks, r):
    own_rows = r.mask_own.shape[0]
    r.need("box", "cols", "mask_own")
    geometry_by_slot(r.geo, r.osc, r.cols[...], r.box[...], r.mask_own[...], r.wbox)
    r.need("cot", "filt_two")

    def slot_basis(step):
        kept = at(r.work, step % 2)
        plain_basis(kept, r.geo, r.osc, r.state, own_rows, step, own_rows)
        return kept

    table_cotangents(r.back, slot_basis, r.plain, r.dotted, r.filt_two, r.cot, chunks)
    r.put("back")
    split_cot = at(r.work, 0)
    put_split(split_cot, 0, r.cot[...])
    r.need("geo_own", "osc_own", "phi_two")

    def own_basis(step):
        kept = r.basis.at[step % 2]
        full_basis(kept, r.geo_own, r.osc_own, r.state, own_rows, step)
        return kept

    second_pairs(
        r.pair,
        r.pair_own,
        split_cot,
        own_basis,
        r.plain,
        r.dotted,
        r.filt_two,
        r.phi_two,
        chunks,
    )
    r.put("pair_own")
    r.need("table", "basis_ghost")

    second_pairs(
        r.pair,
        r.pair_ghost,
        split_cot,
        lambda step: r.basis_ghost.at[step],
        r.plain,
        r.dotted,
        r.filt_two,
        r.table,
        ghost_chunks,
    )
    r.put("pair_ghost")


def first_back_ghost_kernel(sizes, r):
    own_rows = r.back.shape[0]
    channels = r.back.shape[1] // 2
    arrival = receive(r, r.table, sizes)
    r.need("send_rows", "back")
    arrival()
    add_returned(r.back, r.table, r.send_rows, sizes)
    r.need("w_two_out", "inner", "w_two_in", "cot")
    outer = dot3(
        jnp.concatenate([r.back[:, :channels], r.back[:, channels:]], 0), r.w_two_out, nt_dims
    )
    _, slope, bend = silu_parts(r.inner[:own_rows, :])
    pulled = jnp.concatenate(
        [
            outer[:own_rows] * slope,
            outer[own_rows:] * slope + outer[:own_rows] * bend * r.inner[own_rows:, :],
        ],
        0,
    )
    bars = r.cot[...] + dot3(pulled, r.w_two_in, nt_dims)
    put_split(r.bars, 0, bars)
    half = 3 * own_rows
    maps = r.maps
    bar, bar_dot = bars[0:own_rows], bars[own_rows:]
    r.need("maps", "w_left", "w_right")
    for i in range(3):
        a, b = i * own_rows, (i + 1) * own_rows
        left, left_dot = maps[a:b, :], maps[half + a : half + b, :]
        right = maps[2 * half + a : 2 * half + b, :]
        right_dot = maps[3 * half + a : 3 * half + b, :]
        for_left = jnp.concatenate([bar * right, bar_dot * right + bar * right_dot], 0)
        for_right = jnp.concatenate([bar * left, bar_dot * left + bar * left_dot], 0)
        both = dot3(for_left, r.w_left, nt_dims) + dot3(for_right, r.w_right, nt_dims)
        put_split(r.bars, (2 + i) * own_rows, both[:own_rows])
        put_split(r.bars, (5 + i) * own_rows, both[own_rows:])
    r.put("bars")
    r.need("geo_ghost", "gs_ghost", "gv_ghost", "basis_ghost")
    first_pairs(
        r.pair,
        r.cots,
        r.bars,
        r.geo_ghost,
        lambda step: r.basis_ghost.at[step],
        lambda step: (at(r.gs_ghost, step), at(r.gv_ghost, step)),
        r.basis_ghost.shape[0],
    )
    r.by_slot[...] = jnp.zeros_like(r.by_slot)
    r.need("pair_ghost")
    members = r.table.shape[0]
    offset_gradients(r.geo_ghost, r.pair, r.pair_ghost, members, r.by_slot, r.by_atom)
    r.put("by_atom")
    send_chunks(r, lambda number: r.by_slot, sizes)


def first_back_own_kernel(chunks, r):
    own_rows = r.by_atom.shape[0]
    channels = r.phi_own.shape[1] // 2
    r.need("phi_own", "filt_one", "geo_own", "osc_own", "bars")

    def basis_at(step):
        kept = r.basis.at[step % 2]
        full_basis(kept, r.geo_own, r.osc_own, r.state, own_rows, step)
        return kept

    def factors_at(step):
        slot = step % 2
        phi, filt = r.phi_own, r.filt_one
        scaled_rows(r.gs, slot, step, filt, slice(0, channels), phi[:, :channels])
        scaled_rows(r.gv, slot, step, filt, slice(channels, None), phi[:, channels:])
        return at(r.gs, slot), at(r.gv, slot)

    first_pairs(r.pair, r.cots, r.bars, r.geo_own, basis_at, factors_at, chunks)
    r.result[...] = jnp.zeros_like(r.result)
    r.need("pair_own", "by_atom")
    offset_gradients(r.geo_own, r.pair, r.pair_own, own_rows, r.result, r.atoms)
    r.result[...] += (r.atoms[...] + r.by_atom[...]).T[0:8, :]
    r.put("result")


def finish_kernel(sizes, r):
    count = r.send_rows.shape[1] // 8
    own_rows = r.result.shape[1]
    r.table[...] = jnp.zeros_like(r.table)
    arrival = receive(r, r.table, sizes)
    lane = lax.broadcasted_iota(jnp.int32, (1, lanes), 1)
    r.need("send_rows", "result")
    atom = lax.broadcasted_iota(jnp.int32, (own_rows, 8 * count), 0)
    place = jnp.where(atom == r.send_rows[...], 1.0, 0.0).astype(bf16)
    arrival()
    rows = jnp.zeros((8, lanes), f32)
    for number in range(8):
        shift = ((2 * number - 7) * count) % lanes
        moved = r.table[8 * number : 8 * number + 8, :]
        if shift:
            moved = pltpu.roll(moved, shift, 1)
        mine = (lane >= number * count) & (lane < (number + 1) * count)
        rows = jnp.where(mine, moved, rows)
    value = rows[:, : 8 * count]
    high, low = split(value)
    rest = (value - high.astype(f32) - low.astype(f32)).astype(bf16)
    total = r.result[...] + mxu(high, place, nt_dims) + mxu(low, place, nt_dims)
    total = total + mxu(rest, place, nt_dims)
    r.forces[...] = -total[0:3, :]
    r.product[...] = -total[3:6, :]
    r.put("forces", "product")


class Refs:
    def need(self, *names):
        for name in names:
            for copy in self.loads.pop(name, ()):
                copy.wait()

    def put(self, *names):
        for name in names:
            for copy in self.stores[name]:
                copy.start()
            self.started.append(name)

    def close(self):
        self.need(*tuple(self.loads))
        for name in self.started:
            for copy in self.stores[name]:
                copy.wait()


def as_tuple(value):
    return value if isinstance(value, tuple) else (value,)


def planned(name, source, target, sems, table):
    table.setdefault(name, []).append(pltpu.make_async_copy(source, target, sems.pop(0)))


def call(kernel, name, values, inputs, outputs, scratch):
    args, kinds, shapes, buffers = [], [], [], []
    copies = 0
    for entry in inputs:
        for array in as_tuple(values[entry.lstrip("&!%")]):
            if entry[0] in "!%":
                args.append(array)
                kinds.append(pl.BlockSpec(memory_space=pltpu.SMEM if entry[0] == "%" else pl.ANY))
                continue
            args.append(pltpu.with_memory_space_constraint(array, pltpu.HBM))
            kinds.append(pl.BlockSpec(memory_space=pltpu.HBM))
            space = pltpu.SMEM if entry[0] == "&" else pltpu.VMEM
            buffers.append(space(array.shape, array.dtype))
            copies += 1
    for entry, (shape, types) in outputs.items():
        for kind in as_tuple(types):
            shapes.append(pltpu.HBM(shape, kind))
            if entry[0] != "!":
                buffers.append(pltpu.VMEM(shape, kind))
                copies += 1
    for entry, (shape, types) in scratch.items():
        for kind in as_tuple(types):
            buffers.append(pltpu.VMEM(shape, kind))
    buffers.append(pltpu.SemaphoreType.DMA((copies + 1,)))
    buffers.append(pltpu.SemaphoreType.DMA((8,)))

    def run(*refs):
        r = Refs()
        r.loads, r.stores, r.started = {}, {}, []
        refs = list(refs)
        ins, refs = refs[: len(args)], refs[len(args) :]
        outs, refs = refs[: len(shapes)], refs[len(shapes) :]
        r.moves = refs[-1]
        sems = [refs[-2].at[number] for number in range(copies)]

        def take(types):
            group = tuple(refs.pop(0) for _ in types)
            return group, group if len(group) > 1 else group[0]

        for entry in inputs:
            plain = entry.lstrip("&!%")
            arrays = as_tuple(values[plain])
            sources, ins = ins[: len(arrays)], ins[len(arrays) :]
            if entry[0] in "!%":
                setattr(r, plain, sources[0])
                continue
            group, value = take(arrays)
            setattr(r, plain, value)
            for source, buffer in zip(sources, group):
                planned(plain, source, buffer, sems, r.loads)
        for entry, (shape, types) in outputs.items():
            types = as_tuple(types)
            targets, outs = outs[: len(types)], outs[len(types) :]
            if entry[0] == "!":
                setattr(r, entry[1:], targets[0])
                continue
            group, value = take(types)
            setattr(r, entry, value)
            for buffer, target in zip(group, targets):
                planned(entry, buffer, target, sems, r.stores)
        for entry, (shape, types) in scratch.items():
            setattr(r, entry, take(as_tuple(types))[1])
        for group in r.loads.values():
            for copy in group:
                copy.start()
        kernel(r)
        r.close()

    results = pl.pallas_call(
        run,
        out_shape=shapes,
        in_specs=kinds,
        out_specs=[pl.BlockSpec(memory_space=pltpu.HBM) for _ in shapes],
        scratch_shapes=buffers,
        compiler_params=pltpu.CompilerParams(vmem_limit_bytes=48 * 1024 * 1024),
        name=name,
    )(*args)
    results = list(results)
    for entry, (shape, types) in outputs.items():
        types = as_tuple(types)
        group, results = tuple(results[: len(types)]), results[len(types) :]
        values[entry.lstrip("!")] = group if len(group) > 1 else group[0]


def exchanged(buffer):
    return lax.all_to_all(buffer, ("bx", "by"), 0, 0)


def per_device(values):
    sizes = (lax.axis_size("bx"), lax.axis_size("by"))
    devices = sizes[0] * sizes[1]
    n = values["positions"].shape[1]
    channels = values["embedding"].shape[1]
    ghosts = values["send_rows"].shape[1]
    orders = values["filter_one"].shape[0]
    count = ghosts // 8
    scale = 1.0 / math.sqrt(values["neighbours"].shape[0])
    part = functools.partial
    pair = (bf16, bf16)
    own_chunks, ghost_chunks = orders * n // wide, orders * ghosts // wide
    values["w_energy"] = values["w_energy"].reshape(1, channels)

    def factors(chunks):
        return ((chunks, wide, channels), pair)

    geometry = ((geo_slots, n, wide), f32)
    osc = ((osc_slots, n, wide), f32)
    state = ((2, n, wide), f32)
    wbox = ((n, wide), f32)
    pairs = ((8, n, wide), f32)
    cots = ((2, 8 * n, wide), f32)

    call(
        part(pack_kernel, sizes),
        "pack",
        values,
        ("positions", "tangent", "embedding", "&send_rows"),
        {"!out": ((devices, count, channels + lanes), f32)},
        {
            "box": ((n, n), f32),
            "table": ((n, channels + lanes), f32),
            "stage": ((ghosts, channels + lanes), f32),
        },
    )
    values["arrived"] = exchanged(values["out"])
    call(
        part(first_own_kernel, scale, own_chunks),
        "first_own",
        values,
        (
            "positions",
            "tangent",
            "neighbours",
            "w_one_in",
            "w_one_out",
            "embedding",
            "filter_one",
            "filter_two",
        ),
        {
            "box": ((n, n), f32),
            "cols": ((n, n), f32),
            "mask_own": ((n, n), f32),
            "mask_ghost": ((ghosts, n), f32),
            "filt_one": ((orders, 2 * channels), f32),
            "filt_two": ((orders, channels), f32),
            "acc": ((8 * n, channels), f32),
            "geo_own": geometry,
            "osc_own": osc,
            "phi_own": ((n, 2 * channels), f32),
        },
        {
            "gs": factors(2),
            "gv": factors(2),
            "wbox": wbox,
            "state": state,
            "work": ((2, 8 * n, wide), pair),
        },
    )
    call(
        part(first_ghost_kernel, sizes, ghost_chunks),
        "first_ghost",
        values,
        (
            "w_one_in",
            "cols",
            "mask_ghost",
            "w_one_out",
            "filt_one",
            "acc",
            "w_left",
            "w_right",
            "embedding",
            "w_two_in",
            "w_two_out",
            "&send_rows",
            "!arrived",
        ),
        {
            "!out": ((devices, count, 2 * channels), f32),
            "node": ((2 * n, channels), f32),
            "inner": ((2 * n, channels), f32),
            "maps": ((12 * n, channels), f32),
            "phi_two": ((n, 2 * channels), f32),
            "phi_ghost": ((ghosts, 2 * channels), f32),
            "coords_ghost": ((ghosts, lanes), f32),
        },
        {
            "geo": geometry,
            "osc": osc,
            "gs": factors(2),
            "gv": factors(2),
            "wbox": wbox,
            "state": state,
            "work": ((2, 8 * n, wide), pair),
            "table": ((ghosts, channels + lanes), f32),
            "stage": ((ghosts, 2 * channels), f32),
        },
    )
    values["arrived"] = exchanged(values["out"])
    call(
        part(second_own_kernel, own_chunks, ghost_chunks),
        "second_own",
        values,
        (
            "geo_own",
            "osc_own",
            "phi_two",
            "filt_two",
            "box",
            "cols",
            "mask_own",
            "mask_ghost",
            "coords_ghost",
            "phi_ghost",
            "filt_one",
        ),
        {
            "acc_two": ((2 * n, channels), f32),
            "at_ghost": ((own_chunks, 2 * ghosts, wide), pair),
            "geo_ghost": geometry,
            "a_ghost": ((ghost_chunks, 2 * n, wide), pair),
            "basis_ghost": ((ghost_chunks, 3, n, wide), f32),
            "gs_ghost": factors(ghost_chunks),
            "gv_ghost": factors(ghost_chunks),
        },
        {
            "geo": geometry,
            "osc": osc,
            "state": state,
            "wbox": wbox,
            "work": ((2, 2 * n, wide), pair),
            "plain": factors(2),
            "dotted": factors(2),
        },
    )
    call(
        part(second_ghost_kernel, sizes, own_chunks, ghost_chunks),
        "second_ghost",
        values,
        (
            "%counts",
            "filt_two",
            "acc_two",
            "a_ghost",
            "node",
            "w_hidden",
            "w_energy",
            "at_ghost",
            "!arrived",
        ),
        {
            "!out": ((devices, count, 2 * channels), f32),
            "cot": ((2 * n, channels), f32),
            "table": ((ghosts, 2 * channels), f32),
        },
        {
            "plain": factors(2),
            "dotted": factors(2),
            "back_ghost": ((ghosts, 2 * channels), f32),
        },
    )
    values["arrived"] = exchanged(values["out"])
    call(
        part(second_back_kernel, own_chunks, ghost_chunks),
        "second_back",
        values,
        (
            "box",
            "cols",
            "mask_own",
            "cot",
            "filt_two",
            "geo_own",
            "osc_own",
            "phi_two",
            "table",
            "basis_ghost",
        ),
        {
            "back": ((n, 2 * channels), f32),
            "pair_own": ((2, n, lanes), f32),
            "pair_ghost": ((2, n, lanes), f32),
        },
        {
            "basis": ((2, 3, n, wide), f32),
            "geo": geometry,
            "osc": osc,
            "state": state,
            "wbox": wbox,
            "work": ((2, 2 * n, wide), pair),
            "plain": factors(2),
            "dotted": factors(2),
            "pair": ((2, n, wide), f32),
        },
    )
    call(
        part(first_back_ghost_kernel, sizes),
        "first_back_ghost",
        values,
        (
            "&send_rows",
            "back",
            "w_two_out",
            "inner",
            "w_two_in",
            "cot",
            "maps",
            "w_left",
            "w_right",
            "geo_ghost",
            "gs_ghost",
            "gv_ghost",
            "basis_ghost",
            "pair_ghost",
            "!arrived",
        ),
        {
            "!out": ((devices, 8, lanes), f32),
            "bars": ((8 * n, channels), pair),
            "by_atom": ((n, lanes), f32),
        },
        {
            "table": ((ghosts, 2 * channels), f32),
            "by_slot": ((8, lanes), f32),
            "pair": pairs,
            "cots": cots,
        },
    )
    values["arrived"] = exchanged(values["out"])
    call(
        part(first_back_own_kernel, own_chunks),
        "first_back_own",
        values,
        ("phi_own", "filt_one", "geo_own", "osc_own", "bars", "pair_own", "by_atom"),
        {"result": ((8, lanes), f32)},
        {
            "atoms": ((n, lanes), f32),
            "pair": pairs,
            "cots": cots,
            "state": state,
            "gs": factors(2),
            "gv": factors(2),
            "basis": ((2, 3, n, wide), f32),
        },
    )
    call(
        part(finish_kernel, sizes),
        "finish",
        values,
        ("send_rows", "result", "!arrived"),
        {"forces": ((3, n), f32), "product": ((3, n), f32)},
        {"table": ((64, lanes), f32)},
    )
    return values["forces"], values["product"]


argument_names = (
    "positions",
    "tangent",
    "embedding",
    "counts",
    "neighbours",
    "send_rows",
    "w_one_in",
    "w_one_out",
    "filter_one",
    "w_left",
    "w_right",
    "w_two_in",
    "w_two_out",
    "filter_two",
    "w_hidden",
    "w_energy",
)


def solution(mesh):
    brick = ("bx", "by")
    placed = (
        P(None, brick),
        P(None, brick),
        P(brick, None),
        P(brick),
        P(None, brick),
        P(brick, None),
    ) + (P(),) * 10

    def run(*arrays):
        return per_device(dict(zip(argument_names, arrays)))

    return jax.shard_map(
        run,
        mesh=mesh,
        in_specs=placed,
        out_specs=(P(None, brick), P(None, brick)),
        check_vma=False,
    )
```

```python
import functools
import math

import jax
import jax.numpy as jnp
from jax import lax
from jax.experimental import pallas as pl
from jax.experimental.pallas import tpu as pltpu
from jax.sharding import PartitionSpec as P

f32 = jnp.float32
bf16 = jnp.bfloat16
cutoff_radius = 3.0
softening = 0.01
wave = math.pi / cutoff_radius
offsets = ((-1, -1), (-1, 0), (-1, 1), (0, -1), (0, 1), (1, -1), (1, 0), (1, 1))
lanes = 128
wide = 256
row_block = 32
nn_dims = (((1,), (0,)), ((), ()))
nt_dims = (((1,), (1,)), ((), ()))

U, UD, DD, RI = 0, 3, 6, 7
geo_slots = 8
P0, P1, P2, SN, CS, RS, RC = 0, 1, 2, 3, 4, 5, 6
osc_slots = 7
own_group = 2
ghost_group = 5


def split(value):
    high = value.astype(bf16)
    return high, (value - high.astype(f32)).astype(bf16)


def mxu(left, right, dims=nn_dims):
    return lax.dot_general(left, right, dims, preferred_element_type=f32)


def three(lh, ll, rh, rl, dims=nn_dims):
    return mxu(lh, rh, dims) + mxu(ll, rh, dims) + mxu(lh, rl, dims)


def dot3(left, right, dims=nn_dims):
    return three(*split(left), *split(right[...]), dims)


def sigmoid(value):
    return 1.0 / (1.0 + jnp.exp(-jnp.maximum(value, -80.0)))


def silu_parts(value):
    gate = sigmoid(value)
    first = gate * (1.0 + value * (1.0 - gate))
    second = gate * (1.0 - gate) * (2.0 + value * (1.0 - 2.0 * gate))
    return value * gate, first, second


def sin_cos(theta):
    t = jnp.minimum(theta, 6.0) * 0.25
    x = t * t
    s = -1.0 / 39916800.0 + x * (1.0 / 6227020800.0)
    s = 1.0 / 362880.0 + x * s
    s = -1.0 / 5040.0 + x * s
    s = 1.0 / 120.0 + x * s
    s = -1.0 / 6.0 + x * s
    s = t + t * x * s
    c = 1.0 / 479001600.0 - x * (1.0 / 87178291200.0)
    c = -1.0 / 3628800.0 + x * c
    c = 1.0 / 40320.0 + x * c
    c = -1.0 / 720.0 + x * c
    c = 1.0 / 24.0 + x * c
    c = -0.5 + x * c
    c = 1.0 + x * c
    s, c = 2.0 * s * c, 1.0 - 2.0 * s * s
    return 2.0 * s * c, 1.0 - 2.0 * s * s


def fill_geometry(geo, osc, first, second, mask_at, height, members):
    repeats = wide // members
    group = lax.broadcasted_iota(jnp.int32, (1, wide), 1) // members
    for start in range(0, height, row_block):
        rows = pl.ds(start, row_block)
        off = [first(i, start) - second(i, start) for i in range(3)]
        move = [first(i + 3, start) - second(i + 3, start) for i in range(3)]
        square = off[0] * off[0] + off[1] * off[1] + off[2] * off[2] + softening
        inverse = lax.rsqrt(square)
        inverse = inverse * (1.5 - 0.5 * square * inverse * inverse)
        theta = wave * (square * inverse)
        unit = [o * inverse for o in off]
        speed = unit[0] * move[0] + unit[1] * move[1] + unit[2] * move[2]
        for i in range(3):
            geo[U + i, rows, :] = unit[i]
            geo[UD + i, rows, :] = (move[i] - unit[i] * speed) * inverse
        sn, cs = sin_cos(theta)
        g0 = (0.5 * cs + 0.5) * inverse
        g1 = ((-0.5 * wave) * sn - g0) * inverse
        g2 = ((-0.5 * wave * wave) * cs - 2.0 * g1) * inverse
        mask = mask_at(start)
        geo[DD, rows, :] = speed
        osc[P0, rows, :] = mask * g0
        osc[P1, rows, :] = mask * g1
        osc[P2, rows, :] = mask * g2
        geo[RI, rows, :] = inverse
        turn_s, turn_c = sn, cs
        state_s, state_c = sn, cs
        for i in range(1, repeats):
            turn_s, turn_c = turn_s * cs + turn_c * sn, turn_c * cs - turn_s * sn
            state_s = jnp.where(group >= i, turn_s, state_s)
            state_c = jnp.where(group >= i, turn_c, state_c)
        osc[SN, rows, :] = state_s
        osc[CS, rows, :] = state_c
        osc[RS, rows, :] = turn_s
        osc[RC, rows, :] = turn_c


def order_factor(step, members):
    repeats = wide // members
    group = lax.broadcasted_iota(jnp.int32, (1, wide), 1) // members
    return (group + (step * repeats + 1)).astype(f32) * wave


def rotate(wave_state, osc, rows, s, c):
    rs = osc[RS, rows, :]
    rc = osc[RC, rows, :]
    wave_state[0, rows, :] = s * rc + c * rs
    wave_state[1, rows, :] = c * rc - s * rs


def steps(count, members, body):
    group = own_group if members == lanes else ghost_group
    if group >= count:
        for step in range(count):
            body(step, step % 2)
        return

    def several(index, carry):
        for place in range(group):
            body(index * group + place, place % 2)
        return carry

    lax.fori_loop(0, count // group, several, 0)


def start_state(state, osc, height):
    state[0, 0:height, :] = osc[SN, 0:height, :]
    state[1, 0:height, :] = osc[CS, 0:height, :]


def listed(nbr_ref, start, members):
    slot = lax.broadcasted_iota(jnp.int32, (members, lanes), 0) + start
    found = nbr_ref[0:1, :] == slot
    for k in range(1, nbr_ref.shape[0]):
        found = found | (nbr_ref[k : k + 1, :] == slot)
    return jnp.where(found, 1.0, 0.0).astype(f32)


def geometry_by_atom(geo, osc, columns, table, mask, wbox):
    members = mask.shape[0]
    repeats = wide // members
    table = jnp.concatenate([table] * repeats, 1)
    wbox[...] = jnp.concatenate([mask] * repeats, 0).T
    fill_geometry(
        geo,
        osc,
        lambda i, start: table[i : i + 1, :],
        lambda i, start: columns[start : start + row_block, i : i + 1],
        lambda start: wbox[start : start + row_block, :],
        geo.shape[1],
        members,
    )


def geometry_by_slot(geo, osc, columns, centre, mask, wbox):
    height, own_rows = mask.shape
    repeats = wide // own_rows
    centre = jnp.concatenate([centre] * repeats, 1)
    wbox[0:height, :] = jnp.concatenate([mask] * repeats, 1)
    fill_geometry(
        geo,
        osc,
        lambda i, start: columns[start : start + row_block, i : i + 1],
        lambda i, start: centre[i : i + 1, :],
        lambda start: wbox[start : start + row_block, :],
        height,
        own_rows,
    )


def scaled_rows(pair, slot, step, filter_ref, columns, value):
    members = value.shape[0]
    for i in range(wide // members):
        row = filter_ref[pl.ds(step * (wide // members) + i, 1), columns]
        h, l = split(row * value)
        pair[0][slot, i * members : (i + 1) * members, :] = h
        pair[1][slot, i * members : (i + 1) * members, :] = l


def put_split(pair, start, value):
    h, l = split(value)
    pair[0][start : start + value.shape[0], :] = h
    pair[1][start : start + value.shape[0], :] = l


def at(pair, index):
    return pair[0].at[index], pair[1].at[index]


def basis_rows(kept, state, geo, osc, step, factor, start, height):
    rows = pl.ds(start, row_block)
    s, c = state[0, rows, :], state[1, rows, :]
    p0 = osc[P0, rows, :]
    b = p0 * s
    bd = (osc[P1, rows, :] * s + factor * (p0 * c)) * geo[DD, rows, :]
    put_split(kept, start, b)
    put_split(kept, height + start, bd)
    rotate(state, osc, rows, s, c)
    return b, bd


def first_messages(acc, geo, osc, state, work, scalars, vectors, phi, filt, members, chunks):
    height = geo.shape[1]
    channels = phi.shape[1] // 2
    top = 2 * height
    start_state(state, osc, height)

    def chunk(step, slot):
        factor = order_factor(step, members)
        scaled_rows(scalars, slot, step, filt, slice(0, channels), phi[:, :channels])
        scaled_rows(vectors, slot, step, filt, slice(channels, 2 * channels), phi[:, channels:])
        now = at(work, slot)
        for start in range(0, height, row_block):
            rows = pl.ds(start, row_block)
            b, bd = basis_rows(now, state, geo, osc, step, factor, start, height)
            for i in range(3):
                unit = geo[U + i, rows, :]
                put_split(now, (2 + i) * height + start, unit * b)
                put_split(
                    now, (5 + i) * height + start, geo[UD + i, rows, :] * b + unit * bd
                )
        ah, al = now
        acc[:top, :] += three(ah[:top, :], al[:top, :], scalars[0][slot], scalars[1][slot])
        acc[top:, :] += three(ah[top:, :], al[top:, :], vectors[0][slot], vectors[1][slot])

    steps(chunks, members, chunk)


def second_messages(acc, basis_at, plain, dotted, filt, value, chunks):
    height = acc.shape[0] // 2
    channels = acc.shape[1]

    def chunk(step, slot):
        scaled_rows(plain, slot, step, filt, slice(None), value[:, :channels])
        scaled_rows(dotted, slot, step, filt, slice(None), value[:, channels:])
        ah, al = basis_at(step, slot)
        acc[...] += three(ah[...], al[...], plain[0][slot], plain[1][slot])
        acc[height:, :] += three(
            ah[:height, :], al[:height, :], dotted[0][slot], dotted[1][slot]
        )

    steps(chunks, value.shape[0], chunk)


def plain_basis(kept, geo, osc, state, members, step, height):
    factor = order_factor(step, members)
    for start in range(0, height, row_block):
        basis_rows(kept, state, geo, osc, step, factor, start, height)


def full_basis(kept, geo, osc, state, members, step):
    height = geo.shape[1]
    factor = order_factor(step, members)
    for start in range(0, height, row_block):
        rows = pl.ds(start, row_block)
        s, c = state[0, rows, :], state[1, rows, :]
        p0, p1 = osc[P0, rows, :], osc[P1, rows, :]
        b = p0 * s
        kept[0, rows, :] = b
        kept[1, rows, :] = p1 * s + factor * (p0 * c)
        kept[2, rows, :] = (
            osc[P2, rows, :] * s + factor * (2.0 * p1 * c - factor * b)
        ) * geo[DD, rows, :]
        rotate(state, osc, rows, s, c)


def table_cotangents(back, basis_at, plain, dotted, filt, cot, chunks):
    channels = filt.shape[1]
    own_rows = cot.shape[0] // 2
    height = back.shape[0]
    back[...] = jnp.zeros_like(back)

    def chunk(step, slot):
        scaled_rows(plain, slot, step, filt, slice(None), cot[0:own_rows, :])
        scaled_rows(dotted, slot, step, filt, slice(None), cot[own_rows:, :])
        ah, al = basis_at(step, slot)
        both = three(ah[...], al[...], plain[0][slot], plain[1][slot])
        back[:, :channels] += both[:height]
        back[:, channels:] += both[height:] + three(
            ah[:height, :], al[:height, :], dotted[0][slot], dotted[1][slot]
        )

    steps(chunks, own_rows, chunk)


def folded(value, members):
    total = value[:, :lanes] + value[:, lanes:]
    if members < lanes:
        total = total + pltpu.roll(total, members, 1)
    return total


def second_pairs(pair, result, split_cot, basis_at, plain, dotted, filt, value, chunks):
    height = pair.shape[1]
    channels = filt.shape[1]
    pair[...] = jnp.zeros_like(pair)
    ah, al = split_cot

    def chunk(step, slot):
        scaled_rows(plain, slot, step, filt, slice(None), value[:, :channels])
        scaled_rows(dotted, slot, step, filt, slice(None), value[:, channels:])
        both = three(ah[...], al[...], plain[0][slot], plain[1][slot], nt_dims)
        dot = both[height:] + three(
            ah[:height, :], al[:height, :], dotted[0][slot], dotted[1][slot], nt_dims
        )
        basis = basis_at(step, slot)
        for start in range(0, height, row_block):
            rows = pl.ds(start, row_block)
            b1 = basis[1, rows, :]
            g = both[start : start + row_block]
            pair[0, rows, :] += b1 * g
            pair[1, rows, :] += basis[2, rows, :] * g + b1 * dot[start : start + row_block]

    members = value.shape[0]
    steps(chunks, members, chunk)
    result[0] = folded(pair[0], members)
    result[1] = folded(pair[1], members)


def first_pairs(pair, spaces, split_cot, geo, basis_at, factors_at, members, chunks):
    height = geo.shape[1]
    pair[...] = jnp.zeros_like(pair)
    ch, cl = split_cot
    top = 2 * height

    def chunk(step, slot):
        cots = spaces.at[slot]
        scalars, vectors = factors_at(step, slot)
        cots[:top, :] = three(
            ch[:top, :], cl[:top, :], scalars[0][...], scalars[1][...], nt_dims
        )
        cots[top:, :] = three(
            ch[top:, :], cl[top:, :], vectors[0][...], vectors[1][...], nt_dims
        )
        basis = basis_at(step, slot)
        for start in range(0, height, row_block):
            rows = pl.ds(start, row_block)
            b, b1, b2d = [basis[i, rows, :] for i in range(3)]
            b1d = b1 * geo[DD, rows, :]
            along = cots[start : start + row_block, :]
            along_dot = cots[height + start : height + start + row_block, :]
            for i in range(3):
                place = (2 + i) * height + start
                g = cots[place : place + row_block, :]
                place = (5 + i) * height + start
                gd = cots[place : place + row_block, :]
                unit = geo[U + i, rows, :]
                along = along + unit * g
                along_dot = along_dot + unit * gd + geo[UD + i, rows, :] * g
                pair[2 + i, rows, :] += b * g
                pair[5 + i, rows, :] += b * gd + b1d * g
            pair[0, rows, :] += b1 * along
            pair[1, rows, :] += b2d * along + b1 * along_dot

    steps(chunks, members, chunk)


def neighbour_id(target, sizes):
    along = lax.axis_index("bx") + target[0]
    across = lax.axis_index("by") + target[1]
    inside = (along >= 0) & (along < sizes[0]) & (across >= 0) & (across < sizes[1])
    device = jnp.clip(along, 0, sizes[0] - 1) * sizes[1] + jnp.clip(across, 0, sizes[1] - 1)
    return device, inside


def send_chunks(r, chunk_at, sizes):
    for number, target in enumerate(offsets):
        device, inside = neighbour_id(target, sizes)
        copy = pltpu.make_async_copy(chunk_at(number), r.out.at[device], r.moves.at[number])

        @pl.when(inside)
        def _():
            copy.start()

    for number, target in enumerate(offsets):
        device, inside = neighbour_id(target, sizes)
        copy = pltpu.make_async_copy(chunk_at(number), r.out.at[device], r.moves.at[number])

        @pl.when(inside)
        def _():
            copy.wait()


def send_groups(r, table, sizes):
    count = r.out.shape[1]
    send_chunks(r, lambda number: table.at[number * count : (number + 1) * count, :], sizes)


def send_gathered(r, table, stage, send_ref, sizes):
    for slot in range(stage.shape[0]):
        stage[slot : slot + 1, :] = table[pl.ds(send_ref[0, slot], 1), :]
    send_groups(r, stage, sizes)


def receive(r, table, sizes):
    count = r.arrived.shape[1]

    def each(act):
        for number, target in enumerate(offsets):
            device, inside = neighbour_id(target, sizes)
            copy = pltpu.make_async_copy(
                r.arrived.at[device],
                table.at[number * count : (number + 1) * count, :],
                r.moves.at[number],
            )

            @pl.when(inside)
            def _():
                act(copy)

    each(lambda copy: copy.start())
    return lambda: each(lambda copy: copy.wait())


def add_returned(total, table, send_ref, sizes):
    count = table.shape[0] // 8
    for number, target in enumerate(offsets):
        device, inside = neighbour_id(target, sizes)

        @pl.when(inside)
        def _():
            for slot in range(number * count, (number + 1) * count):
                total[pl.ds(send_ref[0, slot], 1), :] += table[slot : slot + 1, :]


def offset_gradients(geo, pair, second, members, by_slot, by_atom):
    near = [folded(pair[i], members) for i in range(8)]
    height = geo.shape[1]
    units = [geo[U + i, :, :lanes] for i in range(3)]
    moves = [geo[UD + i, :, :lanes] for i in range(3)]
    inverse = geo[RI, :, :lanes]
    speed = geo[DD, :, :lanes]
    along = near[0] + second[0]
    along_dot = near[1] + second[1]
    turn, turn_dot = near[2:5], near[5:8]
    inner = units[0] * turn[0] + units[1] * turn[1] + units[2] * turn[2]
    inner_dot = sum(units[i] * turn_dot[i] + moves[i] * turn[i] for i in range(3))
    rate = speed * inverse
    lane = lax.broadcasted_iota(jnp.int32, (1, lanes), 1)
    sums = jnp.zeros((height, lanes), f32)
    for i in range(3):
        part = (turn[i] - units[i] * inner) * inverse
        grad = along * units[i] + part
        grad_dot = (
            along_dot * units[i]
            + along * moves[i]
            + (turn_dot[i] - moves[i] * inner - units[i] * inner_dot) * inverse
            - rate * part
        )
        for row, value in ((i, grad), (3 + i, grad_dot)):
            by_slot[row : row + 1, :] = jnp.sum(value, 0, keepdims=True)
            if members < lanes:
                value = jnp.where(lane < members, value, 0.0)
            sums = jnp.where(lane == row, -jnp.sum(value, 1, keepdims=True), sums)
    by_atom[...] = sums


def pack_kernel(sizes, r):
    channels = r.embedding.shape[1]
    r.box[...] = jnp.zeros_like(r.box)
    r.need(r.positions, r.tangent)
    r.box[0:3, :] = r.positions[...]
    r.box[3:6, :] = r.tangent[...]
    r.table[:, channels:] = r.box[...].T
    r.need(r.embedding)
    r.table[:, :channels] = r.embedding[...]
    r.need(r.send_rows)
    send_gathered(r, r.table, r.stage, r.send_rows, sizes)


def first_own_kernel(scale, chunks, r):
    own_rows = r.positions.shape[1]
    r.box[...] = jnp.zeros_like(r.box)
    r.need(r.positions, r.tangent, r.neighbours)
    r.box[0:3, :] = r.positions[...]
    r.box[3:6, :] = r.tangent[...]
    r.cols[...] = r.box[...].T
    r.mask_own[...] = listed(r.neighbours, 0, own_rows)
    r.mask_ghost[...] = listed(r.neighbours, own_rows, r.mask_ghost.shape[0])
    r.put(r.box, r.cols, r.mask_own, r.mask_ghost)
    geometry_by_atom(r.geo_own, r.osc_own, r.cols[...], r.box[...], r.mask_own[...], r.wbox)
    r.put(r.geo_own, r.osc_own)
    r.need(r.w_one_in, r.w_one_out, r.embedding, r.filter_one, r.filter_two)
    r.filt_one[...] = r.filter_one[...] * scale
    r.filt_two[...] = r.filter_two[...] * scale
    r.put(r.filt_one, r.filt_two)
    r.phi_own[...] = dot3(silu_parts(dot3(r.embedding[...], r.w_one_in))[0], r.w_one_out)
    r.put(r.phi_own)
    r.acc[...] = jnp.zeros_like(r.acc)
    first_messages(
        r.acc,
        r.geo_own,
        r.osc_own,
        r.state,
        r.work,
        r.gs,
        r.gv,
        r.phi_own,
        r.filt_one,
        own_rows,
        chunks,
    )
    r.put(r.acc)


def first_ghost_kernel(sizes, chunks, r):
    own_rows = r.embedding.shape[0]
    channels = r.embedding.shape[1]
    r.table[...] = jnp.zeros_like(r.table)
    arrival = receive(r, r.table, sizes)
    r.need(r.w_one_in, r.w_one_out, r.cols, r.mask_ghost)
    arrival()
    r.coords_ghost[...] = r.table[:, channels:]
    r.put(r.coords_ghost)
    r.phi_ghost[...] = dot3(
        silu_parts(dot3(r.table[:, :channels], r.w_one_in))[0], r.w_one_out
    )
    r.put(r.phi_ghost)
    members = r.mask_ghost.shape[0]
    geometry_by_atom(
        r.geo, r.osc, r.cols[...], ghost_lanes(r.coords_ghost), r.mask_ghost[...], r.wbox
    )
    r.need(r.acc, r.filt_one)
    first_messages(
        r.acc,
        r.geo,
        r.osc,
        r.state,
        r.work,
        r.gs,
        r.gv,
        r.phi_ghost,
        r.filt_one,
        members,
        chunks,
    )
    r.need(r.w_left, r.w_right, r.embedding, r.w_two_in, r.w_two_out, r.send_rows)
    top = 2 * own_rows
    half = 3 * own_rows
    acc, maps = r.acc, r.maps
    ah, al = split(acc[top:, :])
    maps[0 : 2 * half, :] = three(ah, al, *split(r.w_left[...]))
    maps[2 * half :, :] = three(ah, al, *split(r.w_right[...]))
    r.put(r.maps)
    total = r.embedding[...] + acc[0:own_rows, :]
    moved = acc[own_rows:top, :]
    for i in range(3):
        a, b = i * own_rows, (i + 1) * own_rows
        left, left_dot = maps[a:b, :], maps[half + a : half + b, :]
        right = maps[2 * half + a : 2 * half + b, :]
        right_dot = maps[3 * half + a : 3 * half + b, :]
        total = total + left * right
        moved = moved + left_dot * right + left * right_dot
    r.node[0:own_rows, :] = total
    r.node[own_rows:, :] = moved
    r.put(r.node)
    r.inner[...] = dot3(r.node[...], r.w_two_in)
    r.put(r.inner)
    value, slope, _ = silu_parts(r.inner[0:own_rows, :])
    outer = dot3(jnp.concatenate([value, slope * r.inner[own_rows:, :]], 0), r.w_two_out)
    r.phi_two[:, :channels] = outer[:own_rows]
    r.phi_two[:, channels:] = outer[own_rows:]
    r.put(r.phi_two)
    send_gathered(r, r.phi_two, r.stage, r.send_rows, sizes)


def ghost_lanes(coords):
    members = coords.shape[0]
    return jnp.concatenate([coords[...]] * (lanes // members), 0).T[:, :members]


def second_own_kernel(chunks, ghost_chunks, r):
    own_rows = r.mask_own.shape[0]
    ghosts = r.mask_ghost.shape[0]
    channels = r.filt_two.shape[1]
    r.acc_two[...] = jnp.zeros_like(r.acc_two)
    r.need(r.geo_own, r.osc_own, r.filt_two, r.phi_two)

    start_state(r.state, r.osc_own, own_rows)

    def own_basis(step, slot):
        kept = at(r.work, slot)
        plain_basis(kept, r.geo_own, r.osc_own, r.state, own_rows, step, own_rows)
        return kept

    second_messages(r.acc_two, own_basis, r.plain, r.dotted, r.filt_two, r.phi_two, chunks)
    r.put(r.acc_two)
    r.need(r.box, r.cols, r.mask_own, r.mask_ghost, r.coords_ghost)
    geometry_by_slot(
        r.geo, r.osc, r.coords_ghost[...], r.box[...], r.mask_ghost[...], r.wbox
    )
    start_state(r.state, r.osc, ghosts)
    steps(
        chunks,
        own_rows,
        lambda step, slot: plain_basis(
            at(r.at_ghost, step), r.geo, r.osc, r.state, own_rows, step, ghosts
        ),
    )
    r.put(r.at_ghost)
    geometry_by_atom(
        r.geo_ghost,
        r.osc,
        r.cols[...],
        ghost_lanes(r.coords_ghost),
        r.mask_ghost[...],
        r.wbox,
    )
    r.put(r.geo_ghost)
    start_state(r.state, r.osc, own_rows)
    steps(
        ghost_chunks,
        ghosts,
        lambda step, slot: plain_basis(
            at(r.a_ghost, step), r.geo_ghost, r.osc, r.state, ghosts, step, own_rows
        ),
    )
    r.put(r.a_ghost)
    r.need(r.phi_ghost, r.filt_one)
    start_state(r.state, r.osc, own_rows)

    def kept_for_back(step, slot):
        full_basis(r.basis_ghost.at[step], r.geo_ghost, r.osc, r.state, ghosts, step)
        phi = r.phi_ghost
        scaled_rows(r.gs_ghost, step, step, r.filt_one, slice(0, channels), phi[:, :channels])
        scaled_rows(
            r.gv_ghost, step, step, r.filt_one, slice(channels, None), phi[:, channels:]
        )

    steps(ghost_chunks, ghosts, kept_for_back)
    r.put(r.basis_ghost, r.gs_ghost, r.gv_ghost)


def second_ghost_kernel(sizes, chunks, ghost_chunks, r):
    own_rows = r.node.shape[0] // 2
    r.table[...] = jnp.zeros_like(r.table)
    arrival = receive(r, r.table, sizes)
    r.need(r.filt_two, r.acc_two)
    arrival()
    r.put(r.table)

    r.need(r.a_ghost)
    second_messages(
        r.acc_two,
        lambda step, slot: at(r.a_ghost, step),
        r.plain,
        r.dotted,
        r.filt_two,
        r.table,
        ghost_chunks,
    )
    r.need(r.node, r.w_hidden, r.w_energy)
    hidden = dot3(r.node[...] + r.acc_two[...], r.w_hidden)
    _, slope, bend = silu_parts(hidden[:own_rows])
    live = lax.broadcasted_iota(jnp.int32, (own_rows, 1), 0) < r.counts[0]
    weight = jnp.where(live, r.w_energy[...], 0.0)
    bars = jnp.concatenate([weight * slope, weight * bend * hidden[own_rows:]], 0)
    r.cot[...] = dot3(bars, r.w_hidden, nt_dims)
    r.put(r.cot)
    r.need(r.at_ghost)
    table_cotangents(
        r.back_ghost,
        lambda step, slot: at(r.at_ghost, step),
        r.plain,
        r.dotted,
        r.filt_two,
        r.cot,
        chunks,
    )
    send_groups(r, r.back_ghost, sizes)


def second_back_kernel(chunks, ghost_chunks, r):
    own_rows = r.mask_own.shape[0]
    r.need(r.box, r.cols, r.mask_own)
    geometry_by_slot(r.geo, r.osc, r.cols[...], r.box[...], r.mask_own[...], r.wbox)
    r.need(r.cot, r.filt_two)

    start_state(r.state, r.osc, own_rows)

    def slot_basis(step, slot):
        kept = at(r.work, slot)
        plain_basis(kept, r.geo, r.osc, r.state, own_rows, step, own_rows)
        return kept

    table_cotangents(r.back, slot_basis, r.plain, r.dotted, r.filt_two, r.cot, chunks)
    r.put(r.back)
    split_cot = at(r.work, 0)
    put_split(split_cot, 0, r.cot[...])
    r.need(r.geo_own, r.osc_own, r.phi_two)

    start_state(r.state, r.osc_own, own_rows)

    def own_basis(step, slot):
        kept = r.basis.at[slot]
        full_basis(kept, r.geo_own, r.osc_own, r.state, own_rows, step)
        return kept

    second_pairs(
        r.pair,
        r.pair_own,
        split_cot,
        own_basis,
        r.plain,
        r.dotted,
        r.filt_two,
        r.phi_two,
        chunks,
    )
    r.put(r.pair_own)
    r.need(r.table, r.basis_ghost)

    second_pairs(
        r.pair,
        r.pair_ghost,
        split_cot,
        lambda step, slot: r.basis_ghost.at[step],
        r.plain,
        r.dotted,
        r.filt_two,
        r.table,
        ghost_chunks,
    )
    r.put(r.pair_ghost)


def first_back_ghost_kernel(sizes, r):
    own_rows = r.back.shape[0]
    channels = r.back.shape[1] // 2
    arrival = receive(r, r.table, sizes)
    r.need(r.send_rows, r.back)
    arrival()
    add_returned(r.back, r.table, r.send_rows, sizes)
    r.need(r.w_two_out, r.inner, r.w_two_in, r.cot)
    outer = dot3(
        jnp.concatenate([r.back[:, :channels], r.back[:, channels:]], 0), r.w_two_out, nt_dims
    )
    _, slope, bend = silu_parts(r.inner[:own_rows, :])
    pulled = jnp.concatenate(
        [
            outer[:own_rows] * slope,
            outer[own_rows:] * slope + outer[:own_rows] * bend * r.inner[own_rows:, :],
        ],
        0,
    )
    bars = r.cot[...] + dot3(pulled, r.w_two_in, nt_dims)
    put_split(r.bars, 0, bars)
    half = 3 * own_rows
    maps = r.maps
    bar, bar_dot = bars[0:own_rows], bars[own_rows:]
    r.need(r.maps, r.w_left, r.w_right)
    for i in range(3):
        a, b = i * own_rows, (i + 1) * own_rows
        left, left_dot = maps[a:b, :], maps[half + a : half + b, :]
        right = maps[2 * half + a : 2 * half + b, :]
        right_dot = maps[3 * half + a : 3 * half + b, :]
        for_left = jnp.concatenate([bar * right, bar_dot * right + bar * right_dot], 0)
        for_right = jnp.concatenate([bar * left, bar_dot * left + bar * left_dot], 0)
        both = dot3(for_left, r.w_left, nt_dims) + dot3(for_right, r.w_right, nt_dims)
        put_split(r.bars, (2 + i) * own_rows, both[:own_rows])
        put_split(r.bars, (5 + i) * own_rows, both[own_rows:])
    r.put(r.bars)
    r.need(r.geo_ghost, r.gs_ghost, r.gv_ghost, r.basis_ghost)
    first_pairs(
        r.pair,
        r.cots,
        r.bars,
        r.geo_ghost,
        lambda step, slot: r.basis_ghost.at[step],
        lambda step, slot: (at(r.gs_ghost, step), at(r.gv_ghost, step)),
        r.table.shape[0],
        r.basis_ghost.shape[0],
    )
    r.by_slot[...] = jnp.zeros_like(r.by_slot)
    r.need(r.pair_ghost)
    members = r.table.shape[0]
    offset_gradients(r.geo_ghost, r.pair, r.pair_ghost, members, r.by_slot, r.by_atom)
    r.put(r.by_atom)
    send_chunks(r, lambda number: r.by_slot, sizes)


def first_back_own_kernel(chunks, r):
    own_rows = r.by_atom.shape[0]
    channels = r.phi_own.shape[1] // 2
    r.need(r.phi_own, r.filt_one, r.geo_own, r.osc_own, r.bars)

    start_state(r.state, r.osc_own, own_rows)

    def basis_at(step, slot):
        kept = r.basis.at[slot]
        full_basis(kept, r.geo_own, r.osc_own, r.state, own_rows, step)
        return kept

    def factors_at(step, slot):
        phi, filt = r.phi_own, r.filt_one
        scaled_rows(r.gs, slot, step, filt, slice(0, channels), phi[:, :channels])
        scaled_rows(r.gv, slot, step, filt, slice(channels, None), phi[:, channels:])
        return at(r.gs, slot), at(r.gv, slot)

    first_pairs(r.pair, r.cots, r.bars, r.geo_own, basis_at, factors_at, own_rows, chunks)
    r.result[...] = jnp.zeros_like(r.result)
    r.need(r.pair_own, r.by_atom)
    offset_gradients(r.geo_own, r.pair, r.pair_own, own_rows, r.result, r.atoms)
    r.result[...] += (r.atoms[...] + r.by_atom[...]).T[0:8, :]
    r.put(r.result)


def finish_kernel(sizes, r):
    count = r.send_rows.shape[1] // 8
    own_rows = r.result.shape[1]
    r.table[...] = jnp.zeros_like(r.table)
    arrival = receive(r, r.table, sizes)
    lane = lax.broadcasted_iota(jnp.int32, (1, lanes), 1)
    r.need(r.send_rows, r.result)
    atom = lax.broadcasted_iota(jnp.int32, (own_rows, 8 * count), 0)
    place = jnp.where(atom == r.send_rows[...], 1.0, 0.0).astype(bf16)
    arrival()
    rows = jnp.zeros((8, lanes), f32)
    for number in range(8):
        shift = ((2 * number - 7) * count) % lanes
        moved = r.table[8 * number : 8 * number + 8, :]
        if shift:
            moved = pltpu.roll(moved, shift, 1)
        mine = (lane >= number * count) & (lane < (number + 1) * count)
        rows = jnp.where(mine, moved, rows)
    value = rows[:, : 8 * count]
    high, low = split(value)
    rest = (value - high.astype(f32) - low.astype(f32)).astype(bf16)
    total = r.result[...] + mxu(high, place, nt_dims) + mxu(low, place, nt_dims)
    total = total + mxu(rest, place, nt_dims)
    r.forces[...] = -total[0:3, :]
    r.product[...] = -total[3:6, :]
    r.put(r.forces, r.product)


class Refs:
    def need(self, *buffers):
        for buffer in buffers:
            for copy in self.loads.pop(id(buffer), ()):
                copy.wait()

    def put(self, *buffers):
        for buffer in buffers:
            for copy in self.stores[id(buffer)]:
                copy.start()
                self.started.append(copy)

    def close(self):
        for copy in [copy for group in self.loads.values() for copy in group] + self.started:
            copy.wait()


def as_tuple(value):
    return value if isinstance(value, tuple) else (value,)


class Slot:
    def __init__(self, name, value):
        self.name, self.arrays = name, as_tuple(value)


class Slots:
    def __setattr__(self, name, value):
        object.__setattr__(self, name, Slot(name, value))


def call(kernel, v, loads, outs, scratch, index=(), raw=(), scalars=(), sent=()):
    args, kinds, shapes, buffers = [], [], [], []
    copied = [(slot, pltpu.VMEM) for slot in loads] + [(slot, pltpu.SMEM) for slot in index]
    copies = 0
    for slot, space in copied:
        for array in slot.arrays:
            args.append(pltpu.with_memory_space_constraint(array, pltpu.HBM))
            kinds.append(pl.BlockSpec(memory_space=pltpu.HBM))
            buffers.append(space(array.shape, array.dtype))
            copies += 1
    for slot in raw + scalars:
        args.append(slot.arrays[0])
        kinds.append(pl.BlockSpec(memory_space=pl.ANY if slot in raw else pltpu.SMEM))
    for shape, types in outs.values():
        for kind in as_tuple(types):
            shapes.append(pltpu.HBM(shape, kind))
            buffers.append(pltpu.VMEM(shape, kind))
            copies += 1
    if sent:
        shapes.append(pltpu.HBM(sent, f32))
    for shape, types in scratch.values():
        for kind in as_tuple(types):
            buffers.append(pltpu.VMEM(shape, kind))
    buffers.append(pltpu.SemaphoreType.DMA((copies + 1,)))
    buffers.append(pltpu.SemaphoreType.DMA((8,)))

    def run(*refs):
        r = Refs()
        r.loads, r.stores, r.started = {}, {}, []
        ins, refs = refs[: len(args)], refs[len(args) :]
        targets, refs = refs[: len(shapes)], list(refs[len(shapes) :])
        ins, targets = list(ins), list(targets)
        r.moves = refs[-1]
        sems = [refs[-2].at[number] for number in range(copies)]

        def taken(name, number):
            group = tuple(refs.pop(0) for _ in range(number))
            value = group if number > 1 else group[0]
            setattr(r, name, value)
            return group, id(value)

        for slot, _ in copied:
            group, key = taken(slot.name, len(slot.arrays))
            r.loads[key] = []
            for buffer in group:
                copy = pltpu.make_async_copy(ins.pop(0), buffer, sems.pop(0))
                copy.start()
                r.loads[key].append(copy)
        for slot in raw + scalars:
            setattr(r, slot.name, ins.pop(0))
        for name, (shape, types) in outs.items():
            group, key = taken(name, len(as_tuple(types)))
            r.stores[key] = []
            for buffer in group:
                copy = pltpu.make_async_copy(buffer, targets.pop(0), sems.pop(0))
                r.stores[key].append(copy)
        if sent:
            r.out = targets.pop(0)
        for name, (shape, types) in scratch.items():
            taken(name, len(as_tuple(types)))
        kernel(r)
        r.close()

    results = pl.pallas_call(
        run,
        out_shape=shapes,
        in_specs=kinds,
        out_specs=[pl.BlockSpec(memory_space=pltpu.HBM) for _ in shapes],
        scratch_shapes=buffers,
        compiler_params=pltpu.CompilerParams(vmem_limit_bytes=48 * 1024 * 1024),
        name=kernel.func.__name__,
    )(*args)
    results = list(results)
    for name, (shape, types) in outs.items():
        group = tuple(results.pop(0) for _ in as_tuple(types))
        setattr(v, name, group)
    if sent:
        v.arrived = exchanged(results.pop(0))


def exchanged(buffer):
    return lax.all_to_all(buffer, ("bx", "by"), 0, 0)


def per_device(
    positions,
    tangent,
    embedding,
    counts,
    neighbours,
    send_rows,
    w_one_in,
    w_one_out,
    filter_one,
    w_left,
    w_right,
    w_two_in,
    w_two_out,
    filter_two,
    w_hidden,
    w_energy,
):
    w_energy = w_energy.reshape(1, w_energy.shape[0])
    v = Slots()
    for name, value in tuple(locals().items()):
        if value is not v:
            setattr(v, name, value)
    sizes = (lax.axis_size("bx"), lax.axis_size("by"))
    devices = sizes[0] * sizes[1]
    n = positions.shape[1]
    channels = embedding.shape[1]
    ghosts = send_rows.shape[1]
    orders = filter_one.shape[0]
    count = ghosts // 8
    scale = 1.0 / math.sqrt(neighbours.shape[0])
    part = functools.partial
    pair = (bf16, bf16)
    own_chunks, ghost_chunks = orders * n // wide, orders * ghosts // wide

    def factors(chunks):
        return ((chunks, wide, channels), pair)

    geometry = ((geo_slots, n, wide), f32)
    osc = ((osc_slots, n, wide), f32)
    state = ((2, n, wide), f32)
    wbox = ((n, wide), f32)
    pairs = ((8, n, wide), f32)
    cots = ((2, 8 * n, wide), f32)

    call(
        part(pack_kernel, sizes),
        v,
        (v.positions, v.tangent, v.embedding),
        dict(),
        dict(
            box=((n, n), f32),
            table=((n, channels + lanes), f32),
            stage=((ghosts, channels + lanes), f32),
        ),
        index=(v.send_rows,),
        sent=(devices, count, channels + lanes),
    )
    call(
        part(first_own_kernel, scale, own_chunks),
        v,
        (v.positions, v.tangent, v.neighbours, v.w_one_in, v.w_one_out, v.embedding, v.filter_one, v.filter_two),
        dict(
            box=((n, n), f32),
            cols=((n, n), f32),
            mask_own=((n, n), f32),
            mask_ghost=((ghosts, n), f32),
            filt_one=((orders, 2 * channels), f32),
            filt_two=((orders, channels), f32),
            acc=((8 * n, channels), f32),
            geo_own=geometry,
            osc_own=osc,
            phi_own=((n, 2 * channels), f32),
        ),
        dict(
            gs=factors(2),
            gv=factors(2),
            wbox=wbox,
            state=state,
            work=((2, 8 * n, wide), pair),
        ),
    )
    call(
        part(first_ghost_kernel, sizes, ghost_chunks),
        v,
        (v.w_one_in, v.cols, v.mask_ghost, v.w_one_out, v.filt_one, v.acc, v.w_left, v.w_right, v.embedding, v.w_two_in, v.w_two_out),
        dict(
            node=((2 * n, channels), f32),
            inner=((2 * n, channels), f32),
            maps=((12 * n, channels), f32),
            phi_two=((n, 2 * channels), f32),
            phi_ghost=((ghosts, 2 * channels), f32),
            coords_ghost=((ghosts, lanes), f32),
        ),
        dict(
            geo=geometry,
            osc=osc,
            gs=factors(2),
            gv=factors(2),
            wbox=wbox,
            state=state,
            work=((2, 8 * n, wide), pair),
            table=((ghosts, channels + lanes), f32),
            stage=((ghosts, 2 * channels), f32),
        ),
        index=(v.send_rows,),
        raw=(v.arrived,),
        sent=(devices, count, 2 * channels),
    )
    call(
        part(second_own_kernel, own_chunks, ghost_chunks),
        v,
        (v.geo_own, v.osc_own, v.phi_two, v.filt_two, v.box, v.cols, v.mask_own, v.mask_ghost, v.coords_ghost, v.phi_ghost, v.filt_one),
        dict(
            acc_two=((2 * n, channels), f32),
            at_ghost=((own_chunks, 2 * ghosts, wide), pair),
            geo_ghost=geometry,
            a_ghost=((ghost_chunks, 2 * n, wide), pair),
            basis_ghost=((ghost_chunks, 3, n, wide), f32),
            gs_ghost=factors(ghost_chunks),
            gv_ghost=factors(ghost_chunks),
        ),
        dict(
            geo=geometry,
            osc=osc,
            state=state,
            wbox=wbox,
            work=((2, 2 * n, wide), pair),
            plain=factors(2),
            dotted=factors(2),
        ),
    )
    call(
        part(second_ghost_kernel, sizes, own_chunks, ghost_chunks),
        v,
        (v.filt_two, v.acc_two, v.a_ghost, v.node, v.w_hidden, v.w_energy, v.at_ghost),
        dict(
            cot=((2 * n, channels), f32),
            table=((ghosts, 2 * channels), f32),
        ),
        dict(
            plain=factors(2),
            dotted=factors(2),
            back_ghost=((ghosts, 2 * channels), f32),
        ),
        raw=(v.arrived,),
        scalars=(v.counts,),
        sent=(devices, count, 2 * channels),
    )
    call(
        part(second_back_kernel, own_chunks, ghost_chunks),
        v,
        (v.box, v.cols, v.mask_own, v.cot, v.filt_two, v.geo_own, v.osc_own, v.phi_two, v.table, v.basis_ghost),
        dict(
            back=((n, 2 * channels), f32),
            pair_own=((2, n, lanes), f32),
            pair_ghost=((2, n, lanes), f32),
        ),
        dict(
            basis=((2, 3, n, wide), f32),
            geo=geometry,
            osc=osc,
            state=state,
            wbox=wbox,
            work=((2, 2 * n, wide), pair),
            plain=factors(2),
            dotted=factors(2),
            pair=((2, n, wide), f32),
        ),
    )
    call(
        part(first_back_ghost_kernel, sizes),
        v,
        (v.back, v.w_two_out, v.inner, v.w_two_in, v.cot, v.maps, v.w_left, v.w_right, v.geo_ghost, v.gs_ghost, v.gv_ghost, v.basis_ghost, v.pair_ghost),
        dict(
            bars=((8 * n, channels), pair),
            by_atom=((n, lanes), f32),
        ),
        dict(
            table=((ghosts, 2 * channels), f32),
            by_slot=((8, lanes), f32),
            pair=pairs,
            cots=cots,
        ),
        index=(v.send_rows,),
        raw=(v.arrived,),
        sent=(devices, 8, lanes),
    )
    call(
        part(first_back_own_kernel, own_chunks),
        v,
        (v.phi_own, v.filt_one, v.geo_own, v.osc_own, v.bars, v.pair_own, v.by_atom),
        dict(result=((8, lanes), f32)),
        dict(
            atoms=((n, lanes), f32),
            pair=pairs,
            cots=cots,
            state=state,
            gs=factors(2),
            gv=factors(2),
            basis=((2, 3, n, wide), f32),
        ),
    )
    call(
        part(finish_kernel, sizes),
        v,
        (v.send_rows, v.result),
        dict(forces=((3, n), f32), product=((3, n), f32)),
        dict(table=((64, lanes), f32)),
        raw=(v.arrived,),
    )
    return v.forces.arrays[0], v.product.arrays[0]


def solution(mesh):
    brick = ("bx", "by")
    placed = (
        P(None, brick),
        P(None, brick),
        P(brick, None),
        P(brick),
        P(None, brick),
        P(brick, None),
    ) + (P(),) * 10

    return jax.shard_map(
        per_device,
        mesh=mesh,
        in_specs=placed,
        out_specs=(P(None, brick), P(None, brick)),
        check_vma=False,
    )
```

```python
import functools
import math

import jax
import jax.numpy as jnp
from jax import lax
from jax.experimental import pallas as pl
from jax.experimental.pallas import tpu as pltpu
from jax.sharding import PartitionSpec as P

f32 = jnp.float32
bf16 = jnp.bfloat16
cutoff_radius = 3.0
softening = 0.01
wave = math.pi / cutoff_radius
offsets = ((-1, -1), (-1, 0), (-1, 1), (0, -1), (0, 1), (1, -1), (1, 0), (1, 1))
lanes = 128
wide = 256
row_block = 32
nn_dims = (((1,), (0,)), ((), ()))
nt_dims = (((1,), (1,)), ((), ()))

U, UD, DD, RI = 0, 3, 6, 7
geo_slots = 8
P0, P1, P2, SN, CS = 0, 1, 2, 3, 4
osc_slots = 5
own_group = 2
ghost_group = 5


def split(value):
    high = value.astype(bf16)
    return high, (value - high.astype(f32)).astype(bf16)


def mxu(left, right, dims=nn_dims):
    return lax.dot_general(left, right, dims, preferred_element_type=f32)


def three(lh, ll, rh, rl, dims=nn_dims):
    return mxu(lh, rh, dims) + mxu(ll, rh, dims) + mxu(lh, rl, dims)


def dot3(left, right, dims=nn_dims):
    return three(*split(left), *split(right[...]), dims)


def sigmoid(value):
    return 1.0 / (1.0 + jnp.exp(-jnp.maximum(value, -80.0)))


def silu_parts(value):
    gate = sigmoid(value)
    first = gate * (1.0 + value * (1.0 - gate))
    second = gate * (1.0 - gate) * (2.0 + value * (1.0 - 2.0 * gate))
    return value * gate, first, second


def sin_cos(theta):
    t = jnp.minimum(theta, 6.0) * 0.25
    x = t * t
    s = -1.0 / 39916800.0 + x * (1.0 / 6227020800.0)
    s = 1.0 / 362880.0 + x * s
    s = -1.0 / 5040.0 + x * s
    s = 1.0 / 120.0 + x * s
    s = -1.0 / 6.0 + x * s
    s = t + t * x * s
    c = 1.0 / 479001600.0 - x * (1.0 / 87178291200.0)
    c = -1.0 / 3628800.0 + x * c
    c = 1.0 / 40320.0 + x * c
    c = -1.0 / 720.0 + x * c
    c = 1.0 / 24.0 + x * c
    c = -0.5 + x * c
    c = 1.0 + x * c
    s, c = 2.0 * s * c, 1.0 - 2.0 * s * s
    return 2.0 * s * c, 1.0 - 2.0 * s * s


def doubled(value):
    return jnp.concatenate([value, value], 1)


def fill_geometry(geo, osc, first, second, mask_at, height):
    for start in range(0, height, row_block):
        rows = pl.ds(start, row_block)
        off = [first(i, start) - second(i, start) for i in range(3)]
        move = [first(i + 3, start) - second(i + 3, start) for i in range(3)]
        square = off[0] * off[0] + off[1] * off[1] + off[2] * off[2] + softening
        inverse = lax.rsqrt(square)
        inverse = inverse * (1.5 - 0.5 * square * inverse * inverse)
        theta = wave * (square * inverse)
        unit = [o * inverse for o in off]
        speed = unit[0] * move[0] + unit[1] * move[1] + unit[2] * move[2]
        for i in range(3):
            geo[U + i, rows, :] = unit[i]
            geo[UD + i, rows, :] = (move[i] - unit[i] * speed) * inverse
        sn, cs = sin_cos(theta)
        g0 = (0.5 * cs + 0.5) * inverse
        g1 = ((-0.5 * wave) * sn - g0) * inverse
        g2 = ((-0.5 * wave * wave) * cs - 2.0 * g1) * inverse
        mask = mask_at(start)
        geo[DD, rows, :] = speed
        geo[RI, rows, :] = inverse
        osc[P0, rows, :] = mask * g0
        osc[P1, rows, :] = mask * g1
        osc[P2, rows, :] = mask * g2
        osc[SN, rows, :] = sn
        osc[CS, rows, :] = cs


def start_state(state, osc, height, members):
    waves, turn = state
    near = lanes // members
    group = lax.broadcasted_iota(jnp.int32, (1, lanes), 1) // members
    for start in range(0, height, row_block):
        rows = pl.ds(start, row_block)
        sn, cs = osc[SN, rows, :], osc[CS, rows, :]
        s, c = sn, cs
        for half in range(wide // lanes):
            place = pl.ds(half * lanes, lanes)
            if half:
                s, c = s * cs + c * sn, c * cs - s * sn
            state_s, state_c = s, c
            for i in range(1, near):
                s, c = s * cs + c * sn, c * cs - s * sn
                state_s = jnp.where(group >= i, s, state_s)
                state_c = jnp.where(group >= i, c, state_c)
            waves[0, rows, place] = state_s
            waves[1, rows, place] = state_c
        turn[0, rows, :] = s
        turn[1, rows, :] = c


def order_factor(step, members):
    repeats = wide // members
    group = lax.broadcasted_iota(jnp.int32, (1, wide), 1) // members
    return (group + (step * repeats + 1)).astype(f32) * wave


def rotate(state, rows, s, c):
    waves, turn = state
    rs = doubled(turn[0, rows, :])
    rc = doubled(turn[1, rows, :])
    waves[0, rows, :] = s * rc + c * rs
    waves[1, rows, :] = c * rc - s * rs


def steps(count, members, body):
    group = own_group if members == lanes else ghost_group
    if group >= count:
        for step in range(count):
            body(step, step % 2)
        return

    def several(index, carry):
        for place in range(group):
            body(index * group + place, place % 2)
        return carry

    lax.fori_loop(0, count // group, several, 0)


def listed(nbr_ref, start, members):
    slot = lax.broadcasted_iota(jnp.int32, (members, lanes), 0) + start
    found = nbr_ref[0:1, :] == slot
    for k in range(1, nbr_ref.shape[0]):
        found = found | (nbr_ref[k : k + 1, :] == slot)
    return jnp.where(found, 1.0, 0.0).astype(f32)


def geometry_by_atom(geo, osc, columns, table, mask, wbox):
    repeats = lanes // mask.shape[0]
    table = jnp.concatenate([table] * repeats, 1)
    wbox[...] = jnp.concatenate([mask] * repeats, 0).T
    fill_geometry(
        geo,
        osc,
        lambda i, start: table[i : i + 1, :],
        lambda i, start: columns[start : start + row_block, i : i + 1],
        lambda start: wbox[start : start + row_block, :],
        geo.shape[1],
    )


def geometry_by_slot(geo, osc, columns, centre, mask):
    fill_geometry(
        geo,
        osc,
        lambda i, start: columns[start : start + row_block, i : i + 1],
        lambda i, start: centre[i : i + 1, :],
        lambda start: mask[start : start + row_block, :],
        mask.shape[0],
    )


def scaled_rows(pair, slot, step, filter_ref, columns, value):
    members = value.shape[0]
    for i in range(wide // members):
        row = filter_ref[pl.ds(step * (wide // members) + i, 1), columns]
        h, l = split(row * value)
        pair[0][slot, i * members : (i + 1) * members, :] = h
        pair[1][slot, i * members : (i + 1) * members, :] = l


def put_split(pair, start, value):
    h, l = split(value)
    pair[0][start : start + value.shape[0], :] = h
    pair[1][start : start + value.shape[0], :] = l


def at(pair, index):
    return pair[0].at[index], pair[1].at[index]


def basis_rows(kept, state, geo, osc, step, factor, start, height):
    rows = pl.ds(start, row_block)
    s, c = state[0][0, rows, :], state[0][1, rows, :]
    p0 = doubled(osc[P0, rows, :])
    b = p0 * s
    bd = (doubled(osc[P1, rows, :]) * s + factor * (p0 * c)) * doubled(geo[DD, rows, :])
    put_split(kept, start, b)
    put_split(kept, height + start, bd)
    rotate(state, rows, s, c)
    return b, bd


def first_messages(acc, geo, osc, state, work, scalars, vectors, phi, filt, members, chunks):
    height = geo.shape[1]
    channels = phi.shape[1] // 2
    top = 2 * height
    start_state(state, osc, height, members)

    def chunk(step, slot):
        factor = order_factor(step, members)
        scaled_rows(scalars, slot, step, filt, slice(0, channels), phi[:, :channels])
        scaled_rows(vectors, slot, step, filt, slice(channels, 2 * channels), phi[:, channels:])
        now = at(work, slot)
        for start in range(0, height, row_block):
            rows = pl.ds(start, row_block)
            b, bd = basis_rows(now, state, geo, osc, step, factor, start, height)
            for i in range(3):
                unit = doubled(geo[U + i, rows, :])
                put_split(now, (2 + i) * height + start, unit * b)
                put_split(
                    now, (5 + i) * height + start, doubled(geo[UD + i, rows, :]) * b + unit * bd
                )
        ah, al = now
        acc[:top, :] += three(ah[:top, :], al[:top, :], scalars[0][slot], scalars[1][slot])
        acc[top:, :] += three(ah[top:, :], al[top:, :], vectors[0][slot], vectors[1][slot])

    steps(chunks, members, chunk)


def second_messages(acc, basis_at, plain, dotted, filt, value, chunks):
    height = acc.shape[0] // 2
    channels = acc.shape[1]

    def chunk(step, slot):
        scaled_rows(plain, slot, step, filt, slice(None), value[:, :channels])
        scaled_rows(dotted, slot, step, filt, slice(None), value[:, channels:])
        ah, al = basis_at(step, slot)
        acc[...] += three(ah[...], al[...], plain[0][slot], plain[1][slot])
        acc[height:, :] += three(
            ah[:height, :], al[:height, :], dotted[0][slot], dotted[1][slot]
        )

    steps(chunks, value.shape[0], chunk)


def plain_basis(kept, geo, osc, state, members, step, height):
    factor = order_factor(step, members)
    for start in range(0, height, row_block):
        basis_rows(kept, state, geo, osc, step, factor, start, height)


def full_basis(geo, osc, state, members, step):
    factor = order_factor(step, members)

    def at_rows(rows):
        s, c = state[0][0, rows, :], state[0][1, rows, :]
        p0, p1 = doubled(osc[P0, rows, :]), doubled(osc[P1, rows, :])
        b = p0 * s
        b1 = p1 * s + factor * (p0 * c)
        b2 = doubled(osc[P2, rows, :]) * s + factor * (2.0 * p1 * c - factor * b)
        rotate(state, rows, s, c)
        return b, b1, b2 * doubled(geo[DD, rows, :])

    return at_rows


def table_cotangents(back, basis_at, plain, dotted, filt, cot, chunks):
    channels = filt.shape[1]
    own_rows = cot.shape[0] // 2
    height = back.shape[0]
    back[...] = jnp.zeros_like(back)

    def chunk(step, slot):
        scaled_rows(plain, slot, step, filt, slice(None), cot[0:own_rows, :])
        scaled_rows(dotted, slot, step, filt, slice(None), cot[own_rows:, :])
        ah, al = basis_at(step, slot)
        both = three(ah[...], al[...], plain[0][slot], plain[1][slot])
        back[:, :channels] += both[:height]
        back[:, channels:] += both[height:] + three(
            ah[:height, :], al[:height, :], dotted[0][slot], dotted[1][slot]
        )

    steps(chunks, own_rows, chunk)


def folded(value, members):
    total = value[:, :lanes] + value[:, lanes:]
    if members < lanes:
        total = total + pltpu.roll(total, members, 1)
    return total


def second_pairs(pair, result, split_cot, basis_at, plain, dotted, filt, value, chunks):
    height = pair.shape[1]
    channels = filt.shape[1]
    pair[...] = jnp.zeros_like(pair)
    ah, al = split_cot

    def chunk(step, slot):
        scaled_rows(plain, slot, step, filt, slice(None), value[:, :channels])
        scaled_rows(dotted, slot, step, filt, slice(None), value[:, channels:])
        both = three(ah[...], al[...], plain[0][slot], plain[1][slot], nt_dims)
        dot = both[height:] + three(
            ah[:height, :], al[:height, :], dotted[0][slot], dotted[1][slot], nt_dims
        )
        basis = basis_at(step)
        for start in range(0, height, row_block):
            rows = pl.ds(start, row_block)
            _, b1, b2d = basis(rows)
            g = both[start : start + row_block]
            pair[0, rows, :] += b1 * g
            pair[1, rows, :] += b2d * g + b1 * dot[start : start + row_block]

    members = value.shape[0]
    steps(chunks, members, chunk)
    result[0] = folded(pair[0], members)
    result[1] = folded(pair[1], members)


def first_pairs(pair, spaces, split_cot, geo, basis_at, factors_at, members, chunks):
    height = geo.shape[1]
    pair[...] = jnp.zeros_like(pair)
    ch, cl = split_cot
    top = 2 * height

    def chunk(step, slot):
        cots = spaces.at[slot]
        scalars, vectors = factors_at(step, slot)
        cots[:top, :] = three(
            ch[:top, :], cl[:top, :], scalars[0][...], scalars[1][...], nt_dims
        )
        cots[top:, :] = three(
            ch[top:, :], cl[top:, :], vectors[0][...], vectors[1][...], nt_dims
        )
        basis = basis_at(step)
        for start in range(0, height, row_block):
            rows = pl.ds(start, row_block)
            b, b1, b2d = basis(rows)
            b1d = b1 * doubled(geo[DD, rows, :])
            along = cots[start : start + row_block, :]
            along_dot = cots[height + start : height + start + row_block, :]
            for i in range(3):
                place = (2 + i) * height + start
                g = cots[place : place + row_block, :]
                place = (5 + i) * height + start
                gd = cots[place : place + row_block, :]
                unit = doubled(geo[U + i, rows, :])
                along = along + unit * g
                along_dot = along_dot + unit * gd + doubled(geo[UD + i, rows, :]) * g
                pair[2 + i, rows, :] += b * g
                pair[5 + i, rows, :] += b * gd + b1d * g
            pair[0, rows, :] += b1 * along
            pair[1, rows, :] += b2d * along + b1 * along_dot

    steps(chunks, members, chunk)


def neighbour_id(target, sizes):
    along = lax.axis_index("bx") + target[0]
    across = lax.axis_index("by") + target[1]
    inside = (along >= 0) & (along < sizes[0]) & (across >= 0) & (across < sizes[1])
    device = jnp.clip(along, 0, sizes[0] - 1) * sizes[1] + jnp.clip(across, 0, sizes[1] - 1)
    return device, inside


def send_chunks(r, chunk_at, sizes):
    for number, target in enumerate(offsets):
        device, inside = neighbour_id(target, sizes)
        copy = pltpu.make_async_copy(chunk_at(number), r.out.at[device], r.moves.at[number])

        @pl.when(inside)
        def _():
            copy.start()

    for number, target in enumerate(offsets):
        device, inside = neighbour_id(target, sizes)
        copy = pltpu.make_async_copy(chunk_at(number), r.out.at[device], r.moves.at[number])

        @pl.when(inside)
        def _():
            copy.wait()


def send_groups(r, table, sizes):
    count = r.out.shape[1]
    send_chunks(r, lambda number: table.at[number * count : (number + 1) * count, :], sizes)


def send_gathered(r, table, stage, send_ref, sizes):
    for slot in range(stage.shape[0]):
        stage[slot : slot + 1, :] = table[pl.ds(send_ref[0, slot], 1), :]
    send_groups(r, stage, sizes)


def receive(r, table, sizes):
    count = r.arrived.shape[1]
    for number, target in enumerate(offsets):
        device, inside = neighbour_id(target, sizes)

        @pl.when(inside)
        def _():
            table[number * count : (number + 1) * count, :] = r.arrived[device]


def add_returned(total, table, send_row):
    atom = lax.broadcasted_iota(jnp.int32, (total.shape[0], table.shape[0]), 0)
    place = jnp.where(atom == send_row, 1.0, 0.0).astype(bf16)
    high, low = split(table[...])
    rest = (table[...] - high.astype(f32) - low.astype(f32)).astype(bf16)
    total[...] += mxu(place, high) + mxu(place, low) + mxu(place, rest)


def offset_gradients(geo, pair, second, members, by_slot, by_atom):
    near = [folded(pair[i], members) for i in range(8)]
    height = geo.shape[1]
    units = [geo[U + i, :, :lanes] for i in range(3)]
    moves = [geo[UD + i, :, :lanes] for i in range(3)]
    inverse = geo[RI, :, :lanes]
    speed = geo[DD, :, :lanes]
    along = near[0] + second[0]
    along_dot = near[1] + second[1]
    turn, turn_dot = near[2:5], near[5:8]
    inner = units[0] * turn[0] + units[1] * turn[1] + units[2] * turn[2]
    inner_dot = sum(units[i] * turn_dot[i] + moves[i] * turn[i] for i in range(3))
    rate = speed * inverse
    lane = lax.broadcasted_iota(jnp.int32, (1, lanes), 1)
    sums = jnp.zeros((height, lanes), f32)
    for i in range(3):
        part = (turn[i] - units[i] * inner) * inverse
        grad = along * units[i] + part
        grad_dot = (
            along_dot * units[i]
            + along * moves[i]
            + (turn_dot[i] - moves[i] * inner - units[i] * inner_dot) * inverse
            - rate * part
        )
        for row, value in ((i, grad), (3 + i, grad_dot)):
            by_slot[row : row + 1, :] = jnp.sum(value, 0, keepdims=True)
            if members < lanes:
                value = jnp.where(lane < members, value, 0.0)
            sums = jnp.where(lane == row, -jnp.sum(value, 1, keepdims=True), sums)
    by_atom[...] = sums


def pack_kernel(sizes, r):
    channels = r.embedding.shape[1]
    r.box[...] = jnp.zeros_like(r.box)
    r.need(r.positions, r.tangent)
    r.box[0:3, :] = r.positions[...]
    r.box[3:6, :] = r.tangent[...]
    r.table[:, channels:] = r.box[...].T
    r.need(r.embedding)
    r.table[:, :channels] = r.embedding[...]
    r.need(r.send_rows)
    count = r.send_rows.shape[1] // 8
    gap = lanes // count
    for number in range(8):
        ends = jnp.zeros((1, lanes), f32)
        for p in range(count):
            row = r.table[pl.ds(r.send_rows[0, number * count + p], 1), :]
            r.stage[number, :, p * channels : (p + 1) * channels] = row[:, :channels]
            end = row[:, channels:]
            ends = ends + (pltpu.roll(end, p * gap, 1) if p else end)
        r.stage[number, :, count * channels :] = ends
    send_chunks(r, lambda number: r.stage.at[number], sizes)


def first_own_kernel(scale, chunks, r):
    own_rows = r.positions.shape[1]
    r.box[...] = jnp.zeros_like(r.box)
    r.need(r.positions, r.tangent, r.neighbours)
    r.box[0:3, :] = r.positions[...]
    r.box[3:6, :] = r.tangent[...]
    r.cols[...] = r.box[...].T
    r.mask_own[...] = listed(r.neighbours, 0, own_rows)
    r.mask_ghost[...] = listed(r.neighbours, own_rows, r.mask_ghost.shape[0])
    r.put(r.box, r.cols, r.mask_own, r.mask_ghost)
    r.cols_near[...] = r.cols[...]
    r.mask_near[...] = r.mask_ghost[...]
    geometry_by_atom(r.geo_own, r.osc_own, r.cols[...], r.box[...], r.mask_own[...], r.wbox)
    r.put(r.geo_own, r.osc_own)
    r.need(r.w_one_in, r.w_one_out, r.embedding, r.filter_one, r.filter_two)
    r.filt_one[...] = r.filter_one[...] * scale
    r.filt_two[...] = r.filter_two[...] * scale
    r.put(r.filt_one, r.filt_two)
    r.filt_near[...] = r.filt_one[...]
    r.in_near[...] = r.w_one_in[...]
    r.out_near[...] = r.w_one_out[...]
    r.phi_own[...] = dot3(silu_parts(dot3(r.embedding[...], r.w_one_in))[0], r.w_one_out)
    r.put(r.phi_own)
    r.acc[...] = jnp.zeros_like(r.acc)
    first_messages(
        r.acc,
        r.geo_own,
        r.osc_own,
        r.state,
        r.work,
        r.gs,
        r.gv,
        r.phi_own,
        r.filt_one,
        own_rows,
        chunks,
    )


def first_ghost_kernel(sizes, chunks, r):
    own_rows = r.embedding.shape[0]
    channels = r.embedding.shape[1]
    r.table[...] = jnp.zeros_like(r.table)
    count = r.table.shape[0] // 8
    gap = lanes // count
    for number, target in enumerate(offsets):
        device, inside = neighbour_id(target, sizes)

        @pl.when(inside)
        def _():
            chunk = r.arrived[device]
            ends = chunk[:, count * channels :]
            for p in range(count):
                at_row = slice(number * count + p, number * count + p + 1)
                r.table[at_row, :channels] = chunk[:, p * channels : (p + 1) * channels]
                r.table[at_row, channels:] = pltpu.roll(ends, lanes - p * gap, 1) if p else ends

    r.coords_ghost[...] = r.table[:, channels:]
    r.put(r.coords_ghost)
    r.phi_ghost[...] = dot3(
        silu_parts(dot3(r.table[:, :channels], r.in_near))[0], r.out_near
    )
    r.put(r.phi_ghost)
    members = r.mask_near.shape[0]
    geometry_by_atom(
        r.geo, r.osc, r.cols_near[...], ghost_lanes(r.coords_ghost), r.mask_near[...], r.wbox
    )
    first_messages(
        r.acc,
        r.geo,
        r.osc,
        r.state,
        r.work,
        r.gs,
        r.gv,
        r.phi_ghost,
        r.filt_near,
        members,
        chunks,
    )
    r.need(r.w_left, r.w_right, r.embedding, r.w_two_in, r.w_two_out, r.send_rows)
    top = 2 * own_rows
    half = 3 * own_rows
    acc, maps = r.acc, r.maps
    ah, al = split(acc[top:, :])
    maps[0 : 2 * half, :] = three(ah, al, *split(r.w_left[...]))
    maps[2 * half :, :] = three(ah, al, *split(r.w_right[...]))
    r.put(r.maps)
    total = r.embedding[...] + acc[0:own_rows, :]
    moved = acc[own_rows:top, :]
    for i in range(3):
        a, b = i * own_rows, (i + 1) * own_rows
        left, left_dot = maps[a:b, :], maps[half + a : half + b, :]
        right = maps[2 * half + a : 2 * half + b, :]
        right_dot = maps[3 * half + a : 3 * half + b, :]
        total = total + left * right
        moved = moved + left_dot * right + left * right_dot
    r.node[0:own_rows, :] = total
    r.node[own_rows:, :] = moved
    r.put(r.node)
    r.inner[...] = dot3(r.node[...], r.w_two_in)
    r.put(r.inner)
    value, slope, _ = silu_parts(r.inner[0:own_rows, :])
    outer = dot3(jnp.concatenate([value, slope * r.inner[own_rows:, :]], 0), r.w_two_out)
    r.phi_two[:, :channels] = outer[:own_rows]
    r.phi_two[:, channels:] = outer[own_rows:]
    r.put(r.phi_two)
    send_gathered(r, r.phi_two, r.stage, r.send_rows, sizes)


def ghost_lanes(coords):
    members = coords.shape[0]
    return jnp.concatenate([coords[...]] * (lanes // members), 0).T[:, :members]


def second_own_kernel(chunks, ghost_chunks, r):
    own_rows = r.mask_own.shape[0]
    ghosts = r.mask_ghost.shape[0]
    r.acc_two[...] = jnp.zeros_like(r.acc_two)
    r.need(r.geo_own, r.osc_own, r.filt_two, r.phi_two)
    r.filt_near[...] = r.filt_two[...]

    start_state(r.state, r.osc_own, own_rows, own_rows)

    def own_basis(step, slot):
        kept = at(r.work, slot)
        plain_basis(kept, r.geo_own, r.osc_own, r.state, own_rows, step, own_rows)
        return kept

    second_messages(r.acc_two, own_basis, r.plain, r.dotted, r.filt_two, r.phi_two, chunks)
    r.need(r.box, r.cols, r.mask_own, r.mask_ghost, r.coords_ghost)
    geometry_by_slot(r.geo, r.osc, r.coords_ghost[...], r.box[...], r.mask_ghost[...])
    start_state(r.state, r.osc, ghosts, own_rows)
    steps(
        chunks,
        own_rows,
        lambda step, slot: plain_basis(
            at(r.at_ghost, step), r.geo, r.osc, r.state, own_rows, step, ghosts
        ),
    )
    geometry_by_atom(
        r.geo_ghost,
        r.osc_ghost,
        r.cols[...],
        ghost_lanes(r.coords_ghost),
        r.mask_ghost[...],
        r.wbox,
    )
    r.put(r.geo_ghost)
    r.put(r.osc_ghost)
    start_state(r.state, r.osc_ghost, own_rows, ghosts)
    steps(
        ghost_chunks,
        ghosts,
        lambda step, slot: plain_basis(
            at(r.a_ghost, step), r.geo_ghost, r.osc_ghost, r.state, ghosts, step, own_rows
        ),
    )


def second_ghost_kernel(sizes, chunks, ghost_chunks, r):
    own_rows = r.node.shape[0] // 2
    r.table[...] = jnp.zeros_like(r.table)
    receive(r, r.table, sizes)
    r.put(r.table)

    second_messages(
        r.acc_two,
        lambda step, slot: at(r.a_ghost, step),
        r.plain,
        r.dotted,
        r.filt_near,
        r.table,
        ghost_chunks,
    )
    r.need(r.node, r.w_hidden, r.w_energy)
    hidden = dot3(r.node[...] + r.acc_two[...], r.w_hidden)
    _, slope, bend = silu_parts(hidden[:own_rows])
    live = lax.broadcasted_iota(jnp.int32, (own_rows, 1), 0) < r.counts[0]
    weight = jnp.where(live, r.w_energy[...], 0.0)
    bars = jnp.concatenate([weight * slope, weight * bend * hidden[own_rows:]], 0)
    r.cot[...] = dot3(bars, r.w_hidden, nt_dims)
    r.put(r.cot)
    table_cotangents(
        r.back_ghost,
        lambda step, slot: at(r.at_ghost, step),
        r.plain,
        r.dotted,
        r.filt_near,
        r.cot,
        chunks,
    )
    send_groups(r, r.back_ghost, sizes)


def second_back_kernel(chunks, ghost_chunks, r):
    own_rows = r.mask_own.shape[0]
    r.need(r.box, r.cols, r.mask_own)
    geometry_by_slot(r.geo, r.osc, r.cols[...], r.box[...], r.mask_own[...])
    r.need(r.cot, r.filt_two)

    start_state(r.state, r.osc, own_rows, own_rows)

    def slot_basis(step, slot):
        kept = at(r.work, slot)
        plain_basis(kept, r.geo, r.osc, r.state, own_rows, step, own_rows)
        return kept

    table_cotangents(r.back, slot_basis, r.plain, r.dotted, r.filt_two, r.cot, chunks)
    split_cot = at(r.work, 0)
    put_split(split_cot, 0, r.cot[...])
    r.need(r.geo_own, r.osc_own, r.phi_two)

    start_state(r.state, r.osc_own, own_rows, own_rows)

    second_pairs(
        r.pair,
        r.pair_own,
        split_cot,
        lambda step: full_basis(r.geo_own, r.osc_own, r.state, own_rows, step),
        r.plain,
        r.dotted,
        r.filt_two,
        r.phi_two,
        chunks,
    )
    r.put(r.pair_own)
    r.need(r.table, r.geo_ghost, r.osc_ghost)
    ghosts = r.table.shape[0]
    start_state(r.state, r.osc_ghost, own_rows, ghosts)


    second_pairs(
        r.pair,
        r.pair_ghost,
        split_cot,
        lambda step: full_basis(r.geo_ghost, r.osc_ghost, r.state, ghosts, step),
        r.plain,
        r.dotted,
        r.filt_two,
        r.table,
        ghost_chunks,
    )
    r.need(r.send_rows, r.w_two_out, r.inner)
    r.send_near[...] = r.send_rows[...]
    r.out_near[...] = r.w_two_out[...]
    r.inner_near[...] = r.inner[...]


def pairs_again(r, geo, osc, phi, chunks):
    members = phi.shape[0]
    channels = phi.shape[1] // 2
    start_state(r.state, osc, geo.shape[1], members)

    def basis_at(step):
        return full_basis(geo, osc, r.state, members, step)

    def factors_at(step, slot):
        scaled_rows(r.gs, slot, step, r.filt_one, slice(0, channels), phi[:, :channels])
        scaled_rows(r.gv, slot, step, r.filt_one, slice(channels, None), phi[:, channels:])
        return at(r.gs, slot), at(r.gv, slot)

    first_pairs(r.pair, r.cots, r.bars, geo, basis_at, factors_at, members, chunks)


def first_back_ghost_kernel(sizes, chunks, r):
    own_rows = r.back.shape[0]
    channels = r.back.shape[1] // 2
    r.table[...] = jnp.zeros_like(r.table)
    receive(r, r.table, sizes)
    add_returned(r.back, r.table, r.send_near[...])
    r.need(r.w_two_in, r.cot)
    outer = dot3(
        jnp.concatenate([r.back[:, :channels], r.back[:, channels:]], 0), r.out_near, nt_dims
    )
    _, slope, bend = silu_parts(r.inner_near[:own_rows, :])
    pulled = jnp.concatenate(
        [
            outer[:own_rows] * slope,
            outer[own_rows:] * slope + outer[:own_rows] * bend * r.inner_near[own_rows:, :],
        ],
        0,
    )
    bars = r.cot[...] + dot3(pulled, r.w_two_in, nt_dims)
    put_split(r.bars, 0, bars)
    half = 3 * own_rows
    maps = r.maps
    bar, bar_dot = bars[0:own_rows], bars[own_rows:]
    r.need(r.maps, r.w_left, r.w_right)
    for i in range(3):
        a, b = i * own_rows, (i + 1) * own_rows
        left, left_dot = maps[a:b, :], maps[half + a : half + b, :]
        right = maps[2 * half + a : 2 * half + b, :]
        right_dot = maps[3 * half + a : 3 * half + b, :]
        for_left = jnp.concatenate([bar * right, bar_dot * right + bar * right_dot], 0)
        for_right = jnp.concatenate([bar * left, bar_dot * left + bar * left_dot], 0)
        both = dot3(for_left, r.w_left, nt_dims) + dot3(for_right, r.w_right, nt_dims)
        put_split(r.bars, (2 + i) * own_rows, both[:own_rows])
        put_split(r.bars, (5 + i) * own_rows, both[own_rows:])
    r.put(r.bars)
    r.need(r.geo_ghost, r.osc_ghost, r.phi_ghost, r.filt_one)
    pairs_again(r, r.geo_ghost, r.osc_ghost, r.phi_ghost, chunks)
    r.by_slot[...] = jnp.zeros_like(r.by_slot)
    members = r.table.shape[0]
    offset_gradients(r.geo_ghost, r.pair, r.pair_ghost, members, r.by_slot, r.by_atom)
    r.put(r.by_atom)
    send_chunks(r, lambda number: r.by_slot, sizes)


def first_back_own_kernel(chunks, r):
    own_rows = r.by_atom.shape[0]
    r.need(r.phi_own, r.filt_one, r.geo_own, r.osc_own, r.bars)
    pairs_again(r, r.geo_own, r.osc_own, r.phi_own, chunks)
    r.result[...] = jnp.zeros_like(r.result)
    r.need(r.pair_own, r.by_atom)
    offset_gradients(r.geo_own, r.pair, r.pair_own, own_rows, r.result, r.atoms)
    r.result[...] += (r.atoms[...] + r.by_atom[...]).T[0:8, :]
    r.need(r.send_rows)
    r.send_near[...] = r.send_rows[...]


def finish_kernel(sizes, r):
    count = r.send_near.shape[1] // 8
    own_rows = r.result.shape[1]
    r.table[...] = jnp.zeros_like(r.table)
    receive(r, r.table, sizes)
    lane = lax.broadcasted_iota(jnp.int32, (1, lanes), 1)
    atom = lax.broadcasted_iota(jnp.int32, (own_rows, 8 * count), 0)
    place = jnp.where(atom == r.send_near[...], 1.0, 0.0).astype(bf16)
    rows = jnp.zeros((8, lanes), f32)
    for number in range(8):
        shift = ((2 * number - 7) * count) % lanes
        moved = r.table[8 * number : 8 * number + 8, :]
        if shift:
            moved = pltpu.roll(moved, shift, 1)
        mine = (lane >= number * count) & (lane < (number + 1) * count)
        rows = jnp.where(mine, moved, rows)
    value = rows[:, : 8 * count]
    high, low = split(value)
    rest = (value - high.astype(f32) - low.astype(f32)).astype(bf16)
    total = r.result[...] + mxu(high, place, nt_dims) + mxu(low, place, nt_dims)
    total = total + mxu(rest, place, nt_dims)
    r.forces[...] = -total[0:3, :]
    r.product[...] = -total[3:6, :]
    r.put(r.forces, r.product)


class Refs:
    def need(self, *buffers):
        for buffer in buffers:
            for copy in self.loads.pop(id(buffer), ()):
                copy.wait()

    def put(self, *buffers):
        for buffer in buffers:
            for copy in self.stores[id(buffer)]:
                copy.start()
                self.started.append(copy)

    def close(self):
        for copy in [copy for group in self.loads.values() for copy in group] + self.started:
            copy.wait()


def as_tuple(value):
    return value if isinstance(value, tuple) else (value,)


def flat(entry):
    if isinstance(entry, list):
        return entry
    return [(entry[0], kind) for kind in as_tuple(entry[1])]


class Slot:
    def __init__(self, name, value):
        self.name, self.arrays, self.near = name, as_tuple(value), False


class Slots:
    def __setattr__(self, name, value):
        object.__setattr__(self, name, Slot(name, value))


def call(kernel, v, loads, outs, scratch, index=(), raw=(), scalars=(), sent=(), near=None):
    near = near or dict()
    raw = raw + tuple(slot for slot in loads if slot.near)
    loads = tuple(slot for slot in loads if not slot.near)
    args, kinds, shapes, buffers = [], [], [], []
    copied = [(slot, pltpu.VMEM) for slot in loads] + [(slot, pltpu.SMEM) for slot in index]
    copies = 0
    for slot, space in copied:
        for array in slot.arrays:
            args.append(pltpu.with_memory_space_constraint(array, pltpu.HBM))
            kinds.append(pl.BlockSpec(memory_space=pltpu.HBM))
            buffers.append(space(array.shape, array.dtype))
            copies += 1
    for slot in raw + scalars:
        for array in slot.arrays:
            args.append(array)
            kinds.append(pl.BlockSpec(memory_space=pltpu.VMEM if slot in raw else pltpu.SMEM))
    for shape, types in outs.values():
        for kind in as_tuple(types):
            shapes.append(pltpu.HBM(shape, kind))
            buffers.append(pltpu.VMEM(shape, kind))
            copies += 1
    places = [pltpu.HBM] * len(shapes)
    for entry in near.values():
        for shape, kind in flat(entry):
            shapes.append(jax.ShapeDtypeStruct(shape, kind))
            places.append(pltpu.VMEM)
    if sent:
        shapes.append(pltpu.HBM(sent, f32))
        places.append(pltpu.HBM)
    for entry in scratch.values():
        for shape, kind in flat(entry):
            buffers.append(pltpu.VMEM(shape, kind))
    buffers.append(pltpu.SemaphoreType.DMA((copies + 1,)))
    buffers.append(pltpu.SemaphoreType.DMA((8,)))

    def run(*refs):
        r = Refs()
        r.loads, r.stores, r.started = {}, {}, []
        ins, refs = refs[: len(args)], refs[len(args) :]
        targets, refs = refs[: len(shapes)], list(refs[len(shapes) :])
        ins, targets = list(ins), list(targets)
        r.moves = refs[-1]
        sems = [refs[-2].at[number] for number in range(copies)]

        def taken(name, number):
            group = tuple(refs.pop(0) for _ in range(number))
            value = group if number > 1 else group[0]
            setattr(r, name, value)
            return group, id(value)

        for slot, _ in copied:
            group, key = taken(slot.name, len(slot.arrays))
            r.loads[key] = []
            for buffer in group:
                copy = pltpu.make_async_copy(ins.pop(0), buffer, sems.pop(0))
                copy.start()
                r.loads[key].append(copy)
        for slot in raw + scalars:
            group = tuple(ins.pop(0) for _ in slot.arrays)
            setattr(r, slot.name, group if len(group) > 1 else group[0])
        for name, (shape, types) in outs.items():
            group, key = taken(name, len(as_tuple(types)))
            r.stores[key] = []
            for buffer in group:
                copy = pltpu.make_async_copy(buffer, targets.pop(0), sems.pop(0))
                r.stores[key].append(copy)
        for name, entry in near.items():
            group = tuple(targets.pop(0) for _ in flat(entry))
            setattr(r, name, group if len(group) > 1 else group[0])
        if sent:
            r.out = targets.pop(0)
        for name, entry in scratch.items():
            taken(name, len(flat(entry)))
        kernel(r)
        r.close()

    results = pl.pallas_call(
        run,
        out_shape=shapes,
        in_specs=kinds,
        out_specs=[pl.BlockSpec(memory_space=place) for place in places],
        scratch_shapes=buffers,
        compiler_params=pltpu.CompilerParams(vmem_limit_bytes=20 * 1024 * 1024),
        name=kernel.func.__name__,
    )(*args)
    results = list(results)
    for name, (shape, types) in outs.items():
        group = tuple(results.pop(0) for _ in as_tuple(types))
        setattr(v, name, group)
    for name, entry in near.items():
        setattr(v, name, tuple(results.pop(0) for _ in flat(entry)))
        getattr(v, name).near = True
    if sent:
        v.arrived = exchanged(results.pop(0))


def exchanged(buffer):
    return lax.all_to_all(buffer, ("bx", "by"), 0, 0)


def per_device(
    positions,
    tangent,
    embedding,
    counts,
    neighbours,
    send_rows,
    w_one_in,
    w_one_out,
    filter_one,
    w_left,
    w_right,
    w_two_in,
    w_two_out,
    filter_two,
    w_hidden,
    w_energy,
):
    w_energy = w_energy.reshape(1, w_energy.shape[0])
    v = Slots()
    for name, value in tuple(locals().items()):
        if value is not v:
            setattr(v, name, value)
    sizes = (lax.axis_size("bx"), lax.axis_size("by"))
    devices = sizes[0] * sizes[1]
    n = positions.shape[1]
    channels = embedding.shape[1]
    ghosts = send_rows.shape[1]
    orders = filter_one.shape[0]
    count = ghosts // 8
    scale = 1.0 / math.sqrt(neighbours.shape[0])
    part = functools.partial
    pair = (bf16, bf16)
    own_chunks, ghost_chunks = orders * n // wide, orders * ghosts // wide

    def factors(chunks):
        return ((chunks, wide, channels), pair)

    geometry = ((geo_slots, n, lanes), f32)
    osc = ((osc_slots, n, lanes), f32)
    state = [((2, n, wide), f32), ((2, n, lanes), f32)]
    wbox = ((n, lanes), f32)
    pairs = ((8, n, wide), f32)
    cots = ((2, 8 * n, wide), f32)

    call(
        part(pack_kernel, sizes),
        v,
        (v.positions, v.tangent, v.embedding),
        dict(),
        dict(
            box=((n, n), f32),
            table=((n, channels + lanes), f32),
            stage=((8, 1, count * channels + lanes), f32),
        ),
        index=(v.send_rows,),
        sent=(devices, 1, count * channels + lanes),
    )
    call(
        part(first_own_kernel, scale, own_chunks),
        v,
        (v.positions, v.tangent, v.neighbours, v.w_one_in, v.w_one_out, v.embedding, v.filter_one, v.filter_two),
        dict(
            box=((n, n), f32),
            cols=((n, n), f32),
            mask_own=((n, n), f32),
            mask_ghost=((ghosts, n), f32),
            filt_one=((orders, 2 * channels), f32),
            filt_two=((orders, channels), f32),
            geo_own=geometry,
            osc_own=osc,
            phi_own=((n, 2 * channels), f32),
        ),
        dict(
            gs=factors(2),
            gv=factors(2),
            wbox=wbox,
            state=state,
            work=((2, 8 * n, wide), pair),
        ),
        near=dict(
            acc=((8 * n, channels), f32),
            cols_near=((n, n), f32),
            mask_near=((ghosts, n), f32),
            filt_near=((orders, 2 * channels), f32),
            in_near=((channels, channels), f32),
            out_near=((channels, 2 * channels), f32),
        ),
    )
    call(
        part(first_ghost_kernel, sizes, ghost_chunks),
        v,
        (v.cols_near, v.mask_near, v.filt_near, v.in_near, v.out_near, v.acc, v.w_left, v.w_right, v.embedding, v.w_two_in, v.w_two_out),
        dict(
            node=((2 * n, channels), f32),
            inner=((2 * n, channels), f32),
            maps=((12 * n, channels), f32),
            phi_two=((n, 2 * channels), f32),
            phi_ghost=((ghosts, 2 * channels), f32),
            coords_ghost=((ghosts, lanes), f32),
        ),
        dict(
            geo=geometry,
            osc=osc,
            gs=factors(2),
            gv=factors(2),
            wbox=wbox,
            state=state,
            work=((2, 8 * n, wide), pair),
            table=((ghosts, channels + lanes), f32),
            stage=((ghosts, 2 * channels), f32),
        ),
        index=(v.send_rows,),
        raw=(v.arrived,),
        sent=(devices, count, 2 * channels),
    )
    call(
        part(second_own_kernel, own_chunks, ghost_chunks),
        v,
        (v.geo_own, v.osc_own, v.phi_two, v.filt_two, v.box, v.cols, v.mask_own, v.mask_ghost, v.coords_ghost),
        dict(
            geo_ghost=geometry,
            osc_ghost=osc,
        ),
        dict(
            geo=geometry,
            osc=osc,
            state=state,
            wbox=wbox,
            work=((2, 2 * n, wide), pair),
            plain=factors(2),
            dotted=factors(2),
        ),
        near=dict(
            acc_two=((2 * n, channels), f32),
            at_ghost=((own_chunks, 2 * ghosts, wide), pair),
            a_ghost=((ghost_chunks, 2 * n, wide), pair),
            filt_near=((orders, channels), f32),
        ),
    )
    call(
        part(second_ghost_kernel, sizes, own_chunks, ghost_chunks),
        v,
        (v.filt_near, v.acc_two, v.a_ghost, v.node, v.w_hidden, v.w_energy, v.at_ghost),
        dict(
            cot=((2 * n, channels), f32),
            table=((ghosts, 2 * channels), f32),
        ),
        dict(
            plain=factors(2),
            dotted=factors(2),
            back_ghost=((ghosts, 2 * channels), f32),
        ),
        raw=(v.arrived,),
        scalars=(v.counts,),
        sent=(devices, count, 2 * channels),
    )
    call(
        part(second_back_kernel, own_chunks, ghost_chunks),
        v,
        (v.box, v.cols, v.mask_own, v.cot, v.filt_two, v.geo_own, v.osc_own, v.phi_two, v.table, v.geo_ghost, v.osc_ghost, v.send_rows, v.w_two_out, v.inner),
        dict(
            pair_own=((2, n, lanes), f32),
        ),
        dict(
            geo=geometry,
            osc=osc,
            state=state,
            wbox=wbox,
            work=((2, 2 * n, wide), pair),
            plain=factors(2),
            dotted=factors(2),
            pair=((2, n, wide), f32),
        ),
        near=dict(
            back=((n, 2 * channels), f32),
            pair_ghost=((2, n, lanes), f32),
            send_near=((1, ghosts), jnp.int32),
            out_near=((channels, channels), f32),
            inner_near=((2 * n, channels), f32),
        ),
    )
    call(
        part(first_back_ghost_kernel, sizes, ghost_chunks),
        v,
        (v.send_near, v.back, v.out_near, v.inner_near, v.w_two_in, v.cot, v.maps, v.w_left, v.w_right, v.phi_ghost, v.filt_one, v.osc_ghost, v.geo_ghost, v.pair_ghost),
        dict(
            bars=((8 * n, channels), pair),
            by_atom=((n, lanes), f32),
        ),
        dict(
            table=((ghosts, 2 * channels), f32),
            by_slot=((8, lanes), f32),
            pair=pairs,
            cots=cots,
            state=state,
            gs=factors(2),
            gv=factors(2),
        ),
        raw=(v.arrived,),
        sent=(devices, 8, lanes),
    )
    call(
        part(first_back_own_kernel, own_chunks),
        v,
        (v.phi_own, v.filt_one, v.geo_own, v.osc_own, v.bars, v.pair_own, v.by_atom, v.send_rows),
        dict(),
        dict(
            atoms=((n, lanes), f32),
            pair=pairs,
            cots=cots,
            state=state,
            gs=factors(2),
            gv=factors(2),
        ),
        near=dict(result=((8, lanes), f32), send_near=((1, ghosts), jnp.int32)),
    )
    call(
        part(finish_kernel, sizes),
        v,
        (v.send_near, v.result),
        dict(forces=((3, n), f32), product=((3, n), f32)),
        dict(table=((64, lanes), f32)),
        raw=(v.arrived,),
    )
    return v.forces.arrays[0], v.product.arrays[0]


def solution(mesh):
    brick = ("bx", "by")
    placed = (
        P(None, brick),
        P(None, brick),
        P(brick, None),
        P(brick),
        P(None, brick),
        P(brick, None),
    ) + (P(),) * 10

    return jax.shard_map(
        per_device,
        mesh=mesh,
        in_specs=placed,
        out_specs=(P(None, brick), P(None, brick)),
        check_vma=False,
    )
```

```python
import functools
import math

import jax
import jax.numpy as jnp
from jax import lax
from jax.experimental import pallas as pl
from jax.experimental.pallas import tpu as pltpu
from jax.sharding import PartitionSpec as P

f32 = jnp.float32
bf16 = jnp.bfloat16
cutoff_radius = 3.0
softening = 0.01
wave = math.pi / cutoff_radius
offsets = ((-1, -1), (-1, 0), (-1, 1), (0, -1), (0, 1), (1, -1), (1, 0), (1, 1))
lanes = 128
wide = 256
row_block = 32
nn_dims = (((1,), (0,)), ((), ()))
nt_dims = (((1,), (1,)), ((), ()))

U, UD, DD, RI = 0, 3, 6, 7
geo_slots = 8
P0, P1, P2, SN, CS = 0, 1, 2, 3, 4
osc_slots = 5
own_group = 2
ghost_group = 5


def split(value):
    high = value.astype(bf16)
    return high, (value - high.astype(f32)).astype(bf16)


def mxu(left, right, dims=nn_dims):
    return lax.dot_general(left, right, dims, preferred_element_type=f32)


def three(lh, ll, rh, rl, dims=nn_dims):
    return mxu(lh, rh, dims) + mxu(ll, rh, dims) + mxu(lh, rl, dims)


def dot3(left, right, dims=nn_dims):
    return three(*split(left), *split(right[...]), dims)


def sigmoid(value):
    return 1.0 / (1.0 + jnp.exp(-jnp.maximum(value, -80.0)))


def silu_parts(value):
    gate = sigmoid(value)
    first = gate * (1.0 + value * (1.0 - gate))
    second = gate * (1.0 - gate) * (2.0 + value * (1.0 - 2.0 * gate))
    return value * gate, first, second


def sin_cos(theta):
    t = jnp.minimum(theta, 6.0) * 0.25
    x = t * t
    s = -1.0 / 39916800.0 + x * (1.0 / 6227020800.0)
    s = 1.0 / 362880.0 + x * s
    s = -1.0 / 5040.0 + x * s
    s = 1.0 / 120.0 + x * s
    s = -1.0 / 6.0 + x * s
    s = t + t * x * s
    c = 1.0 / 479001600.0 - x * (1.0 / 87178291200.0)
    c = -1.0 / 3628800.0 + x * c
    c = 1.0 / 40320.0 + x * c
    c = -1.0 / 720.0 + x * c
    c = 1.0 / 24.0 + x * c
    c = -0.5 + x * c
    c = 1.0 + x * c
    s, c = 2.0 * s * c, 1.0 - 2.0 * s * s
    return 2.0 * s * c, 1.0 - 2.0 * s * s


def doubled(value):
    return jnp.concatenate([value, value], 1)


def fill_geometry(geo, osc, first, second, mask_at, height):
    for start in range(0, height, row_block):
        rows = pl.ds(start, row_block)
        off = [first(i, start) - second(i, start) for i in range(3)]
        move = [first(i + 3, start) - second(i + 3, start) for i in range(3)]
        square = off[0] * off[0] + off[1] * off[1] + off[2] * off[2] + softening
        inverse = lax.rsqrt(square)
        inverse = inverse * (1.5 - 0.5 * square * inverse * inverse)
        theta = wave * (square * inverse)
        unit = [o * inverse for o in off]
        speed = unit[0] * move[0] + unit[1] * move[1] + unit[2] * move[2]
        for i in range(3):
            geo[U + i, rows, :] = unit[i]
            geo[UD + i, rows, :] = (move[i] - unit[i] * speed) * inverse
        sn, cs = sin_cos(theta)
        g0 = (0.5 * cs + 0.5) * inverse
        g1 = ((-0.5 * wave) * sn - g0) * inverse
        g2 = ((-0.5 * wave * wave) * cs - 2.0 * g1) * inverse
        mask = mask_at(start)
        geo[DD, rows, :] = speed
        geo[RI, rows, :] = inverse
        osc[P0, rows, :] = mask * g0
        osc[P1, rows, :] = mask * g1
        osc[P2, rows, :] = mask * g2
        osc[SN, rows, :] = sn
        osc[CS, rows, :] = cs


def start_state(state, osc, height, members):
    waves, turn = state
    near = lanes // members
    group = lax.broadcasted_iota(jnp.int32, (1, lanes), 1) // members
    for start in range(0, height, row_block):
        rows = pl.ds(start, row_block)
        sn, cs = osc[SN, rows, :], osc[CS, rows, :]
        s, c = sn, cs
        for half in range(wide // lanes):
            place = pl.ds(half * lanes, lanes)
            if half:
                s, c = s * cs + c * sn, c * cs - s * sn
            state_s, state_c = s, c
            for i in range(1, near):
                s, c = s * cs + c * sn, c * cs - s * sn
                state_s = jnp.where(group >= i, s, state_s)
                state_c = jnp.where(group >= i, c, state_c)
            waves[0, rows, place] = state_s
            waves[1, rows, place] = state_c
        turn[0, rows, :] = s
        turn[1, rows, :] = c


def order_factor(step, members):
    repeats = wide // members
    group = lax.broadcasted_iota(jnp.int32, (1, wide), 1) // members
    return (group + (step * repeats + 1)).astype(f32) * wave


def rotate(state, rows, s, c):
    waves, turn = state
    rs = doubled(turn[0, rows, :])
    rc = doubled(turn[1, rows, :])
    waves[0, rows, :] = s * rc + c * rs
    waves[1, rows, :] = c * rc - s * rs


def steps(count, members, body):
    group = own_group if members == lanes else ghost_group
    if group >= count:
        for step in range(count):
            body(step, step % 2)
        return

    def several(index, carry):
        for place in range(group):
            body(index * group + place, place % 2)
        return carry

    lax.fori_loop(0, count // group, several, 0)


def listed(nbr_ref, start, members):
    slot = lax.broadcasted_iota(jnp.int32, (members, lanes), 0) + start
    found = nbr_ref[0:1, :] == slot
    for k in range(1, nbr_ref.shape[0]):
        found = found | (nbr_ref[k : k + 1, :] == slot)
    return jnp.where(found, 1.0, 0.0).astype(f32)


def fill_mask(wbox, mask):
    wbox[...] = jnp.concatenate([mask] * (lanes // mask.shape[0]), 0).T


def geometry_by_atom(geo, osc, columns, table, wbox):
    table = jnp.concatenate([table] * (lanes // table.shape[1]), 1)
    fill_geometry(
        geo,
        osc,
        lambda i, start: table[i : i + 1, :],
        lambda i, start: columns[start : start + row_block, i : i + 1],
        lambda start: wbox[start : start + row_block, :],
        geo.shape[1],
    )


def picked(place, value):
    high, low = split(value)
    rest = (value - high.astype(f32) - low.astype(f32)).astype(bf16)
    return mxu(place, high) + mxu(place, low) + mxu(place, rest)


def geometry_by_slot(geo, osc, columns, centre, mask):
    fill_geometry(
        geo,
        osc,
        lambda i, start: columns[start : start + row_block, i : i + 1],
        lambda i, start: centre[i : i + 1, :],
        lambda start: mask[start : start + row_block, :],
        mask.shape[0],
    )


def scaled_rows(pair, slot, step, filter_ref, columns, value):
    members = value.shape[0]
    for i in range(wide // members):
        row = filter_ref[pl.ds(step * (wide // members) + i, 1), columns]
        h, l = split(row * value)
        pair[0][slot, i * members : (i + 1) * members, :] = h
        pair[1][slot, i * members : (i + 1) * members, :] = l


def put_split(pair, start, value):
    h, l = split(value)
    pair[0][start : start + value.shape[0], :] = h
    pair[1][start : start + value.shape[0], :] = l


def at(pair, index):
    return pair[0].at[index], pair[1].at[index]


def basis_rows(kept, state, geo, osc, step, factor, start, height):
    rows = pl.ds(start, row_block)
    s, c = state[0][0, rows, :], state[0][1, rows, :]
    p0 = doubled(osc[P0, rows, :])
    b = p0 * s
    bd = (doubled(osc[P1, rows, :]) * s + factor * (p0 * c)) * doubled(geo[DD, rows, :])
    put_split(kept, start, b)
    put_split(kept, height + start, bd)
    rotate(state, rows, s, c)
    return b, bd


def first_messages(acc, geo, osc, state, work, scalars, vectors, phi, filt, members, chunks):
    height = geo.shape[1]
    channels = phi.shape[1] // 2
    top = 2 * height
    start_state(state, osc, height, members)

    def chunk(step, slot):
        factor = order_factor(step, members)
        scaled_rows(scalars, slot, step, filt, slice(0, channels), phi[:, :channels])
        scaled_rows(vectors, slot, step, filt, slice(channels, 2 * channels), phi[:, channels:])
        now = at(work, slot)
        for start in range(0, height, row_block):
            rows = pl.ds(start, row_block)
            b, bd = basis_rows(now, state, geo, osc, step, factor, start, height)
            for i in range(3):
                unit = doubled(geo[U + i, rows, :])
                put_split(now, (2 + i) * height + start, unit * b)
                put_split(
                    now, (5 + i) * height + start, doubled(geo[UD + i, rows, :]) * b + unit * bd
                )
        ah, al = now
        acc[:top, :] += three(ah[:top, :], al[:top, :], scalars[0][slot], scalars[1][slot])
        acc[top:, :] += three(ah[top:, :], al[top:, :], vectors[0][slot], vectors[1][slot])

    steps(chunks, members, chunk)


def second_messages(acc, basis_at, plain, dotted, filt, value, chunks):
    height = acc.shape[0] // 2
    channels = acc.shape[1]

    def chunk(step, slot):
        scaled_rows(plain, slot, step, filt, slice(None), value[:, :channels])
        scaled_rows(dotted, slot, step, filt, slice(None), value[:, channels:])
        ah, al = basis_at(step, slot)
        acc[...] += three(ah[...], al[...], plain[0][slot], plain[1][slot])
        acc[height:, :] += three(
            ah[:height, :], al[:height, :], dotted[0][slot], dotted[1][slot]
        )

    steps(chunks, value.shape[0], chunk)


def plain_basis(kept, geo, osc, state, members, step, height):
    factor = order_factor(step, members)
    for start in range(0, height, row_block):
        basis_rows(kept, state, geo, osc, step, factor, start, height)


def full_basis(geo, osc, state, members, step):
    factor = order_factor(step, members)

    def at_rows(rows):
        s, c = state[0][0, rows, :], state[0][1, rows, :]
        p0, p1 = doubled(osc[P0, rows, :]), doubled(osc[P1, rows, :])
        b = p0 * s
        b1 = p1 * s + factor * (p0 * c)
        b2 = doubled(osc[P2, rows, :]) * s + factor * (2.0 * p1 * c - factor * b)
        rotate(state, rows, s, c)
        return b, b1, b2 * doubled(geo[DD, rows, :])

    return at_rows


def table_cotangents(back, basis_at, plain, dotted, filt, cot, chunks):
    channels = filt.shape[1]
    own_rows = cot.shape[0] // 2
    height = back.shape[0]
    back[...] = jnp.zeros_like(back)

    def chunk(step, slot):
        scaled_rows(plain, slot, step, filt, slice(None), cot[0:own_rows, :])
        scaled_rows(dotted, slot, step, filt, slice(None), cot[own_rows:, :])
        ah, al = basis_at(step, slot)
        both = three(ah[...], al[...], plain[0][slot], plain[1][slot])
        back[:, :channels] += both[:height]
        back[:, channels:] += both[height:] + three(
            ah[:height, :], al[:height, :], dotted[0][slot], dotted[1][slot]
        )

    steps(chunks, own_rows, chunk)


def folded(value, members):
    total = value[:, :lanes] + value[:, lanes:]
    if members < lanes:
        total = total + pltpu.roll(total, members, 1)
    return total


def second_pairs(pair, result, split_cot, basis_at, plain, dotted, filt, value, chunks):
    height = pair.shape[1]
    channels = filt.shape[1]
    pair[...] = jnp.zeros_like(pair)
    ah, al = split_cot

    def chunk(step, slot):
        scaled_rows(plain, slot, step, filt, slice(None), value[:, :channels])
        scaled_rows(dotted, slot, step, filt, slice(None), value[:, channels:])
        both = three(ah[...], al[...], plain[0][slot], plain[1][slot], nt_dims)
        dot = both[height:] + three(
            ah[:height, :], al[:height, :], dotted[0][slot], dotted[1][slot], nt_dims
        )
        basis = basis_at(step)
        for start in range(0, height, row_block):
            rows = pl.ds(start, row_block)
            _, b1, b2d = basis(rows)
            g = both[start : start + row_block]
            pair[0, rows, :] += b1 * g
            pair[1, rows, :] += b2d * g + b1 * dot[start : start + row_block]

    members = value.shape[0]
    steps(chunks, members, chunk)
    result[0] = folded(pair[0], members)
    result[1] = folded(pair[1], members)


def first_pairs(pair, spaces, split_cot, geo, basis_at, factors_at, members, chunks):
    height = geo.shape[1]
    pair[...] = jnp.zeros_like(pair)
    ch, cl = split_cot
    top = 2 * height

    def chunk(step, slot):
        cots = spaces.at[slot]
        scalars, vectors = factors_at(step, slot)
        cots[:top, :] = three(
            ch[:top, :], cl[:top, :], scalars[0][...], scalars[1][...], nt_dims
        )
        cots[top:, :] = three(
            ch[top:, :], cl[top:, :], vectors[0][...], vectors[1][...], nt_dims
        )
        basis = basis_at(step)
        for start in range(0, height, row_block):
            rows = pl.ds(start, row_block)
            b, b1, b2d = basis(rows)
            b1d = b1 * doubled(geo[DD, rows, :])
            along = cots[start : start + row_block, :]
            along_dot = cots[height + start : height + start + row_block, :]
            for i in range(3):
                place = (2 + i) * height + start
                g = cots[place : place + row_block, :]
                place = (5 + i) * height + start
                gd = cots[place : place + row_block, :]
                unit = doubled(geo[U + i, rows, :])
                along = along + unit * g
                along_dot = along_dot + unit * gd + doubled(geo[UD + i, rows, :]) * g
                pair[2 + i, rows, :] += b * g
                pair[5 + i, rows, :] += b * gd + b1d * g
            pair[0, rows, :] += b1 * along
            pair[1, rows, :] += b2d * along + b1 * along_dot

    steps(chunks, members, chunk)


def neighbour_id(target, sizes):
    along = lax.axis_index("bx") + target[0]
    across = lax.axis_index("by") + target[1]
    inside = (along >= 0) & (along < sizes[0]) & (across >= 0) & (across < sizes[1])
    device = jnp.clip(along, 0, sizes[0] - 1) * sizes[1] + jnp.clip(across, 0, sizes[1] - 1)
    return device, inside


def send_chunks(r, chunk_at, sizes):
    for number, target in enumerate(offsets):
        device, inside = neighbour_id(target, sizes)
        copy = pltpu.make_async_copy(chunk_at(number), r.out.at[device], r.moves.at[number])

        @pl.when(inside)
        def _():
            copy.start()

    for number, target in enumerate(offsets):
        device, inside = neighbour_id(target, sizes)
        copy = pltpu.make_async_copy(chunk_at(number), r.out.at[device], r.moves.at[number])

        @pl.when(inside)
        def _():
            copy.wait()


def send_groups(r, table, sizes):
    count = r.out.shape[1]
    send_chunks(r, lambda number: table.at[number * count : (number + 1) * count, :], sizes)


def send_gathered(r, table, stage, send_ref, sizes):
    for slot in range(stage.shape[0]):
        stage[slot : slot + 1, :] = table[pl.ds(send_ref[0, slot], 1), :]
    send_groups(r, stage, sizes)


def receive(r, table, sizes):
    count = r.arrived.shape[1]
    for number, target in enumerate(offsets):
        device, inside = neighbour_id(target, sizes)

        @pl.when(inside)
        def _():
            table[number * count : (number + 1) * count, :] = r.arrived[device]


def add_returned(total, table, send_row):
    atom = lax.broadcasted_iota(jnp.int32, (total.shape[0], table.shape[0]), 0)
    place = jnp.where(atom == send_row, 1.0, 0.0).astype(bf16)
    high, low = split(table[...])
    rest = (table[...] - high.astype(f32) - low.astype(f32)).astype(bf16)
    total[...] += mxu(place, high) + mxu(place, low) + mxu(place, rest)


def offset_gradients(geo, pair, second, members, by_slot, by_atom):
    near = [folded(pair[i], members) for i in range(8)]
    height = geo.shape[1]
    units = [geo[U + i, :, :lanes] for i in range(3)]
    moves = [geo[UD + i, :, :lanes] for i in range(3)]
    inverse = geo[RI, :, :lanes]
    speed = geo[DD, :, :lanes]
    along = near[0] + second[0]
    along_dot = near[1] + second[1]
    turn, turn_dot = near[2:5], near[5:8]
    inner = units[0] * turn[0] + units[1] * turn[1] + units[2] * turn[2]
    inner_dot = sum(units[i] * turn_dot[i] + moves[i] * turn[i] for i in range(3))
    rate = speed * inverse
    lane = lax.broadcasted_iota(jnp.int32, (1, lanes), 1)
    sums = jnp.zeros((height, lanes), f32)
    for i in range(3):
        part = (turn[i] - units[i] * inner) * inverse
        grad = along * units[i] + part
        grad_dot = (
            along_dot * units[i]
            + along * moves[i]
            + (turn_dot[i] - moves[i] * inner - units[i] * inner_dot) * inverse
            - rate * part
        )
        for row, value in ((i, grad), (3 + i, grad_dot)):
            by_slot[row : row + 1, :] = jnp.sum(value, 0, keepdims=True)
            if members < lanes:
                value = jnp.where(lane < members, value, 0.0)
            sums = jnp.where(lane == row, -jnp.sum(value, 1, keepdims=True), sums)
    by_atom[...] = sums


def pack_kernel(sizes, r):
    channels = r.embedding.shape[1]
    r.box[...] = jnp.zeros_like(r.box)
    r.need(r.positions, r.tangent)
    r.box[0:3, :] = r.positions[...]
    r.box[3:6, :] = r.tangent[...]
    r.table[:, channels:] = r.box[...].T
    r.need(r.embedding)
    r.table[:, :channels] = r.embedding[...]
    r.need(r.send_rows)
    count = r.send_rows.shape[1] // 8
    gap = lanes // count
    for number in range(8):
        ends = jnp.zeros((1, lanes), f32)
        for p in range(count):
            row = r.table[pl.ds(r.send_rows[0, number * count + p], 1), :]
            r.stage[number, :, p * channels : (p + 1) * channels] = row[:, :channels]
            end = row[:, channels:]
            ends = ends + (pltpu.roll(end, p * gap, 1) if p else end)
        r.stage[number, :, count * channels :] = ends
    send_chunks(r, lambda number: r.stage.at[number], sizes)


def first_own_kernel(scale, chunks, r):
    own_rows = r.positions.shape[1]
    ghosts = r.mask_ghost.shape[0]
    r.box[...] = jnp.zeros_like(r.box)
    r.need(r.positions, r.tangent, r.neighbours)
    r.box[0:3, :] = r.positions[...]
    r.box[3:6, :] = r.tangent[...]
    r.cols[...] = r.box[...].T
    r.mask_own[...] = listed(r.neighbours, 0, own_rows)
    r.mask_ghost[...] = listed(r.neighbours, own_rows, ghosts)
    r.put(r.box, r.cols, r.mask_own, r.mask_ghost)
    fill_mask(r.wbox, r.mask_own[...])
    geometry_by_atom(r.geo_own, r.osc_own, r.cols[...], r.box[...], r.wbox)
    r.put(r.geo_own, r.osc_own)
    r.need(r.w_one_in, r.w_one_out, r.embedding, r.filter_one, r.filter_two, r.send_rows)
    r.filt_one[...] = r.filter_one[...] * scale
    r.filt_two[...] = r.filter_two[...] * scale
    r.put(r.filt_one, r.filt_two)
    r.filt_near[...] = r.filt_one[...]
    r.in_near[...] = r.w_one_in[...]
    r.out_near[...] = r.w_one_out[...]
    r.phi_own[...] = dot3(silu_parts(dot3(r.embedding[...], r.w_one_in))[0], r.w_one_out)
    r.put(r.phi_own)
    r.acc[...] = jnp.zeros_like(r.acc)
    first_messages(
        r.acc,
        r.geo_own,
        r.osc_own,
        r.state,
        r.work,
        r.gs,
        r.gv,
        r.phi_own,
        r.filt_one,
        own_rows,
        chunks,
    )
    r.put(r.acc)
    sent = jnp.concatenate([r.send_rows[...]] * (own_rows // ghosts), 1)
    atom = lax.broadcasted_iota(jnp.int32, (own_rows, own_rows), 0)
    place = jnp.where(atom == sent, 1.0, 0.0).astype(f32).T[:ghosts].astype(bf16)
    r.cols_sent[...] = picked(place, r.cols[...])
    r.emb_sent[...] = picked(place, r.embedding[...])
    fill_mask(r.wbox, r.mask_ghost[...])
    r.wbox_sent[...] = mxu(place, r.wbox[...].astype(bf16))
    for i in range(8):
        r.acc_sent[i * ghosts : (i + 1) * ghosts, :] = picked(
            place, r.acc[i * own_rows : (i + 1) * own_rows, :]
        )


def node_states(acc, embedding, maps, node, inner, w_left, w_right, w_two_in, w_two_out):
    rows = embedding.shape[0]
    top = 2 * rows
    half = 3 * rows
    ah, al = split(acc[top:, :])
    maps[0 : 2 * half, :] = three(ah, al, *split(w_left[...]))
    maps[2 * half :, :] = three(ah, al, *split(w_right[...]))
    total = embedding[...] + acc[0:rows, :]
    moved = acc[rows:top, :]
    for i in range(3):
        a, b = i * rows, (i + 1) * rows
        left, left_dot = maps[a:b, :], maps[half + a : half + b, :]
        right = maps[2 * half + a : 2 * half + b, :]
        right_dot = maps[3 * half + a : 3 * half + b, :]
        total = total + left * right
        moved = moved + left_dot * right + left * right_dot
    node[0:rows, :] = total
    node[rows:, :] = moved
    inner[...] = dot3(node[...], w_two_in)
    value, slope, _ = silu_parts(inner[0:rows, :])
    outer = dot3(jnp.concatenate([value, slope * inner[rows:, :]], 0), w_two_out)
    return outer[:rows], outer[rows:]


def first_sent_kernel(sizes, chunks, r):
    channels = r.emb_sent.shape[1]
    r.table[...] = jnp.zeros_like(r.table)
    members = r.table.shape[0]
    count = members // 8
    gap = lanes // count
    for number, target in enumerate(offsets):
        device, inside = neighbour_id(target, sizes)

        @pl.when(inside)
        def _():
            chunk = r.arrived[device]
            ends = chunk[:, count * channels :]
            for p in range(count):
                at_row = slice(number * count + p, number * count + p + 1)
                r.table[at_row, :channels] = chunk[:, p * channels : (p + 1) * channels]
                r.table[at_row, channels:] = pltpu.roll(ends, lanes - p * gap, 1) if p else ends

    r.coords_ghost[...] = r.table[:, channels:]
    r.put(r.coords_ghost)
    r.phi_ghost[...] = dot3(
        silu_parts(dot3(r.table[:, :channels], r.in_near))[0], r.out_near
    )
    r.put(r.phi_ghost)
    geometry_by_atom(
        r.geo, r.osc, r.cols_sent[...], ghost_lanes(r.coords_ghost), r.wbox_sent
    )
    first_messages(
        r.acc_sent,
        r.geo,
        r.osc,
        r.state,
        r.work,
        r.gs,
        r.gv,
        r.phi_ghost,
        r.filt_near,
        members,
        chunks,
    )
    r.need(r.w_left, r.w_right, r.w_two_in, r.w_two_out)
    plain, dotted = node_states(
        r.acc_sent,
        r.emb_sent,
        r.maps,
        r.node,
        r.inner,
        r.w_left,
        r.w_right,
        r.w_two_in,
        r.w_two_out,
    )
    r.stage[:, :channels] = plain
    r.stage[:, channels:] = dotted
    send_groups(r, r.stage, sizes)


def ghost_lanes(coords):
    members = coords.shape[0]
    return jnp.concatenate([coords[...]] * (lanes // members), 0).T[:, :members]


def second_own_kernel(chunks, ghost_chunks, r):
    own_rows = r.mask_own.shape[0]
    ghosts = r.mask_ghost.shape[0]
    channels = r.embedding.shape[1]
    r.need(r.cols, r.mask_ghost, r.coords_ghost)
    fill_mask(r.wbox, r.mask_ghost[...])
    geometry_by_atom(
        r.geo_ghost, r.osc_ghost, r.cols[...], ghost_lanes(r.coords_ghost), r.wbox
    )
    r.put(r.geo_ghost, r.osc_ghost)
    r.need(r.phi_ghost, r.filt_one, r.acc)
    first_messages(
        r.acc,
        r.geo_ghost,
        r.osc_ghost,
        r.state,
        r.work_one,
        r.gs,
        r.gv,
        r.phi_ghost,
        r.filt_one,
        ghosts,
        ghost_chunks,
    )
    r.need(r.w_left, r.w_right, r.w_two_in, r.w_two_out, r.embedding)
    plain, dotted = node_states(
        r.acc,
        r.embedding,
        r.maps,
        r.node,
        r.inner,
        r.w_left,
        r.w_right,
        r.w_two_in,
        r.w_two_out,
    )
    r.phi_two[:, :channels] = plain
    r.phi_two[:, channels:] = dotted
    r.put(r.node, r.maps, r.inner, r.phi_two)
    r.acc_two[...] = jnp.zeros_like(r.acc_two)
    r.need(r.geo_own, r.osc_own, r.filt_two)
    r.filt_near[...] = r.filt_two[...]
    start_state(r.state, r.osc_own, own_rows, own_rows)

    def own_basis(step, slot):
        kept = at(r.work, slot)
        plain_basis(kept, r.geo_own, r.osc_own, r.state, own_rows, step, own_rows)
        return kept

    second_messages(r.acc_two, own_basis, r.gs, r.gv, r.filt_two, r.phi_two, chunks)
    r.need(r.box)
    geometry_by_slot(r.geo, r.osc, r.coords_ghost[...], r.box[...], r.mask_ghost[...])
    start_state(r.state, r.osc, ghosts, own_rows)

    def slot_rows(step, slot):
        kept = at(r.work, slot)
        plain_basis(kept, r.geo, r.osc, r.state, own_rows, step, ghosts)
        for i in range(wide // lanes):
            part = slice(i * lanes, (i + 1) * lanes)
            order = step * (wide // lanes) + i
            for half, place in zip(kept, (slice(0, lanes), slice(lanes, wide))):
                r.at_plain[order, :, place] = half[0:ghosts, part]
                r.at_dot[order, :, place] = half[ghosts : 2 * ghosts, part]

    steps(chunks, own_rows, slot_rows)
    start_state(r.state, r.osc_ghost, own_rows, ghosts)
    steps(
        ghost_chunks,
        ghosts,
        lambda step, slot: plain_basis(
            at(r.a_ghost, step), r.geo_ghost, r.osc_ghost, r.state, ghosts, step, own_rows
        ),
    )


def ghost_cotangents(back, plain, dotted, filt, cot):
    orders, height, _ = plain.shape
    own_rows = cot.shape[0] // 2
    channels = cot.shape[1]
    beside = jnp.concatenate([cot[0:own_rows, :], cot[own_rows:, :]], 1)
    high, low = split(beside)
    both = jnp.concatenate([high, high], 0)
    rest = jnp.concatenate([low, jnp.zeros_like(low)], 0)
    together = orders // 4
    value = jnp.zeros((height, channels), f32)
    moved = jnp.zeros((height, channels), f32)
    for start in range(0, orders, together):
        rows = plain[start : start + together].reshape(together * height, wide)
        first = mxu(rows, both) + mxu(rows, rest)
        rows = dotted[start : start + together].reshape(together * height, wide)
        second = first[:, channels:] + (
            mxu(rows, both[:, :channels]) + mxu(rows, rest[:, :channels])
        )
        for i in range(together):
            weight = filt[start + i : start + i + 1, :]
            value = value + weight * first[i * height : (i + 1) * height, :channels]
            moved = moved + weight * second[i * height : (i + 1) * height, :]
    back[:, :channels] = value
    back[:, channels:] = moved


def second_ghost_kernel(sizes, ghost_chunks, r):
    own_rows = r.node.shape[0] // 2
    r.table[...] = jnp.zeros_like(r.table)
    receive(r, r.table, sizes)
    r.put(r.table)

    second_messages(
        r.acc_two,
        lambda step, slot: at(r.a_ghost, step),
        r.plain,
        r.dotted,
        r.filt_near,
        r.table,
        ghost_chunks,
    )
    r.need(r.node, r.w_hidden, r.w_energy)
    hidden = dot3(r.node[...] + r.acc_two[...], r.w_hidden)
    _, slope, bend = silu_parts(hidden[:own_rows])
    live = lax.broadcasted_iota(jnp.int32, (own_rows, 1), 0) < r.counts[0]
    weight = jnp.where(live, r.w_energy[...], 0.0)
    bars = jnp.concatenate([weight * slope, weight * bend * hidden[own_rows:]], 0)
    r.cot[...] = dot3(bars, r.w_hidden, nt_dims)
    r.put(r.cot)
    ghost_cotangents(r.back_ghost, r.at_plain, r.at_dot, r.filt_near, r.cot)
    send_groups(r, r.back_ghost, sizes)


def second_back_kernel(chunks, ghost_chunks, r):
    own_rows = r.mask_own.shape[0]
    r.need(r.box, r.cols, r.mask_own)
    geometry_by_slot(r.geo, r.osc, r.cols[...], r.box[...], r.mask_own[...])
    r.need(r.cot, r.filt_two)

    start_state(r.state, r.osc, own_rows, own_rows)

    def slot_basis(step, slot):
        kept = at(r.work, slot)
        plain_basis(kept, r.geo, r.osc, r.state, own_rows, step, own_rows)
        return kept

    table_cotangents(r.back, slot_basis, r.plain, r.dotted, r.filt_two, r.cot, chunks)
    split_cot = at(r.work, 0)
    put_split(split_cot, 0, r.cot[...])
    r.need(r.geo_own, r.osc_own, r.phi_two)

    start_state(r.state, r.osc_own, own_rows, own_rows)

    second_pairs(
        r.pair,
        r.pair_own,
        split_cot,
        lambda step: full_basis(r.geo_own, r.osc_own, r.state, own_rows, step),
        r.plain,
        r.dotted,
        r.filt_two,
        r.phi_two,
        chunks,
    )
    r.put(r.pair_own)
    r.need(r.table, r.geo_ghost, r.osc_ghost)
    ghosts = r.table.shape[0]
    start_state(r.state, r.osc_ghost, own_rows, ghosts)


    second_pairs(
        r.pair,
        r.pair_ghost,
        split_cot,
        lambda step: full_basis(r.geo_ghost, r.osc_ghost, r.state, ghosts, step),
        r.plain,
        r.dotted,
        r.filt_two,
        r.table,
        ghost_chunks,
    )


def pairs_again(r, geo, osc, phi, chunks):
    members = phi.shape[0]
    channels = phi.shape[1] // 2
    start_state(r.state, osc, geo.shape[1], members)

    def basis_at(step):
        return full_basis(geo, osc, r.state, members, step)

    def factors_at(step, slot):
        scaled_rows(r.gs, slot, step, r.filt_one, slice(0, channels), phi[:, :channels])
        scaled_rows(r.gv, slot, step, r.filt_one, slice(channels, None), phi[:, channels:])
        return at(r.gs, slot), at(r.gv, slot)

    first_pairs(r.pair, r.cots, r.bars, geo, basis_at, factors_at, members, chunks)


def first_back_ghost_kernel(sizes, chunks, r):
    own_rows = r.back.shape[0]
    channels = r.back.shape[1] // 2
    r.table[...] = jnp.zeros_like(r.table)
    receive(r, r.table, sizes)
    add_returned(r.back, r.table, r.send_rows[...])
    outer = dot3(
        jnp.concatenate([r.back[:, :channels], r.back[:, channels:]], 0), r.w_two_out, nt_dims
    )
    _, slope, bend = silu_parts(r.inner[:own_rows, :])
    pulled = jnp.concatenate(
        [
            outer[:own_rows] * slope,
            outer[own_rows:] * slope + outer[:own_rows] * bend * r.inner[own_rows:, :],
        ],
        0,
    )
    bars = r.cot[...] + dot3(pulled, r.w_two_in, nt_dims)
    put_split(r.bars, 0, bars)
    half = 3 * own_rows
    maps = r.maps
    bar, bar_dot = bars[0:own_rows], bars[own_rows:]
    r.need(r.w_left, r.w_right)
    for i in range(3):
        a, b = i * own_rows, (i + 1) * own_rows
        left, left_dot = maps[a:b, :], maps[half + a : half + b, :]
        right = maps[2 * half + a : 2 * half + b, :]
        right_dot = maps[3 * half + a : 3 * half + b, :]
        for_left = jnp.concatenate([bar * right, bar_dot * right + bar * right_dot], 0)
        for_right = jnp.concatenate([bar * left, bar_dot * left + bar * left_dot], 0)
        both = dot3(for_left, r.w_left, nt_dims) + dot3(for_right, r.w_right, nt_dims)
        put_split(r.bars, (2 + i) * own_rows, both[:own_rows])
        put_split(r.bars, (5 + i) * own_rows, both[own_rows:])
    r.put(r.bars)
    r.need(r.geo_ghost, r.osc_ghost, r.phi_ghost, r.filt_one)
    pairs_again(r, r.geo_ghost, r.osc_ghost, r.phi_ghost, chunks)
    r.by_slot[...] = jnp.zeros_like(r.by_slot)
    members = r.table.shape[0]
    offset_gradients(r.geo_ghost, r.pair, r.pair_ghost, members, r.by_slot, r.by_atom)
    r.put(r.by_atom)
    send_chunks(r, lambda number: r.by_slot, sizes)


def first_back_own_kernel(chunks, r):
    own_rows = r.by_atom.shape[0]
    r.need(r.phi_own, r.filt_one, r.geo_own, r.osc_own, r.bars)
    pairs_again(r, r.geo_own, r.osc_own, r.phi_own, chunks)
    r.result[...] = jnp.zeros_like(r.result)
    r.need(r.pair_own, r.by_atom)
    offset_gradients(r.geo_own, r.pair, r.pair_own, own_rows, r.result, r.atoms)
    r.result[...] += (r.atoms[...] + r.by_atom[...]).T[0:8, :]
    r.need(r.send_rows)
    r.send_near[...] = r.send_rows[...]


def finish_kernel(sizes, r):
    count = r.send_near.shape[1] // 8
    own_rows = r.result.shape[1]
    r.table[...] = jnp.zeros_like(r.table)
    receive(r, r.table, sizes)
    lane = lax.broadcasted_iota(jnp.int32, (1, lanes), 1)
    atom = lax.broadcasted_iota(jnp.int32, (own_rows, 8 * count), 0)
    place = jnp.where(atom == r.send_near[...], 1.0, 0.0).astype(bf16)
    rows = jnp.zeros((8, lanes), f32)
    for number in range(8):
        shift = ((2 * number - 7) * count) % lanes
        moved = r.table[8 * number : 8 * number + 8, :]
        if shift:
            moved = pltpu.roll(moved, shift, 1)
        mine = (lane >= number * count) & (lane < (number + 1) * count)
        rows = jnp.where(mine, moved, rows)
    value = rows[:, : 8 * count]
    high, low = split(value)
    rest = (value - high.astype(f32) - low.astype(f32)).astype(bf16)
    total = r.result[...] + mxu(high, place, nt_dims) + mxu(low, place, nt_dims)
    total = total + mxu(rest, place, nt_dims)
    r.forces[...] = -total[0:3, :]
    r.product[...] = -total[3:6, :]
    r.put(r.forces, r.product)


class Refs:
    def need(self, *buffers):
        for buffer in buffers:
            for copy in self.loads.pop(id(buffer), ()):
                copy.wait()

    def put(self, *buffers):
        for buffer in buffers:
            for copy in self.stores[id(buffer)]:
                copy.start()
                self.started.append(copy)

    def close(self):
        for copy in [copy for group in self.loads.values() for copy in group] + self.started:
            copy.wait()


def as_tuple(value):
    return value if isinstance(value, tuple) else (value,)


def flat(entry):
    if isinstance(entry, list):
        return entry
    return [(entry[0], kind) for kind in as_tuple(entry[1])]


class Slot:
    def __init__(self, name, value):
        self.name, self.arrays, self.near = name, as_tuple(value), False


class Slots:
    def __setattr__(self, name, value):
        object.__setattr__(self, name, Slot(name, value))


def call(kernel, v, loads, outs, scratch, index=(), raw=(), scalars=(), sent=(), near=None, carry=()):
    near = near or dict()
    raw = raw + tuple(slot for slot in loads if slot.near)
    loads = tuple(slot for slot in loads if not slot.near)
    args, kinds, shapes, buffers = [], [], [], []
    copied = [(slot, pltpu.VMEM) for slot in loads] + [(slot, pltpu.SMEM) for slot in index]
    copies = 0
    for slot, space in copied:
        for array in slot.arrays:
            args.append(pltpu.with_memory_space_constraint(array, pltpu.HBM))
            kinds.append(pl.BlockSpec(memory_space=pltpu.HBM))
            buffers.append(space(array.shape, array.dtype))
            copies += 1
    for slot in raw + scalars:
        for array in slot.arrays:
            args.append(array)
            kinds.append(pl.BlockSpec(memory_space=pltpu.VMEM if slot in raw else pltpu.SMEM))
    for shape, types in outs.values():
        for kind in as_tuple(types):
            shapes.append(pltpu.HBM(shape, kind))
            buffers.append(pltpu.VMEM(shape, kind))
            copies += 1
    places = [pltpu.HBM] * len(shapes)
    for slot in carry:
        array = slot.arrays[0]
        args.append(pltpu.with_memory_space_constraint(array, pltpu.HBM))
        kinds.append(pl.BlockSpec(memory_space=pltpu.HBM))
        shapes.append(jax.ShapeDtypeStruct(array.shape, array.dtype))
        places.append(pltpu.VMEM)
        copies += 1
    for entry in near.values():
        for shape, kind in flat(entry):
            shapes.append(jax.ShapeDtypeStruct(shape, kind))
            places.append(pltpu.VMEM)
    if sent:
        shapes.append(pltpu.HBM(sent, f32))
        places.append(pltpu.HBM)
    for entry in scratch.values():
        for shape, kind in flat(entry):
            buffers.append(pltpu.VMEM(shape, kind))
    buffers.append(pltpu.SemaphoreType.DMA((copies + 1,)))
    buffers.append(pltpu.SemaphoreType.DMA((8,)))

    def run(*refs):
        r = Refs()
        r.loads, r.stores, r.started = {}, {}, []
        ins, refs = refs[: len(args)], refs[len(args) :]
        targets, refs = refs[: len(shapes)], list(refs[len(shapes) :])
        ins, targets = list(ins), list(targets)
        r.moves = refs[-1]
        sems = [refs[-2].at[number] for number in range(copies)]

        def taken(name, number):
            group = tuple(refs.pop(0) for _ in range(number))
            value = group if number > 1 else group[0]
            setattr(r, name, value)
            return group, id(value)

        for slot, _ in copied:
            group, key = taken(slot.name, len(slot.arrays))
            r.loads[key] = []
            for buffer in group:
                copy = pltpu.make_async_copy(ins.pop(0), buffer, sems.pop(0))
                copy.start()
                r.loads[key].append(copy)
        for slot in raw + scalars:
            group = tuple(ins.pop(0) for _ in slot.arrays)
            setattr(r, slot.name, group if len(group) > 1 else group[0])
        for name, (shape, types) in outs.items():
            group, key = taken(name, len(as_tuple(types)))
            r.stores[key] = []
            for buffer in group:
                copy = pltpu.make_async_copy(buffer, targets.pop(0), sems.pop(0))
                r.stores[key].append(copy)
        for slot in carry:
            buffer = targets.pop(0)
            setattr(r, slot.name, buffer)
            copy = pltpu.make_async_copy(ins.pop(0), buffer, sems.pop(0))
            copy.start()
            r.loads[id(buffer)] = [copy]
        for name, entry in near.items():
            group = tuple(targets.pop(0) for _ in flat(entry))
            setattr(r, name, group if len(group) > 1 else group[0])
        if sent:
            r.out = targets.pop(0)
        for name, entry in scratch.items():
            taken(name, len(flat(entry)))
        kernel(r)
        r.close()

    results = pl.pallas_call(
        run,
        out_shape=shapes,
        in_specs=kinds,
        out_specs=[pl.BlockSpec(memory_space=place) for place in places],
        scratch_shapes=buffers,
        compiler_params=pltpu.CompilerParams(vmem_limit_bytes=20 * 1024 * 1024),
        name=kernel.func.__name__,
    )(*args)
    results = list(results)
    for name, (shape, types) in outs.items():
        group = tuple(results.pop(0) for _ in as_tuple(types))
        setattr(v, name, group)
    carried = Slots()
    for slot in carry:
        setattr(carried, slot.name, results.pop(0))
        getattr(carried, slot.name).near = True
    for name, entry in near.items():
        setattr(v, name, tuple(results.pop(0) for _ in flat(entry)))
        getattr(v, name).near = True
    if sent:
        v.arrived = exchanged(results.pop(0))
    return carried


def exchanged(buffer):
    return lax.all_to_all(buffer, ("bx", "by"), 0, 0)


def per_device(
    positions,
    tangent,
    embedding,
    counts,
    neighbours,
    send_rows,
    w_one_in,
    w_one_out,
    filter_one,
    w_left,
    w_right,
    w_two_in,
    w_two_out,
    filter_two,
    w_hidden,
    w_energy,
):
    w_energy = w_energy.reshape(1, w_energy.shape[0])
    v = Slots()
    for name, value in tuple(locals().items()):
        if value is not v:
            setattr(v, name, value)
    sizes = (lax.axis_size("bx"), lax.axis_size("by"))
    devices = sizes[0] * sizes[1]
    n = positions.shape[1]
    channels = embedding.shape[1]
    ghosts = send_rows.shape[1]
    orders = filter_one.shape[0]
    count = ghosts // 8
    scale = 1.0 / math.sqrt(neighbours.shape[0])
    part = functools.partial
    pair = (bf16, bf16)
    own_chunks, ghost_chunks = orders * n // wide, orders * ghosts // wide

    def factors(chunks):
        return ((chunks, wide, channels), pair)

    geometry = ((geo_slots, n, lanes), f32)
    osc = ((osc_slots, n, lanes), f32)
    state = [((2, n, wide), f32), ((2, n, lanes), f32)]
    wbox = ((n, lanes), f32)
    pairs = ((8, n, wide), f32)
    cots = ((2, 8 * n, wide), f32)

    call(
        part(pack_kernel, sizes),
        v,
        (v.positions, v.tangent, v.embedding),
        dict(),
        dict(
            box=((n, n), f32),
            table=((n, channels + lanes), f32),
            stage=((8, 1, count * channels + lanes), f32),
        ),
        index=(v.send_rows,),
        sent=(devices, 1, count * channels + lanes),
    )
    call(
        part(first_own_kernel, scale, own_chunks),
        v,
        (v.positions, v.tangent, v.neighbours, v.w_one_in, v.w_one_out, v.embedding, v.filter_one, v.filter_two, v.send_rows),
        dict(
            box=((n, n), f32),
            cols=((n, n), f32),
            mask_own=((n, n), f32),
            mask_ghost=((ghosts, n), f32),
            filt_one=((orders, 2 * channels), f32),
            filt_two=((orders, channels), f32),
            geo_own=geometry,
            osc_own=osc,
            phi_own=((n, 2 * channels), f32),
            acc=((8 * n, channels), f32),
        ),
        dict(
            gs=factors(2),
            gv=factors(2),
            wbox=wbox,
            state=state,
            work=((2, 8 * n, wide), pair),
        ),
        near=dict(
            acc_sent=((8 * ghosts, channels), f32),
            cols_sent=((ghosts, n), f32),
            emb_sent=((ghosts, channels), f32),
            wbox_sent=((ghosts, lanes), f32),
            filt_near=((orders, 2 * channels), f32),
            in_near=((channels, channels), f32),
            out_near=((channels, 2 * channels), f32),
        ),
    )
    call(
        part(first_sent_kernel, sizes, ghost_chunks),
        v,
        (
            v.acc_sent,
            v.cols_sent,
            v.emb_sent,
            v.wbox_sent,
            v.filt_near,
            v.in_near,
            v.out_near,
            v.w_left,
            v.w_right,
            v.w_two_in,
            v.w_two_out,
        ),
        dict(
            phi_ghost=((ghosts, 2 * channels), f32),
            coords_ghost=((ghosts, lanes), f32),
        ),
        dict(
            geo=((geo_slots, ghosts, lanes), f32),
            osc=((osc_slots, ghosts, lanes), f32),
            gs=factors(2),
            gv=factors(2),
            state=[((2, ghosts, wide), f32), ((2, ghosts, lanes), f32)],
            work=((2, 8 * ghosts, wide), pair),
            node=((2 * ghosts, channels), f32),
            inner=((2 * ghosts, channels), f32),
            maps=((12 * ghosts, channels), f32),
            table=((ghosts, channels + lanes), f32),
            stage=((ghosts, 2 * channels), f32),
        ),
        raw=(v.arrived,),
        sent=(devices, count, 2 * channels),
    )
    call(
        part(second_own_kernel, own_chunks, ghost_chunks),
        v,
        (
            v.cols,
            v.mask_ghost,
            v.coords_ghost,
            v.phi_ghost,
            v.filt_one,
            v.acc,
            v.w_left,
            v.w_right,
            v.embedding,
            v.w_two_in,
            v.w_two_out,
            v.geo_own,
            v.osc_own,
            v.filt_two,
            v.box,
            v.mask_own,
        ),
        dict(
            geo_ghost=geometry,
            osc_ghost=osc,
            maps=((12 * n, channels), f32),
            node=((2 * n, channels), f32),
            inner=((2 * n, channels), f32),
            phi_two=((n, 2 * channels), f32),
        ),
        dict(
            geo=geometry,
            osc=osc,
            state=state,
            wbox=wbox,
            work_one=((2, 8 * n, wide), pair),
            work=((2, 2 * n, wide), pair),
            gs=factors(2),
            gv=factors(2),
        ),
        near=dict(
            acc_two=((2 * n, channels), f32),
            at_plain=((orders, ghosts, wide), bf16),
            at_dot=((orders, ghosts, wide), bf16),
            a_ghost=((ghost_chunks, 2 * n, wide), pair),
            filt_near=((orders, channels), f32),
        ),
    )
    call(
        part(second_ghost_kernel, sizes, ghost_chunks),
        v,
        (v.filt_near, v.acc_two, v.a_ghost, v.node, v.w_hidden, v.w_energy, v.at_plain, v.at_dot),
        dict(
            cot=((2 * n, channels), f32),
            table=((ghosts, 2 * channels), f32),
        ),
        dict(
            plain=factors(2),
            dotted=factors(2),
            back_ghost=((ghosts, 2 * channels), f32),
        ),
        raw=(v.arrived,),
        scalars=(v.counts,),
        sent=(devices, count, 2 * channels),
    )
    carried = call(
        part(second_back_kernel, own_chunks, ghost_chunks),
        v,
        (v.box, v.cols, v.mask_own, v.filt_two, v.geo_own, v.osc_own, v.phi_two, v.table, v.geo_ghost, v.osc_ghost),
        dict(
            pair_own=((2, n, lanes), f32),
        ),
        dict(
            geo=geometry,
            osc=osc,
            state=state,
            wbox=wbox,
            work=((2, 2 * n, wide), pair),
            plain=factors(2),
            dotted=factors(2),
            pair=((2, n, wide), f32),
        ),
        near=dict(
            back=((n, 2 * channels), f32),
            pair_ghost=((2, n, lanes), f32),
        ),
        carry=(v.cot, v.send_rows, v.w_two_out, v.inner, v.w_two_in, v.maps),
    )
    call(
        part(first_back_ghost_kernel, sizes, ghost_chunks),
        v,
        (carried.send_rows, v.back, carried.w_two_out, carried.inner, carried.w_two_in, carried.cot, carried.maps, v.w_left, v.w_right, v.phi_ghost, v.filt_one, v.osc_ghost, v.geo_ghost, v.pair_ghost),
        dict(
            bars=((8 * n, channels), pair),
            by_atom=((n, lanes), f32),
        ),
        dict(
            table=((ghosts, 2 * channels), f32),
            by_slot=((8, lanes), f32),
            pair=pairs,
            cots=cots,
            state=state,
            gs=factors(2),
            gv=factors(2),
        ),
        raw=(v.arrived,),
        sent=(devices, 8, lanes),
    )
    call(
        part(first_back_own_kernel, own_chunks),
        v,
        (v.bars, v.phi_own, v.filt_one, v.geo_own, v.osc_own, v.pair_own, v.by_atom, v.send_rows),
        dict(),
        dict(
            atoms=((n, lanes), f32),
            pair=pairs,
            cots=cots,
            state=state,
            gs=factors(2),
            gv=factors(2),
        ),
        near=dict(result=((8, lanes), f32), send_near=((1, ghosts), jnp.int32)),
    )
    call(
        part(finish_kernel, sizes),
        v,
        (v.send_near, v.result),
        dict(forces=((3, n), f32), product=((3, n), f32)),
        dict(table=((64, lanes), f32)),
        raw=(v.arrived,),
    )
    return v.forces.arrays[0], v.product.arrays[0]


def solution(mesh):
    brick = ("bx", "by")
    placed = (
        P(None, brick),
        P(None, brick),
        P(brick, None),
        P(brick),
        P(None, brick),
        P(brick, None),
    ) + (P(),) * 10

    return jax.shard_map(
        per_device,
        mesh=mesh,
        in_specs=placed,
        out_specs=(P(None, brick), P(None, brick)),
        check_vma=False,
    )
```

```python
import functools
import math

import jax
import jax.numpy as jnp
from jax import lax
from jax.experimental import pallas as pl
from jax.experimental.pallas import tpu as pltpu
from jax.sharding import PartitionSpec as P

f32 = jnp.float32
bf16 = jnp.bfloat16
cutoff_radius = 3.0
softening = 0.01
wave = math.pi / cutoff_radius
offsets = ((-1, -1), (-1, 0), (-1, 1), (0, -1), (0, 1), (1, -1), (1, 0), (1, 1))
lanes = 128
wide = 256
row_block = 32
nn_dims = (((1,), (0,)), ((), ()))
nt_dims = (((1,), (1,)), ((), ()))

U, UD, DD, RI = 0, 3, 6, 7
geo_slots = 8
P0, P1, P2, SN, CS = 0, 1, 2, 3, 4
osc_slots = 5
own_group = 2
ghost_group = 5


def split(value):
    high = value.astype(bf16)
    return high, (value - high.astype(f32)).astype(bf16)


def mxu(left, right, dims=nn_dims):
    return lax.dot_general(left, right, dims, preferred_element_type=f32)


def three(lh, ll, rh, rl, dims=nn_dims):
    return mxu(lh, rh, dims) + mxu(ll, rh, dims) + mxu(lh, rl, dims)


def dot3(left, right, dims=nn_dims):
    return three(*split(left), *split(right[...]), dims)


def sigmoid(value):
    return 1.0 / (1.0 + jnp.exp(-jnp.maximum(value, -80.0)))


def silu_parts(value):
    gate = sigmoid(value)
    first = gate * (1.0 + value * (1.0 - gate))
    second = gate * (1.0 - gate) * (2.0 + value * (1.0 - 2.0 * gate))
    return value * gate, first, second


def sin_cos(theta):
    t = jnp.minimum(theta, 6.0) * 0.25
    x = t * t
    s = -1.0 / 39916800.0 + x * (1.0 / 6227020800.0)
    s = 1.0 / 362880.0 + x * s
    s = -1.0 / 5040.0 + x * s
    s = 1.0 / 120.0 + x * s
    s = -1.0 / 6.0 + x * s
    s = t + t * x * s
    c = 1.0 / 479001600.0 - x * (1.0 / 87178291200.0)
    c = -1.0 / 3628800.0 + x * c
    c = 1.0 / 40320.0 + x * c
    c = -1.0 / 720.0 + x * c
    c = 1.0 / 24.0 + x * c
    c = -0.5 + x * c
    c = 1.0 + x * c
    s, c = 2.0 * s * c, 1.0 - 2.0 * s * s
    return 2.0 * s * c, 1.0 - 2.0 * s * s


def doubled(value):
    return jnp.concatenate([value, value], 1)


def fill_geometry(geo, osc, first, second, mask_at, height):
    for start in range(0, height, row_block):
        rows = pl.ds(start, row_block)
        off = [first(i, start) - second(i, start) for i in range(3)]
        move = [first(i + 3, start) - second(i + 3, start) for i in range(3)]
        square = off[0] * off[0] + off[1] * off[1] + off[2] * off[2] + softening
        inverse = lax.rsqrt(square)
        inverse = inverse * (1.5 - 0.5 * square * inverse * inverse)
        theta = wave * (square * inverse)
        unit = [o * inverse for o in off]
        speed = unit[0] * move[0] + unit[1] * move[1] + unit[2] * move[2]
        for i in range(3):
            geo[U + i, rows, :] = unit[i]
            geo[UD + i, rows, :] = (move[i] - unit[i] * speed) * inverse
        sn, cs = sin_cos(theta)
        g0 = (0.5 * cs + 0.5) * inverse
        g1 = ((-0.5 * wave) * sn - g0) * inverse
        g2 = ((-0.5 * wave * wave) * cs - 2.0 * g1) * inverse
        mask = mask_at(start)
        geo[DD, rows, :] = speed
        geo[RI, rows, :] = inverse
        osc[P0, rows, :] = mask * g0
        osc[P1, rows, :] = mask * g1
        osc[P2, rows, :] = mask * g2
        osc[SN, rows, :] = sn
        osc[CS, rows, :] = cs


def start_state(state, osc, height, members):
    waves, turn = state
    near = lanes // members
    group = lax.broadcasted_iota(jnp.int32, (1, lanes), 1) // members
    for start in range(0, height, row_block):
        rows = pl.ds(start, row_block)
        sn, cs = osc[SN, rows, :], osc[CS, rows, :]
        s, c = sn, cs
        for half in range(wide // lanes):
            place = pl.ds(half * lanes, lanes)
            if half:
                s, c = s * cs + c * sn, c * cs - s * sn
            state_s, state_c = s, c
            for i in range(1, near):
                s, c = s * cs + c * sn, c * cs - s * sn
                state_s = jnp.where(group >= i, s, state_s)
                state_c = jnp.where(group >= i, c, state_c)
            waves[0, rows, place] = state_s
            waves[1, rows, place] = state_c
        turn[0, rows, :] = s
        turn[1, rows, :] = c


def order_factor(step, members):
    repeats = wide // members
    group = lax.broadcasted_iota(jnp.int32, (1, wide), 1) // members
    return (group + (step * repeats + 1)).astype(f32) * wave


def rotate(state, rows, s, c):
    waves, turn = state
    rs = doubled(turn[0, rows, :])
    rc = doubled(turn[1, rows, :])
    waves[0, rows, :] = s * rc + c * rs
    waves[1, rows, :] = c * rc - s * rs


def steps(count, members, body, group=None):
    group = group or (own_group if members == lanes else ghost_group)
    if group >= count:
        for step in range(count):
            body(step, step % 2)
        return

    def several(index, carry):
        for place in range(group):
            body(index * group + place, place % 2)
        return carry

    lax.fori_loop(0, count // group, several, 0)


def listed(nbr_ref, start, members):
    slot = lax.broadcasted_iota(jnp.int32, (members, lanes), 0) + start
    found = nbr_ref[0:1, :] == slot
    for k in range(1, nbr_ref.shape[0]):
        found = found | (nbr_ref[k : k + 1, :] == slot)
    return jnp.where(found, 1.0, 0.0).astype(f32)


def fill_mask(wbox, mask):
    wbox[...] = jnp.concatenate([mask] * (lanes // mask.shape[0]), 0).T


def geometry_by_atom(geo, osc, columns, table, wbox):
    table = jnp.concatenate([table] * (lanes // table.shape[1]), 1)
    fill_geometry(
        geo,
        osc,
        lambda i, start: table[i : i + 1, :],
        lambda i, start: columns[start : start + row_block, i : i + 1],
        lambda start: wbox[start : start + row_block, :],
        geo.shape[1],
    )


def picked(place, value):
    high, low = split(value)
    rest = (value - high.astype(f32) - low.astype(f32)).astype(bf16)
    return mxu(place, high) + mxu(place, low) + mxu(place, rest)


def geometry_by_slot(geo, osc, columns, centre, mask):
    fill_geometry(
        geo,
        osc,
        lambda i, start: columns[start : start + row_block, i : i + 1],
        lambda i, start: centre[i : i + 1, :],
        lambda start: mask[start : start + row_block, :],
        mask.shape[0],
    )


def scaled_rows(pair, slot, step, filter_ref, columns, value):
    members = value.shape[0]
    for i in range(wide // members):
        row = filter_ref[pl.ds(step * (wide // members) + i, 1), columns]
        h, l = split(row * value)
        pair[0][slot, i * members : (i + 1) * members, :] = h
        pair[1][slot, i * members : (i + 1) * members, :] = l


def put_split(pair, start, value):
    h, l = split(value)
    pair[0][start : start + value.shape[0], :] = h
    pair[1][start : start + value.shape[0], :] = l


def at(pair, index):
    return pair[0].at[index], pair[1].at[index]


def basis_rows(kept, state, geo, osc, step, factor, start, height):
    rows = pl.ds(start, row_block)
    s, c = state[0][0, rows, :], state[0][1, rows, :]
    p0 = doubled(osc[P0, rows, :])
    b = p0 * s
    bd = (doubled(osc[P1, rows, :]) * s + factor * (p0 * c)) * doubled(geo[DD, rows, :])
    put_split(kept, start, b)
    put_split(kept, height + start, bd)
    rotate(state, rows, s, c)
    return b, bd


def first_messages(acc, geo, osc, state, work, scalars, vectors, phi, filt, members, chunks):
    height = geo.shape[1]
    channels = phi.shape[1] // 2
    top = 2 * height
    start_state(state, osc, height, members)

    def chunk(step, slot):
        factor = order_factor(step, members)
        scaled_rows(scalars, slot, step, filt, slice(0, channels), phi[:, :channels])
        scaled_rows(vectors, slot, step, filt, slice(channels, 2 * channels), phi[:, channels:])
        now = at(work, slot)
        for start in range(0, height, row_block):
            rows = pl.ds(start, row_block)
            b, bd = basis_rows(now, state, geo, osc, step, factor, start, height)
            for i in range(3):
                unit = doubled(geo[U + i, rows, :])
                put_split(now, (2 + i) * height + start, unit * b)
                put_split(
                    now, (5 + i) * height + start, doubled(geo[UD + i, rows, :]) * b + unit * bd
                )
        ah, al = now
        acc[:top, :] += three(ah[:top, :], al[:top, :], scalars[0][slot], scalars[1][slot])
        acc[top:, :] += three(ah[top:, :], al[top:, :], vectors[0][slot], vectors[1][slot])

    steps(chunks, members, chunk, 10)


def second_messages(acc, basis_at, plain, dotted, filt, value, chunks):
    height = acc.shape[0] // 2
    channels = acc.shape[1]

    def chunk(step, slot):
        scaled_rows(plain, slot, step, filt, slice(None), value[:, :channels])
        scaled_rows(dotted, slot, step, filt, slice(None), value[:, channels:])
        ah, al = basis_at(step, slot)
        acc[...] += three(ah[...], al[...], plain[0][slot], plain[1][slot])
        acc[height:, :] += three(
            ah[:height, :], al[:height, :], dotted[0][slot], dotted[1][slot]
        )

    steps(chunks, value.shape[0], chunk)


def plain_basis(kept, geo, osc, state, members, step, height):
    factor = order_factor(step, members)
    for start in range(0, height, row_block):
        basis_rows(kept, state, geo, osc, step, factor, start, height)


def full_basis(geo, osc, state, members, step):
    factor = order_factor(step, members)

    def at_rows(rows):
        s, c = state[0][0, rows, :], state[0][1, rows, :]
        p0, p1 = doubled(osc[P0, rows, :]), doubled(osc[P1, rows, :])
        b = p0 * s
        b1 = p1 * s + factor * (p0 * c)
        b2 = doubled(osc[P2, rows, :]) * s + factor * (2.0 * p1 * c - factor * b)
        rotate(state, rows, s, c)
        return b, b1, b2 * doubled(geo[DD, rows, :])

    return at_rows


def table_cotangents(back, basis_at, plain, dotted, filt, cot, chunks):
    channels = filt.shape[1]
    own_rows = cot.shape[0] // 2
    height = back.shape[0]
    back[...] = jnp.zeros_like(back)

    def chunk(step, slot):
        scaled_rows(plain, slot, step, filt, slice(None), cot[0:own_rows, :])
        scaled_rows(dotted, slot, step, filt, slice(None), cot[own_rows:, :])
        ah, al = basis_at(step, slot)
        both = three(ah[...], al[...], plain[0][slot], plain[1][slot])
        back[:, :channels] += both[:height]
        back[:, channels:] += both[height:] + three(
            ah[:height, :], al[:height, :], dotted[0][slot], dotted[1][slot]
        )

    steps(chunks, own_rows, chunk)


def halved(value):
    return value[:, :lanes] + value[:, lanes:]


def folded(total, members):
    if members < lanes:
        total = total + pltpu.roll(total, members, 1)
    return total


def second_pairs(pair, result, split_cot, basis_at, plain, dotted, filt, value, chunks):
    height = pair.shape[1]
    channels = filt.shape[1]
    pair[...] = jnp.zeros_like(pair)
    ah, al = split_cot

    def chunk(step, slot):
        scaled_rows(plain, slot, step, filt, slice(None), value[:, :channels])
        scaled_rows(dotted, slot, step, filt, slice(None), value[:, channels:])
        both = three(ah[...], al[...], plain[0][slot], plain[1][slot], nt_dims)
        dot = both[height:] + three(
            ah[:height, :], al[:height, :], dotted[0][slot], dotted[1][slot], nt_dims
        )
        basis = basis_at(step)
        for start in range(0, height, row_block):
            rows = pl.ds(start, row_block)
            _, b1, b2d = basis(rows)
            g = both[start : start + row_block]
            pair[0, rows, :] += halved(b1 * g)
            pair[1, rows, :] += halved(b2d * g + b1 * dot[start : start + row_block])

    members = value.shape[0]
    steps(chunks, members, chunk)
    result[0] = folded(pair[0], members)
    result[1] = folded(pair[1], members)


def first_pairs(pair, spaces, split_cot, geo, basis_at, factors_at, members, chunks):
    height = geo.shape[1]
    pair[...] = jnp.zeros_like(pair)
    ch, cl = split_cot
    top = 2 * height

    def chunk(step, slot):
        cots = spaces.at[slot]
        scalars, vectors = factors_at(step, slot)
        cots[:top, :] = three(
            ch[:top, :], cl[:top, :], scalars[0][...], scalars[1][...], nt_dims
        )
        cots[top:, :] = three(
            ch[top:, :], cl[top:, :], vectors[0][...], vectors[1][...], nt_dims
        )
        basis = basis_at(step)
        for start in range(0, height, row_block):
            rows = pl.ds(start, row_block)
            b, b1, b2d = basis(rows)
            b1d = b1 * doubled(geo[DD, rows, :])
            along = cots[start : start + row_block, :]
            along_dot = cots[height + start : height + start + row_block, :]
            for i in range(3):
                place = (2 + i) * height + start
                g = cots[place : place + row_block, :]
                place = (5 + i) * height + start
                gd = cots[place : place + row_block, :]
                unit = doubled(geo[U + i, rows, :])
                along = along + unit * g
                along_dot = along_dot + unit * gd + doubled(geo[UD + i, rows, :]) * g
                pair[2 + i, rows, :] += halved(b * g)
                pair[5 + i, rows, :] += halved(b * gd + b1d * g)
            pair[0, rows, :] += halved(b1 * along)
            pair[1, rows, :] += halved(b2d * along + b1 * along_dot)

    steps(chunks, members, chunk)


def neighbour_id(target, sizes):
    along = lax.axis_index("bx") + target[0]
    across = lax.axis_index("by") + target[1]
    inside = (along >= 0) & (along < sizes[0]) & (across >= 0) & (across < sizes[1])
    device = jnp.clip(along, 0, sizes[0] - 1) * sizes[1] + jnp.clip(across, 0, sizes[1] - 1)
    return device, inside


def send_chunks(r, chunk_at, sizes):
    for number, target in enumerate(offsets):
        device, inside = neighbour_id(target, sizes)
        copy = pltpu.make_async_copy(chunk_at(number), r.out.at[device], r.moves.at[number])

        @pl.when(inside)
        def _():
            copy.start()

    for number, target in enumerate(offsets):
        device, inside = neighbour_id(target, sizes)
        copy = pltpu.make_async_copy(chunk_at(number), r.out.at[device], r.moves.at[number])

        @pl.when(inside)
        def _():
            copy.wait()


def send_groups(r, table, sizes):
    count = r.out.shape[1]
    send_chunks(r, lambda number: table.at[number * count : (number + 1) * count, :], sizes)


def send_gathered(r, table, stage, send_ref, sizes):
    for slot in range(stage.shape[0]):
        stage[slot : slot + 1, :] = table[pl.ds(send_ref[0, slot], 1), :]
    send_groups(r, stage, sizes)


def receive(r, table, sizes):
    count = r.arrived.shape[1]
    for number, target in enumerate(offsets):
        device, inside = neighbour_id(target, sizes)

        @pl.when(inside)
        def _():
            table[number * count : (number + 1) * count, :] = r.arrived[device]


def add_returned(total, table, send_row):
    atom = lax.broadcasted_iota(jnp.int32, (total.shape[0], table.shape[0]), 0)
    place = jnp.where(atom == send_row, 1.0, 0.0).astype(bf16)
    high, low = split(table[...])
    rest = (table[...] - high.astype(f32) - low.astype(f32)).astype(bf16)
    total[...] += mxu(place, high) + mxu(place, low) + mxu(place, rest)


def offset_gradients(geo, pair, second, members, by_slot, by_atom):
    near = [folded(pair[i], members) for i in range(8)]
    height = geo.shape[1]
    units = [geo[U + i, :, :lanes] for i in range(3)]
    moves = [geo[UD + i, :, :lanes] for i in range(3)]
    inverse = geo[RI, :, :lanes]
    speed = geo[DD, :, :lanes]
    along = near[0] + second[0]
    along_dot = near[1] + second[1]
    turn, turn_dot = near[2:5], near[5:8]
    inner = units[0] * turn[0] + units[1] * turn[1] + units[2] * turn[2]
    inner_dot = sum(units[i] * turn_dot[i] + moves[i] * turn[i] for i in range(3))
    rate = speed * inverse
    lane = lax.broadcasted_iota(jnp.int32, (1, lanes), 1)
    sums = jnp.zeros((height, lanes), f32)
    for i in range(3):
        part = (turn[i] - units[i] * inner) * inverse
        grad = along * units[i] + part
        grad_dot = (
            along_dot * units[i]
            + along * moves[i]
            + (turn_dot[i] - moves[i] * inner - units[i] * inner_dot) * inverse
            - rate * part
        )
        for row, value in ((i, grad), (3 + i, grad_dot)):
            by_slot[row : row + 1, :] = jnp.sum(value, 0, keepdims=True)
            if members < lanes:
                value = jnp.where(lane < members, value, 0.0)
            sums = jnp.where(lane == row, -jnp.sum(value, 1, keepdims=True), sums)
    by_atom[...] = sums


def pack_kernel(sizes, r):
    channels = r.embedding.shape[1]
    r.box[...] = jnp.zeros_like(r.box)
    r.need(r.positions, r.tangent)
    r.box[0:3, :] = r.positions[...]
    r.box[3:6, :] = r.tangent[...]
    r.table[:, channels:] = r.box[...].T
    r.need(r.embedding)
    r.table[:, :channels] = r.embedding[...]
    r.need(r.send_rows)
    count = r.send_rows.shape[1] // 8
    gap = lanes // count
    for number in range(8):
        ends = jnp.zeros((1, lanes), f32)
        for p in range(count):
            row = r.table[pl.ds(r.send_rows[0, number * count + p], 1), :]
            r.stage[number, :, p * channels : (p + 1) * channels] = row[:, :channels]
            end = row[:, channels:]
            ends = ends + (pltpu.roll(end, p * gap, 1) if p else end)
        r.stage[number, :, count * channels :] = ends
    send_chunks(r, lambda number: r.stage.at[number], sizes)


def first_own_kernel(scale, chunks, r):
    own_rows = r.positions.shape[1]
    ghosts = r.mask_ghost.shape[0]
    r.box[...] = jnp.zeros_like(r.box)
    r.need(r.positions, r.tangent, r.neighbours)
    r.box[0:3, :] = r.positions[...]
    r.box[3:6, :] = r.tangent[...]
    r.cols[...] = r.box[...].T
    r.mask_own[...] = listed(r.neighbours, 0, own_rows)
    r.mask_ghost[...] = listed(r.neighbours, own_rows, ghosts)
    r.put(r.box, r.cols, r.mask_own, r.mask_ghost)
    fill_mask(r.wbox, r.mask_own[...])
    geometry_by_atom(r.geo_own, r.osc_own, r.cols[...], r.box[...], r.wbox)
    r.put(r.geo_own, r.osc_own)
    r.need(r.w_one_in, r.w_one_out, r.embedding, r.filter_one, r.filter_two, r.send_rows)
    r.filt_one[...] = r.filter_one[...] * scale
    r.filt_two[...] = r.filter_two[...] * scale
    r.put(r.filt_one, r.filt_two)
    r.filt_near[...] = r.filt_one[...]
    r.in_near[...] = r.w_one_in[...]
    r.out_near[...] = r.w_one_out[...]
    r.phi_own[...] = dot3(silu_parts(dot3(r.embedding[...], r.w_one_in))[0], r.w_one_out)
    r.put(r.phi_own)
    r.acc[...] = jnp.zeros_like(r.acc)
    first_messages(
        r.acc,
        r.geo_own,
        r.osc_own,
        r.state,
        r.work,
        r.gs,
        r.gv,
        r.phi_own,
        r.filt_one,
        own_rows,
        chunks,
    )
    r.put(r.acc)
    sent = jnp.concatenate([r.send_rows[...]] * (own_rows // ghosts), 1)
    atom = lax.broadcasted_iota(jnp.int32, (own_rows, own_rows), 0)
    place = jnp.where(atom == sent, 1.0, 0.0).astype(f32).T[:ghosts].astype(bf16)
    r.cols_sent[...] = picked(place, r.cols[...])
    r.emb_sent[...] = picked(place, r.embedding[...])
    fill_mask(r.wbox, r.mask_ghost[...])
    r.wbox_sent[...] = mxu(place, r.wbox[...].astype(bf16))
    for i in range(8):
        r.acc_sent[i * ghosts : (i + 1) * ghosts, :] = picked(
            place, r.acc[i * own_rows : (i + 1) * own_rows, :]
        )


def node_states(acc, embedding, maps, node, inner, w_left, w_right, w_two_in, w_two_out):
    rows = embedding.shape[0]
    top = 2 * rows
    half = 3 * rows
    ah, al = split(acc[top:, :])
    maps[0 : 2 * half, :] = three(ah, al, *split(w_left[...]))
    maps[2 * half :, :] = three(ah, al, *split(w_right[...]))
    total = embedding[...] + acc[0:rows, :]
    moved = acc[rows:top, :]
    for i in range(3):
        a, b = i * rows, (i + 1) * rows
        left, left_dot = maps[a:b, :], maps[half + a : half + b, :]
        right = maps[2 * half + a : 2 * half + b, :]
        right_dot = maps[3 * half + a : 3 * half + b, :]
        total = total + left * right
        moved = moved + left_dot * right + left * right_dot
    node[0:rows, :] = total
    node[rows:, :] = moved
    inner[...] = dot3(node[...], w_two_in)
    value, slope, _ = silu_parts(inner[0:rows, :])
    outer = dot3(jnp.concatenate([value, slope * inner[rows:, :]], 0), w_two_out)
    return outer[:rows], outer[rows:]


def first_sent_kernel(sizes, chunks, r):
    channels = r.emb_sent.shape[1]
    r.table[...] = jnp.zeros_like(r.table)
    members = r.table.shape[0]
    count = members // 8
    gap = lanes // count
    for number, target in enumerate(offsets):
        device, inside = neighbour_id(target, sizes)

        @pl.when(inside)
        def _():
            chunk = r.arrived[device]
            ends = chunk[:, count * channels :]
            for p in range(count):
                at_row = slice(number * count + p, number * count + p + 1)
                r.table[at_row, :channels] = chunk[:, p * channels : (p + 1) * channels]
                r.table[at_row, channels:] = pltpu.roll(ends, lanes - p * gap, 1) if p else ends

    r.coords_ghost[...] = r.table[:, channels:]
    r.put(r.coords_ghost)
    r.phi_ghost[...] = dot3(
        silu_parts(dot3(r.table[:, :channels], r.in_near))[0], r.out_near
    )
    r.put(r.phi_ghost)
    geometry_by_atom(
        r.geo, r.osc, r.cols_sent[...], ghost_lanes(r.coords_ghost), r.wbox_sent
    )
    first_messages(
        r.acc_sent,
        r.geo,
        r.osc,
        r.state,
        r.work,
        r.gs,
        r.gv,
        r.phi_ghost,
        r.filt_near,
        members,
        chunks,
    )
    r.need(r.w_left, r.w_right, r.w_two_in, r.w_two_out)
    plain, dotted = node_states(
        r.acc_sent,
        r.emb_sent,
        r.maps,
        r.node,
        r.inner,
        r.w_left,
        r.w_right,
        r.w_two_in,
        r.w_two_out,
    )
    r.stage[:, :channels] = plain
    r.stage[:, channels:] = dotted
    send_groups(r, r.stage, sizes)


def ghost_lanes(coords):
    members = coords.shape[0]
    return jnp.concatenate([coords[...]] * (lanes // members), 0).T[:, :members]


def second_own_kernel(chunks, ghost_chunks, r):
    own_rows = r.mask_own.shape[0]
    ghosts = r.mask_ghost.shape[0]
    channels = r.embedding.shape[1]
    r.need(r.cols, r.mask_ghost, r.coords_ghost)
    fill_mask(r.wbox, r.mask_ghost[...])
    geometry_by_atom(
        r.geo_ghost, r.osc_ghost, r.cols[...], ghost_lanes(r.coords_ghost), r.wbox
    )
    r.put(r.geo_ghost, r.osc_ghost)
    r.need(r.phi_ghost, r.filt_one, r.acc)
    first_messages(
        r.acc,
        r.geo_ghost,
        r.osc_ghost,
        r.state,
        r.work_one,
        r.gs,
        r.gv,
        r.phi_ghost,
        r.filt_one,
        ghosts,
        ghost_chunks,
    )
    r.need(r.w_left, r.w_right, r.w_two_in, r.w_two_out, r.embedding)
    plain, dotted = node_states(
        r.acc,
        r.embedding,
        r.maps,
        r.node,
        r.inner,
        r.w_left,
        r.w_right,
        r.w_two_in,
        r.w_two_out,
    )
    r.phi_two[:, :channels] = plain
    r.phi_two[:, channels:] = dotted
    r.put(r.node, r.maps, r.inner, r.phi_two)
    r.acc_two[...] = jnp.zeros_like(r.acc_two)
    r.need(r.geo_own, r.osc_own, r.filt_two)
    r.filt_near[...] = r.filt_two[...]
    start_state(r.state, r.osc_own, own_rows, own_rows)

    def own_basis(step, slot):
        kept = at(r.work, slot)
        plain_basis(kept, r.geo_own, r.osc_own, r.state, own_rows, step, own_rows)
        return kept

    second_messages(r.acc_two, own_basis, r.gs, r.gv, r.filt_two, r.phi_two, chunks)
    r.need(r.box)
    geometry_by_slot(r.geo, r.osc, r.coords_ghost[...], r.box[...], r.mask_ghost[...])
    start_state(r.state, r.osc, ghosts, own_rows)

    def slot_rows(step, slot):
        kept = at(r.work, slot)
        plain_basis(kept, r.geo, r.osc, r.state, own_rows, step, ghosts)
        for i in range(wide // lanes):
            part = slice(i * lanes, (i + 1) * lanes)
            order = step * (wide // lanes) + i
            for half, place in zip(kept, (slice(0, lanes), slice(lanes, wide))):
                r.at_plain[order, :, place] = half[0:ghosts, part]
                r.at_dot[order, :, place] = half[ghosts : 2 * ghosts, part]

    steps(chunks, own_rows, slot_rows)
    start_state(r.state, r.osc_ghost, own_rows, ghosts)
    steps(
        ghost_chunks,
        ghosts,
        lambda step, slot: plain_basis(
            at(r.a_ghost, step), r.geo_ghost, r.osc_ghost, r.state, ghosts, step, own_rows
        ),
    )


def ghost_cotangents(back, plain, dotted, filt, cot):
    orders, height, _ = plain.shape
    own_rows = cot.shape[0] // 2
    channels = cot.shape[1]
    beside = jnp.concatenate([cot[0:own_rows, :], cot[own_rows:, :]], 1)
    high, low = split(beside)
    both = jnp.concatenate([high, high], 0)
    rest = jnp.concatenate([low, jnp.zeros_like(low)], 0)
    together = orders // 4
    value = jnp.zeros((height, channels), f32)
    moved = jnp.zeros((height, channels), f32)
    for start in range(0, orders, together):
        rows = plain[start : start + together].reshape(together * height, wide)
        first = mxu(rows, both) + mxu(rows, rest)
        rows = dotted[start : start + together].reshape(together * height, wide)
        second = first[:, channels:] + (
            mxu(rows, both[:, :channels]) + mxu(rows, rest[:, :channels])
        )
        for i in range(together):
            weight = filt[start + i : start + i + 1, :]
            value = value + weight * first[i * height : (i + 1) * height, :channels]
            moved = moved + weight * second[i * height : (i + 1) * height, :]
    back[:, :channels] = value
    back[:, channels:] = moved


def second_ghost_kernel(sizes, ghost_chunks, r):
    own_rows = r.node.shape[0] // 2
    r.table[...] = jnp.zeros_like(r.table)
    receive(r, r.table, sizes)
    r.put(r.table)

    second_messages(
        r.acc_two,
        lambda step, slot: at(r.a_ghost, step),
        r.plain,
        r.dotted,
        r.filt_near,
        r.table,
        ghost_chunks,
    )
    r.need(r.node, r.w_hidden, r.w_energy)
    hidden = dot3(r.node[...] + r.acc_two[...], r.w_hidden)
    _, slope, bend = silu_parts(hidden[:own_rows])
    live = lax.broadcasted_iota(jnp.int32, (own_rows, 1), 0) < r.counts[0]
    weight = jnp.where(live, r.w_energy[...], 0.0)
    bars = jnp.concatenate([weight * slope, weight * bend * hidden[own_rows:]], 0)
    r.cot[...] = dot3(bars, r.w_hidden, nt_dims)
    r.put(r.cot)
    ghost_cotangents(r.back_ghost, r.at_plain, r.at_dot, r.filt_near, r.cot)
    send_groups(r, r.back_ghost, sizes)


def second_back_kernel(chunks, ghost_chunks, r):
    own_rows = r.mask_own.shape[0]
    r.need(r.box, r.cols, r.mask_own)
    geometry_by_slot(r.geo, r.osc, r.cols[...], r.box[...], r.mask_own[...])
    r.need(r.cot, r.filt_two)

    start_state(r.state, r.osc, own_rows, own_rows)

    def slot_basis(step, slot):
        kept = at(r.work, slot)
        plain_basis(kept, r.geo, r.osc, r.state, own_rows, step, own_rows)
        return kept

    table_cotangents(r.back, slot_basis, r.plain, r.dotted, r.filt_two, r.cot, chunks)
    split_cot = at(r.work, 0)
    put_split(split_cot, 0, r.cot[...])
    r.need(r.geo_own, r.osc_own, r.phi_two)

    start_state(r.state, r.osc_own, own_rows, own_rows)

    second_pairs(
        r.pair,
        r.pair_own,
        split_cot,
        lambda step: full_basis(r.geo_own, r.osc_own, r.state, own_rows, step),
        r.plain,
        r.dotted,
        r.filt_two,
        r.phi_two,
        chunks,
    )
    r.put(r.pair_own)
    r.need(r.table, r.geo_ghost, r.osc_ghost)
    ghosts = r.table.shape[0]
    start_state(r.state, r.osc_ghost, own_rows, ghosts)


    second_pairs(
        r.pair,
        r.pair_ghost,
        split_cot,
        lambda step: full_basis(r.geo_ghost, r.osc_ghost, r.state, ghosts, step),
        r.plain,
        r.dotted,
        r.filt_two,
        r.table,
        ghost_chunks,
    )


def pairs_again(r, geo, osc, phi, chunks):
    members = phi.shape[0]
    channels = phi.shape[1] // 2
    start_state(r.state, osc, geo.shape[1], members)

    def basis_at(step):
        return full_basis(geo, osc, r.state, members, step)

    def factors_at(step, slot):
        scaled_rows(r.gs, slot, step, r.filt_one, slice(0, channels), phi[:, :channels])
        scaled_rows(r.gv, slot, step, r.filt_one, slice(channels, None), phi[:, channels:])
        return at(r.gs, slot), at(r.gv, slot)

    first_pairs(r.pair, r.cots, r.bars, geo, basis_at, factors_at, members, chunks)


def first_back_ghost_kernel(sizes, chunks, r):
    own_rows = r.back.shape[0]
    channels = r.back.shape[1] // 2
    r.table[...] = jnp.zeros_like(r.table)
    receive(r, r.table, sizes)
    add_returned(r.back, r.table, r.send_rows[...])
    outer = dot3(
        jnp.concatenate([r.back[:, :channels], r.back[:, channels:]], 0), r.w_two_out, nt_dims
    )
    _, slope, bend = silu_parts(r.inner[:own_rows, :])
    pulled = jnp.concatenate(
        [
            outer[:own_rows] * slope,
            outer[own_rows:] * slope + outer[:own_rows] * bend * r.inner[own_rows:, :],
        ],
        0,
    )
    bars = r.cot[...] + dot3(pulled, r.w_two_in, nt_dims)
    put_split(r.bars, 0, bars)
    half = 3 * own_rows
    maps = r.maps
    bar, bar_dot = bars[0:own_rows], bars[own_rows:]
    r.need(r.w_left, r.w_right)
    for i in range(3):
        a, b = i * own_rows, (i + 1) * own_rows
        left, left_dot = maps[a:b, :], maps[half + a : half + b, :]
        right = maps[2 * half + a : 2 * half + b, :]
        right_dot = maps[3 * half + a : 3 * half + b, :]
        for_left = jnp.concatenate([bar * right, bar_dot * right + bar * right_dot], 0)
        for_right = jnp.concatenate([bar * left, bar_dot * left + bar * left_dot], 0)
        both = dot3(for_left, r.w_left, nt_dims) + dot3(for_right, r.w_right, nt_dims)
        put_split(r.bars, (2 + i) * own_rows, both[:own_rows])
        put_split(r.bars, (5 + i) * own_rows, both[own_rows:])
    r.put(r.bars)
    r.need(r.geo_ghost, r.osc_ghost, r.phi_ghost, r.filt_one)
    pairs_again(r, r.geo_ghost, r.osc_ghost, r.phi_ghost, chunks)
    r.by_slot[...] = jnp.zeros_like(r.by_slot)
    members = r.table.shape[0]
    offset_gradients(r.geo_ghost, r.pair, r.pair_ghost, members, r.by_slot, r.by_atom)
    r.put(r.by_atom)
    send_chunks(r, lambda number: r.by_slot, sizes)


def first_back_own_kernel(chunks, r):
    own_rows = r.by_atom.shape[0]
    r.need(r.phi_own, r.filt_one, r.geo_own, r.osc_own, r.bars)
    pairs_again(r, r.geo_own, r.osc_own, r.phi_own, chunks)
    r.result[...] = jnp.zeros_like(r.result)
    r.need(r.pair_own, r.by_atom)
    offset_gradients(r.geo_own, r.pair, r.pair_own, own_rows, r.result, r.atoms)
    r.result[...] += (r.atoms[...] + r.by_atom[...]).T[0:8, :]
    r.need(r.send_rows)
    r.send_near[...] = r.send_rows[...]


def finish_kernel(sizes, r):
    count = r.send_near.shape[1] // 8
    own_rows = r.result.shape[1]
    r.table[...] = jnp.zeros_like(r.table)
    receive(r, r.table, sizes)
    lane = lax.broadcasted_iota(jnp.int32, (1, lanes), 1)
    atom = lax.broadcasted_iota(jnp.int32, (own_rows, 8 * count), 0)
    place = jnp.where(atom == r.send_near[...], 1.0, 0.0).astype(bf16)
    rows = jnp.zeros((8, lanes), f32)
    for number in range(8):
        shift = ((2 * number - 7) * count) % lanes
        moved = r.table[8 * number : 8 * number + 8, :]
        if shift:
            moved = pltpu.roll(moved, shift, 1)
        mine = (lane >= number * count) & (lane < (number + 1) * count)
        rows = jnp.where(mine, moved, rows)
    value = rows[:, : 8 * count]
    high, low = split(value)
    rest = (value - high.astype(f32) - low.astype(f32)).astype(bf16)
    total = r.result[...] + mxu(high, place, nt_dims) + mxu(low, place, nt_dims)
    total = total + mxu(rest, place, nt_dims)
    r.forces[...] = -total[0:3, :]
    r.product[...] = -total[3:6, :]
    r.put(r.forces, r.product)


class Refs:
    def need(self, *buffers):
        for buffer in buffers:
            for copy in self.loads.pop(id(buffer), ()):
                copy.wait()

    def put(self, *buffers):
        for buffer in buffers:
            for copy in self.stores[id(buffer)]:
                copy.start()
                self.started.append(copy)

    def close(self):
        for copy in [copy for group in self.loads.values() for copy in group] + self.started:
            copy.wait()


def as_tuple(value):
    return value if isinstance(value, tuple) else (value,)


def flat(entry):
    if isinstance(entry, list):
        return entry
    return [(entry[0], kind) for kind in as_tuple(entry[1])]


class Slot:
    def __init__(self, name, value):
        self.name, self.arrays, self.near = name, as_tuple(value), False


class Slots:
    def __setattr__(self, name, value):
        object.__setattr__(self, name, Slot(name, value))


def call(kernel, v, loads, outs, scratch, index=(), raw=(), scalars=(), sent=(), near=None, carry=()):
    near = near or dict()
    raw = raw + tuple(slot for slot in loads if slot.near)
    loads = tuple(slot for slot in loads if not slot.near)
    args, kinds, shapes, buffers = [], [], [], []
    copied = [(slot, pltpu.VMEM) for slot in loads] + [(slot, pltpu.SMEM) for slot in index]
    copies = 0
    for slot, space in copied:
        for array in slot.arrays:
            args.append(pltpu.with_memory_space_constraint(array, pltpu.HBM))
            kinds.append(pl.BlockSpec(memory_space=pltpu.HBM))
            buffers.append(space(array.shape, array.dtype))
            copies += 1
    for slot in raw + scalars:
        for array in slot.arrays:
            args.append(array)
            kinds.append(pl.BlockSpec(memory_space=pltpu.VMEM if slot in raw else pltpu.SMEM))
    for shape, types in outs.values():
        for kind in as_tuple(types):
            shapes.append(pltpu.HBM(shape, kind))
            buffers.append(pltpu.VMEM(shape, kind))
            copies += 1
    places = [pltpu.HBM] * len(shapes)
    for slot in carry:
        array = slot.arrays[0]
        args.append(pltpu.with_memory_space_constraint(array, pltpu.HBM))
        kinds.append(pl.BlockSpec(memory_space=pltpu.HBM))
        shapes.append(jax.ShapeDtypeStruct(array.shape, array.dtype))
        places.append(pltpu.VMEM)
        copies += 1
    for entry in near.values():
        for shape, kind in flat(entry):
            shapes.append(jax.ShapeDtypeStruct(shape, kind))
            places.append(pltpu.VMEM)
    if sent:
        shapes.append(pltpu.HBM(sent, f32))
        places.append(pltpu.HBM)
    for entry in scratch.values():
        for shape, kind in flat(entry):
            buffers.append(pltpu.VMEM(shape, kind))
    buffers.append(pltpu.SemaphoreType.DMA((copies + 1,)))
    buffers.append(pltpu.SemaphoreType.DMA((8,)))

    def run(*refs):
        r = Refs()
        r.loads, r.stores, r.started = {}, {}, []
        ins, refs = refs[: len(args)], refs[len(args) :]
        targets, refs = refs[: len(shapes)], list(refs[len(shapes) :])
        ins, targets = list(ins), list(targets)
        r.moves = refs[-1]
        sems = [refs[-2].at[number] for number in range(copies)]

        def taken(name, number):
            group = tuple(refs.pop(0) for _ in range(number))
            value = group if number > 1 else group[0]
            setattr(r, name, value)
            return group, id(value)

        for slot, _ in copied:
            group, key = taken(slot.name, len(slot.arrays))
            r.loads[key] = []
            for buffer in group:
                copy = pltpu.make_async_copy(ins.pop(0), buffer, sems.pop(0))
                copy.start()
                r.loads[key].append(copy)
        for slot in raw + scalars:
            group = tuple(ins.pop(0) for _ in slot.arrays)
            setattr(r, slot.name, group if len(group) > 1 else group[0])
        for name, (shape, types) in outs.items():
            group, key = taken(name, len(as_tuple(types)))
            r.stores[key] = []
            for buffer in group:
                copy = pltpu.make_async_copy(buffer, targets.pop(0), sems.pop(0))
                r.stores[key].append(copy)
        for slot in carry:
            buffer = targets.pop(0)
            setattr(r, slot.name, buffer)
            copy = pltpu.make_async_copy(ins.pop(0), buffer, sems.pop(0))
            copy.start()
            r.loads[id(buffer)] = [copy]
        for name, entry in near.items():
            group = tuple(targets.pop(0) for _ in flat(entry))
            setattr(r, name, group if len(group) > 1 else group[0])
        if sent:
            r.out = targets.pop(0)
        for name, entry in scratch.items():
            taken(name, len(flat(entry)))
        kernel(r)
        r.close()

    results = pl.pallas_call(
        run,
        out_shape=shapes,
        in_specs=kinds,
        out_specs=[pl.BlockSpec(memory_space=place) for place in places],
        scratch_shapes=buffers,
        compiler_params=pltpu.CompilerParams(vmem_limit_bytes=20 * 1024 * 1024),
        name=kernel.func.__name__,
    )(*args)
    results = list(results)
    for name, (shape, types) in outs.items():
        group = tuple(results.pop(0) for _ in as_tuple(types))
        setattr(v, name, group)
    carried = Slots()
    for slot in carry:
        setattr(carried, slot.name, results.pop(0))
        getattr(carried, slot.name).near = True
    for name, entry in near.items():
        setattr(v, name, tuple(results.pop(0) for _ in flat(entry)))
        getattr(v, name).near = True
    if sent:
        v.arrived = exchanged(results.pop(0))
    return carried


def exchanged(buffer):
    return lax.all_to_all(buffer, ("bx", "by"), 0, 0)


def per_device(
    positions,
    tangent,
    embedding,
    counts,
    neighbours,
    send_rows,
    w_one_in,
    w_one_out,
    filter_one,
    w_left,
    w_right,
    w_two_in,
    w_two_out,
    filter_two,
    w_hidden,
    w_energy,
):
    w_energy = w_energy.reshape(1, w_energy.shape[0])
    v = Slots()
    for name, value in tuple(locals().items()):
        if value is not v:
            setattr(v, name, value)
    sizes = (lax.axis_size("bx"), lax.axis_size("by"))
    devices = sizes[0] * sizes[1]
    n = positions.shape[1]
    channels = embedding.shape[1]
    ghosts = send_rows.shape[1]
    orders = filter_one.shape[0]
    count = ghosts // 8
    scale = 1.0 / math.sqrt(neighbours.shape[0])
    part = functools.partial
    pair = (bf16, bf16)
    own_chunks, ghost_chunks = orders * n // wide, orders * ghosts // wide

    def factors(chunks):
        return ((chunks, wide, channels), pair)

    geometry = ((geo_slots, n, lanes), f32)
    osc = ((osc_slots, n, lanes), f32)
    state = [((2, n, wide), f32), ((2, n, lanes), f32)]
    wbox = ((n, lanes), f32)
    pairs = ((8, n, lanes), f32)
    cots = ((2, 8 * n, wide), f32)

    call(
        part(pack_kernel, sizes),
        v,
        (v.positions, v.tangent, v.embedding),
        dict(),
        dict(
            box=((n, n), f32),
            table=((n, channels + lanes), f32),
            stage=((8, 1, count * channels + lanes), f32),
        ),
        index=(v.send_rows,),
        sent=(devices, 1, count * channels + lanes),
    )
    call(
        part(first_own_kernel, scale, own_chunks),
        v,
        (v.positions, v.tangent, v.neighbours, v.w_one_in, v.w_one_out, v.embedding, v.filter_one, v.filter_two, v.send_rows),
        dict(
            box=((n, n), f32),
            cols=((n, n), f32),
            mask_own=((n, n), f32),
            mask_ghost=((ghosts, n), f32),
            filt_one=((orders, 2 * channels), f32),
            filt_two=((orders, channels), f32),
            geo_own=geometry,
            osc_own=osc,
            phi_own=((n, 2 * channels), f32),
            acc=((8 * n, channels), f32),
        ),
        dict(
            gs=factors(2),
            gv=factors(2),
            wbox=wbox,
            state=state,
            work=((2, 8 * n, wide), pair),
        ),
        near=dict(
            acc_sent=((8 * ghosts, channels), f32),
            cols_sent=((ghosts, n), f32),
            emb_sent=((ghosts, channels), f32),
            wbox_sent=((ghosts, lanes), f32),
            filt_near=((orders, 2 * channels), f32),
            in_near=((channels, channels), f32),
            out_near=((channels, 2 * channels), f32),
        ),
    )
    call(
        part(first_sent_kernel, sizes, ghost_chunks),
        v,
        (
            v.acc_sent,
            v.cols_sent,
            v.emb_sent,
            v.wbox_sent,
            v.filt_near,
            v.in_near,
            v.out_near,
            v.w_left,
            v.w_right,
            v.w_two_in,
            v.w_two_out,
        ),
        dict(
            phi_ghost=((ghosts, 2 * channels), f32),
            coords_ghost=((ghosts, lanes), f32),
        ),
        dict(
            geo=((geo_slots, ghosts, lanes), f32),
            osc=((osc_slots, ghosts, lanes), f32),
            gs=factors(2),
            gv=factors(2),
            state=[((2, ghosts, wide), f32), ((2, ghosts, lanes), f32)],
            work=((2, 8 * ghosts, wide), pair),
            node=((2 * ghosts, channels), f32),
            inner=((2 * ghosts, channels), f32),
            maps=((12 * ghosts, channels), f32),
            table=((ghosts, channels + lanes), f32),
            stage=((ghosts, 2 * channels), f32),
        ),
        raw=(v.arrived,),
        sent=(devices, count, 2 * channels),
    )
    call(
        part(second_own_kernel, own_chunks, ghost_chunks),
        v,
        (
            v.cols,
            v.mask_ghost,
            v.coords_ghost,
            v.phi_ghost,
            v.filt_one,
            v.acc,
            v.w_left,
            v.w_right,
            v.embedding,
            v.w_two_in,
            v.w_two_out,
            v.geo_own,
            v.osc_own,
            v.filt_two,
            v.box,
            v.mask_own,
        ),
        dict(
            geo_ghost=geometry,
            osc_ghost=osc,
            maps=((12 * n, channels), f32),
            node=((2 * n, channels), f32),
            inner=((2 * n, channels), f32),
            phi_two=((n, 2 * channels), f32),
        ),
        dict(
            geo=geometry,
            osc=osc,
            state=state,
            wbox=wbox,
            work_one=((2, 8 * n, wide), pair),
            work=((2, 2 * n, wide), pair),
            gs=factors(2),
            gv=factors(2),
        ),
        near=dict(
            acc_two=((2 * n, channels), f32),
            at_plain=((orders, ghosts, wide), bf16),
            at_dot=((orders, ghosts, wide), bf16),
            a_ghost=((ghost_chunks, 2 * n, wide), pair),
            filt_near=((orders, channels), f32),
        ),
    )
    call(
        part(second_ghost_kernel, sizes, ghost_chunks),
        v,
        (v.filt_near, v.acc_two, v.a_ghost, v.node, v.w_hidden, v.w_energy, v.at_plain, v.at_dot),
        dict(
            cot=((2 * n, channels), f32),
            table=((ghosts, 2 * channels), f32),
        ),
        dict(
            plain=factors(2),
            dotted=factors(2),
            back_ghost=((ghosts, 2 * channels), f32),
        ),
        raw=(v.arrived,),
        scalars=(v.counts,),
        sent=(devices, count, 2 * channels),
    )
    carried = call(
        part(second_back_kernel, own_chunks, ghost_chunks),
        v,
        (v.box, v.cols, v.mask_own, v.filt_two, v.geo_own, v.osc_own, v.phi_two, v.table, v.geo_ghost, v.osc_ghost),
        dict(
            pair_own=((2, n, lanes), f32),
        ),
        dict(
            geo=geometry,
            osc=osc,
            state=state,
            wbox=wbox,
            work=((2, 2 * n, wide), pair),
            plain=factors(2),
            dotted=factors(2),
            pair=((2, n, lanes), f32),
        ),
        near=dict(
            back=((n, 2 * channels), f32),
            pair_ghost=((2, n, lanes), f32),
        ),
        carry=(v.cot, v.send_rows, v.w_two_out, v.inner, v.w_two_in, v.maps),
    )
    call(
        part(first_back_ghost_kernel, sizes, ghost_chunks),
        v,
        (carried.send_rows, v.back, carried.w_two_out, carried.inner, carried.w_two_in, carried.cot, carried.maps, v.w_left, v.w_right, v.phi_ghost, v.filt_one, v.osc_ghost, v.geo_ghost, v.pair_ghost),
        dict(
            bars=((8 * n, channels), pair),
            by_atom=((n, lanes), f32),
        ),
        dict(
            table=((ghosts, 2 * channels), f32),
            by_slot=((8, lanes), f32),
            pair=pairs,
            cots=cots,
            state=state,
            gs=factors(2),
            gv=factors(2),
        ),
        raw=(v.arrived,),
        sent=(devices, 8, lanes),
    )
    call(
        part(first_back_own_kernel, own_chunks),
        v,
        (v.bars, v.phi_own, v.filt_one, v.geo_own, v.osc_own, v.pair_own, v.by_atom, v.send_rows),
        dict(),
        dict(
            atoms=((n, lanes), f32),
            pair=pairs,
            cots=cots,
            state=state,
            gs=factors(2),
            gv=factors(2),
        ),
        near=dict(result=((8, lanes), f32), send_near=((1, ghosts), jnp.int32)),
    )
    call(
        part(finish_kernel, sizes),
        v,
        (v.send_near, v.result),
        dict(forces=((3, n), f32), product=((3, n), f32)),
        dict(table=((64, lanes), f32)),
        raw=(v.arrived,),
    )
    return v.forces.arrays[0], v.product.arrays[0]


def solution(mesh):
    brick = ("bx", "by")
    placed = (
        P(None, brick),
        P(None, brick),
        P(brick, None),
        P(brick),
        P(None, brick),
        P(brick, None),
    ) + (P(),) * 10

    return jax.shard_map(
        per_device,
        mesh=mesh,
        in_specs=placed,
        out_specs=(P(None, brick), P(None, brick)),
        check_vma=False,
    )
```

```python
import functools
import math

import jax
import jax.numpy as jnp
from jax import lax
from jax.experimental import pallas as pl
from jax.experimental.pallas import tpu as pltpu
from jax.sharding import PartitionSpec as P

f32 = jnp.float32
bf16 = jnp.bfloat16
cutoff_radius = 3.0
softening = 0.01
wave = math.pi / cutoff_radius
offsets = ((-1, -1), (-1, 0), (-1, 1), (0, -1), (0, 1), (1, -1), (1, 0), (1, 1))
lanes = 128
wide = 256
row_block = 64
nn_dims = (((1,), (0,)), ((), ()))
nt_dims = (((1,), (1,)), ((), ()))

U, UD, DD, RI = 0, 3, 6, 7
geo_slots = 8
P0, P1, P2, SN, CS = 0, 1, 2, 3, 4
osc_slots = 5
own_group = 2
ghost_group = 5


def split(value):
    high = value.astype(bf16)
    return high, (value - high.astype(f32)).astype(bf16)


def mxu(left, right, dims=nn_dims):
    return lax.dot_general(left, right, dims, preferred_element_type=f32)


def three(lh, ll, rh, rl, dims=nn_dims):
    return mxu(lh, rh, dims) + mxu(ll, rh, dims) + mxu(lh, rl, dims)


def dot3(left, right, dims=nn_dims):
    return three(*split(left), *split(right[...]), dims)


def sigmoid(value):
    return 1.0 / (1.0 + jnp.exp(-jnp.maximum(value, -80.0)))


def silu_parts(value):
    gate = sigmoid(value)
    first = gate * (1.0 + value * (1.0 - gate))
    second = gate * (1.0 - gate) * (2.0 + value * (1.0 - 2.0 * gate))
    return value * gate, first, second


def sin_cos(theta):
    t = jnp.minimum(theta, 6.0) * 0.25
    x = t * t
    s = -1.0 / 39916800.0 + x * (1.0 / 6227020800.0)
    s = 1.0 / 362880.0 + x * s
    s = -1.0 / 5040.0 + x * s
    s = 1.0 / 120.0 + x * s
    s = -1.0 / 6.0 + x * s
    s = t + t * x * s
    c = 1.0 / 479001600.0 - x * (1.0 / 87178291200.0)
    c = -1.0 / 3628800.0 + x * c
    c = 1.0 / 40320.0 + x * c
    c = -1.0 / 720.0 + x * c
    c = 1.0 / 24.0 + x * c
    c = -0.5 + x * c
    c = 1.0 + x * c
    s, c = 2.0 * s * c, 1.0 - 2.0 * s * s
    return 2.0 * s * c, 1.0 - 2.0 * s * s


def doubled(value):
    return jnp.concatenate([value, value], 1)


def fill_geometry(geo, osc, first, second, mask_at, height):
    for start in range(0, height, row_block):
        rows = pl.ds(start, row_block)
        off = [first(i, start) - second(i, start) for i in range(3)]
        move = [first(i + 3, start) - second(i + 3, start) for i in range(3)]
        square = off[0] * off[0] + off[1] * off[1] + off[2] * off[2] + softening
        inverse = lax.rsqrt(square)
        inverse = inverse * (1.5 - 0.5 * square * inverse * inverse)
        theta = wave * (square * inverse)
        unit = [o * inverse for o in off]
        speed = unit[0] * move[0] + unit[1] * move[1] + unit[2] * move[2]
        for i in range(3):
            geo[U + i, rows, :] = unit[i]
            geo[UD + i, rows, :] = (move[i] - unit[i] * speed) * inverse
        sn, cs = sin_cos(theta)
        g0 = (0.5 * cs + 0.5) * inverse
        g1 = ((-0.5 * wave) * sn - g0) * inverse
        g2 = ((-0.5 * wave * wave) * cs - 2.0 * g1) * inverse
        mask = mask_at(start)
        geo[DD, rows, :] = speed
        geo[RI, rows, :] = inverse
        osc[P0, rows, :] = mask * g0
        osc[P1, rows, :] = mask * g1
        osc[P2, rows, :] = mask * g2
        osc[SN, rows, :] = sn
        osc[CS, rows, :] = cs


def start_state(state, osc, height, members):
    waves, turn = state
    near = lanes // members
    group = lax.broadcasted_iota(jnp.int32, (1, lanes), 1) // members
    for start in range(0, height, row_block):
        rows = pl.ds(start, row_block)
        sn, cs = osc[SN, rows, :], osc[CS, rows, :]
        s, c = sn, cs
        for half in range(wide // lanes):
            place = pl.ds(half * lanes, lanes)
            if half:
                s, c = s * cs + c * sn, c * cs - s * sn
            state_s, state_c = s, c
            for i in range(1, near):
                s, c = s * cs + c * sn, c * cs - s * sn
                state_s = jnp.where(group >= i, s, state_s)
                state_c = jnp.where(group >= i, c, state_c)
            waves[0, rows, place] = state_s
            waves[1, rows, place] = state_c
        turn[0, rows, :] = s
        turn[1, rows, :] = c


def order_factor(step, members):
    repeats = wide // members
    group = lax.broadcasted_iota(jnp.int32, (1, wide), 1) // members
    return (group + (step * repeats + 1)).astype(f32) * wave


def rotate(state, rows, s, c):
    waves, turn = state
    rs = doubled(turn[0, rows, :])
    rc = doubled(turn[1, rows, :])
    waves[0, rows, :] = s * rc + c * rs
    waves[1, rows, :] = c * rc - s * rs


def steps(count, members, body, group=None):
    group = group or (own_group if members == lanes else ghost_group)
    if group >= count:
        for step in range(count):
            body(step, step % 2)
        return

    def several(index, carry):
        for place in range(group):
            body(index * group + place, place % 2)
        return carry

    lax.fori_loop(0, count // group, several, 0)


def listed(nbr_ref, start, members):
    slot = lax.broadcasted_iota(jnp.int32, (members, lanes), 0) + start
    found = nbr_ref[0:1, :] == slot
    for k in range(1, nbr_ref.shape[0]):
        found = found | (nbr_ref[k : k + 1, :] == slot)
    return jnp.where(found, 1.0, 0.0).astype(f32)


def fill_mask(wbox, mask):
    wbox[...] = jnp.concatenate([mask] * (lanes // mask.shape[0]), 0).T


def geometry_by_atom(geo, osc, columns, table, wbox):
    table = jnp.concatenate([table] * (lanes // table.shape[1]), 1)
    fill_geometry(
        geo,
        osc,
        lambda i, start: table[i : i + 1, :],
        lambda i, start: columns[start : start + row_block, i : i + 1],
        lambda start: wbox[start : start + row_block, :],
        geo.shape[1],
    )


def picked(place, value):
    high, low = split(value)
    rest = (value - high.astype(f32) - low.astype(f32)).astype(bf16)
    return mxu(place, high) + mxu(place, low) + mxu(place, rest)


def geometry_by_slot(geo, osc, columns, centre, mask):
    fill_geometry(
        geo,
        osc,
        lambda i, start: columns[start : start + row_block, i : i + 1],
        lambda i, start: centre[i : i + 1, :],
        lambda start: mask[start : start + row_block, :],
        mask.shape[0],
    )


def scaled_rows(pair, slot, step, filter_ref, columns, value):
    members = value.shape[0]
    for i in range(wide // members):
        row = filter_ref[pl.ds(step * (wide // members) + i, 1), columns]
        h, l = split(row * value)
        pair[0][slot, i * members : (i + 1) * members, :] = h
        pair[1][slot, i * members : (i + 1) * members, :] = l


def store_pair(pair, value):
    put_split(pair, 0, value)


def put_split(pair, start, value):
    h, l = split(value)
    pair[0][start : start + value.shape[0], :] = h
    pair[1][start : start + value.shape[0], :] = l


def at(pair, index):
    return pair[0].at[index], pair[1].at[index]


def basis_rows(kept, state, geo, osc, step, factor, start, height):
    rows = pl.ds(start, row_block)
    s, c = state[0][0, rows, :], state[0][1, rows, :]
    p0 = doubled(osc[P0, rows, :])
    b = p0 * s
    bd = (doubled(osc[P1, rows, :]) * s + factor * (p0 * c)) * doubled(geo[DD, rows, :])
    put_split(kept, start, b)
    put_split(kept, height + start, bd)
    rotate(state, rows, s, c)
    return b, bd


def first_messages(acc, geo, osc, state, work, scalars, vectors, phi, filt, members, chunks):
    height = geo.shape[1]
    channels = phi.shape[1] // 2
    top = 2 * height
    start_state(state, osc, height, members)

    def chunk(step, slot):
        factor = order_factor(step, members)
        scaled_rows(scalars, slot, step, filt, slice(0, channels), phi[:, :channels])
        scaled_rows(vectors, slot, step, filt, slice(channels, 2 * channels), phi[:, channels:])
        now = at(work, slot)
        for start in range(0, height, row_block):
            rows = pl.ds(start, row_block)
            b, bd = basis_rows(now, state, geo, osc, step, factor, start, height)
            for i in range(3):
                unit = doubled(geo[U + i, rows, :])
                put_split(now, (2 + i) * height + start, unit * b)
                put_split(
                    now, (5 + i) * height + start, doubled(geo[UD + i, rows, :]) * b + unit * bd
                )
        ah, al = now
        acc[:top, :] += three(ah[:top, :], al[:top, :], scalars[0][slot], scalars[1][slot])
        acc[top:, :] += three(ah[top:, :], al[top:, :], vectors[0][slot], vectors[1][slot])

    steps(chunks, members, chunk, chunks)


def second_messages(acc, basis_at, plain, dotted, filt, value, chunks):
    height = acc.shape[0] // 2
    channels = acc.shape[1]

    def chunk(step, slot):
        scaled_rows(plain, slot, step, filt, slice(None), value[:, :channels])
        scaled_rows(dotted, slot, step, filt, slice(None), value[:, channels:])
        ah, al = basis_at(step, slot)
        acc[...] += three(ah[...], al[...], plain[0][slot], plain[1][slot])
        acc[height:, :] += three(
            ah[:height, :], al[:height, :], dotted[0][slot], dotted[1][slot]
        )

    steps(chunks, value.shape[0], chunk)


def plain_basis(kept, geo, osc, state, members, step, height):
    factor = order_factor(step, members)
    for start in range(0, height, row_block):
        basis_rows(kept, state, geo, osc, step, factor, start, height)


def full_basis(geo, osc, state, members, step):
    factor = order_factor(step, members)

    def at_rows(rows):
        s, c = state[0][0, rows, :], state[0][1, rows, :]
        p0, p1 = doubled(osc[P0, rows, :]), doubled(osc[P1, rows, :])
        b = p0 * s
        b1 = p1 * s + factor * (p0 * c)
        b2 = doubled(osc[P2, rows, :]) * s + factor * (2.0 * p1 * c - factor * b)
        rotate(state, rows, s, c)
        return b, b1, b2 * doubled(geo[DD, rows, :])

    return at_rows


def table_cotangents(back, basis_at, plain, dotted, filt, cot, chunks):
    channels = filt.shape[1]
    own_rows = cot.shape[0] // 2
    height = back.shape[0]
    back[...] = jnp.zeros_like(back)

    def chunk(step, slot):
        scaled_rows(plain, slot, step, filt, slice(None), cot[0:own_rows, :])
        scaled_rows(dotted, slot, step, filt, slice(None), cot[own_rows:, :])
        ah, al = basis_at(step, slot)
        both = three(ah[...], al[...], plain[0][slot], plain[1][slot])
        back[:, :channels] += both[:height]
        back[:, channels:] += both[height:] + three(
            ah[:height, :], al[:height, :], dotted[0][slot], dotted[1][slot]
        )

    steps(chunks, own_rows, chunk)


def halved(value):
    return value[:, :lanes] + value[:, lanes:]


def folded(total, members):
    if members < lanes:
        total = total + pltpu.roll(total, members, 1)
    return total


def second_pairs(pair, result, split_cot, basis_at, plain, dotted, filt, value, chunks):
    height = pair.shape[1]
    channels = filt.shape[1]
    pair[...] = jnp.zeros_like(pair)
    ah, al = split_cot

    def chunk(step, slot):
        scaled_rows(plain, slot, step, filt, slice(None), value[:, :channels])
        scaled_rows(dotted, slot, step, filt, slice(None), value[:, channels:])
        both = three(ah[...], al[...], plain[0][slot], plain[1][slot], nt_dims)
        dot = both[height:] + three(
            ah[:height, :], al[:height, :], dotted[0][slot], dotted[1][slot], nt_dims
        )
        basis = basis_at(step)
        for start in range(0, height, row_block):
            rows = pl.ds(start, row_block)
            _, b1, b2d = basis(rows)
            g = both[start : start + row_block]
            pair[0, rows, :] += halved(b1 * g)
            pair[1, rows, :] += halved(b2d * g + b1 * dot[start : start + row_block])

    members = value.shape[0]
    steps(chunks, members, chunk)
    result[0] = folded(pair[0], members)
    result[1] = folded(pair[1], members)


def first_pairs(pair, spaces, split_cot, geo, basis_at, factors_at, members, chunks):
    height = geo.shape[1]
    pair[...] = jnp.zeros_like(pair)
    ch, cl = split_cot
    top = 2 * height

    def chunk(step, slot):
        cots = spaces.at[slot]
        scalars, vectors = factors_at(step, slot)
        cots[:top, :] = three(
            ch[:top, :], cl[:top, :], scalars[0][...], scalars[1][...], nt_dims
        )
        cots[top:, :] = three(
            ch[top:, :], cl[top:, :], vectors[0][...], vectors[1][...], nt_dims
        )
        basis = basis_at(step)
        for start in range(0, height, row_block):
            rows = pl.ds(start, row_block)
            b, b1, b2d = basis(rows)
            b1d = b1 * doubled(geo[DD, rows, :])
            along = cots[start : start + row_block, :]
            along_dot = cots[height + start : height + start + row_block, :]
            for i in range(3):
                place = (2 + i) * height + start
                g = cots[place : place + row_block, :]
                place = (5 + i) * height + start
                gd = cots[place : place + row_block, :]
                unit = doubled(geo[U + i, rows, :])
                along = along + unit * g
                along_dot = along_dot + unit * gd + doubled(geo[UD + i, rows, :]) * g
                pair[2 + i, rows, :] += halved(b * g)
                pair[5 + i, rows, :] += halved(b * gd + b1d * g)
            pair[0, rows, :] += halved(b1 * along)
            pair[1, rows, :] += halved(b2d * along + b1 * along_dot)

    steps(chunks, members, chunk)


def neighbour_id(target, sizes):
    along = lax.axis_index("bx") + target[0]
    across = lax.axis_index("by") + target[1]
    inside = (along >= 0) & (along < sizes[0]) & (across >= 0) & (across < sizes[1])
    device = jnp.clip(along, 0, sizes[0] - 1) * sizes[1] + jnp.clip(across, 0, sizes[1] - 1)
    return device, inside


def send_chunks(r, chunk_at, sizes, beside=lambda: None):
    def each(act):
        for number, target in enumerate(offsets):
            device, inside = neighbour_id(target, sizes)
            copy = pltpu.make_async_copy(chunk_at(number), r.out.at[device], r.moves.at[number])

            @pl.when(inside)
            def _():
                act(copy)

    each(lambda copy: copy.start())
    beside()
    each(lambda copy: copy.wait())


def send_groups(r, table, sizes):
    count = r.out.shape[1]
    send_chunks(r, lambda number: table.at[number * count : (number + 1) * count, :], sizes)


def send_gathered(r, table, stage, send_ref, sizes):
    for slot in range(stage.shape[0]):
        stage[slot : slot + 1, :] = table[pl.ds(send_ref[0, slot], 1), :]
    send_groups(r, stage, sizes)


def receive(r, table, sizes):
    count = r.arrived.shape[1]
    for number, target in enumerate(offsets):
        device, inside = neighbour_id(target, sizes)

        @pl.when(inside)
        def _():
            table[number * count : (number + 1) * count, :] = r.arrived[device]


def add_returned(total, table, send_row):
    atom = lax.broadcasted_iota(jnp.int32, (total.shape[0], table.shape[0]), 0)
    place = jnp.where(atom == send_row, 1.0, 0.0).astype(bf16)
    high, low = split(table[...])
    rest = (table[...] - high.astype(f32) - low.astype(f32)).astype(bf16)
    total[...] += mxu(place, high) + mxu(place, low) + mxu(place, rest)


def offset_gradients(geo, pair, second, members):
    near = [folded(pair[i], members) for i in range(8)]
    units = [geo[U + i, :, :lanes] for i in range(3)]
    moves = [geo[UD + i, :, :lanes] for i in range(3)]
    inverse = geo[RI, :, :lanes]
    speed = geo[DD, :, :lanes]
    along = near[0] + second[0]
    along_dot = near[1] + second[1]
    turn, turn_dot = near[2:5], near[5:8]
    inner = units[0] * turn[0] + units[1] * turn[1] + units[2] * turn[2]
    inner_dot = sum(units[i] * turn_dot[i] + moves[i] * turn[i] for i in range(3))
    rate = speed * inverse
    grads, dots = [], []
    for i in range(3):
        part = (turn[i] - units[i] * inner) * inverse
        grad = along * units[i] + part
        grad_dot = (
            along_dot * units[i]
            + along * moves[i]
            + (turn_dot[i] - moves[i] * inner - units[i] * inner_dot) * inverse
            - rate * part
        )
        grads.append(grad)
        dots.append(grad_dot)
    return grads + dots


def slot_sums(by_slot, values):
    by_slot[...] = jnp.zeros_like(by_slot)
    for row, value in enumerate(values):
        by_slot[row : row + 1, :] = jnp.sum(value, 0, keepdims=True)


def atom_sums(by_atom, values, members):
    lane = lax.broadcasted_iota(jnp.int32, (1, lanes), 1)
    sums = jnp.zeros(by_atom.shape, f32)
    for row, value in enumerate(values):
        if members < lanes:
            value = jnp.where(lane < members, value, 0.0)
        sums = jnp.where(lane == row, -jnp.sum(value, 1, keepdims=True), sums)
    by_atom[...] = sums


def pack_kernel(sizes, r):
    channels = r.embedding.shape[1]
    r.box[...] = jnp.zeros_like(r.box)
    r.need(r.positions, r.tangent)
    r.box[0:3, :] = r.positions[...]
    r.box[3:6, :] = r.tangent[...]
    r.table[:, channels:] = r.box[...].T
    r.need(r.embedding)
    r.table[:, :channels] = r.embedding[...]
    r.need(r.send_rows)
    count = r.send_rows.shape[1] // 8
    gap = lanes // count
    for number in range(8):
        ends = jnp.zeros((1, lanes), f32)
        for p in range(count):
            row = r.table[pl.ds(r.send_rows[0, number * count + p], 1), :]
            r.stage[number, :, p * channels : (p + 1) * channels] = row[:, :channels]
            end = row[:, channels:]
            ends = ends + (pltpu.roll(end, p * gap, 1) if p else end)
        r.stage[number, :, count * channels :] = ends
    send_chunks(r, lambda number: r.stage.at[number], sizes)


def projected(features, inner, outer):
    middle = silu_parts(three(*split(features), inner[0][...], inner[1][...]))[0]
    return three(*split(middle), outer[0][...], outer[1][...])


def first_own_kernel(scale, chunks, r):
    own_rows = r.positions.shape[1]
    ghosts = r.mask_ghost.shape[0]
    r.box[...] = jnp.zeros_like(r.box)
    r.need(r.positions, r.tangent, r.neighbours)
    r.box[0:3, :] = r.positions[...]
    r.box[3:6, :] = r.tangent[...]
    r.cols[...] = r.box[...].T
    r.mask_own[...] = listed(r.neighbours, 0, own_rows)
    r.mask_ghost[...] = listed(r.neighbours, own_rows, ghosts)
    r.put(r.box, r.cols, r.mask_own, r.mask_ghost)
    fill_mask(r.wbox, r.mask_own[...])
    geometry_by_atom(r.geo_own, r.osc_own, r.cols[...], r.box[...], r.wbox)
    r.put(r.geo_own, r.osc_own)
    r.need(r.w_one_in, r.w_one_out, r.embedding, r.filter_one, r.filter_two, r.send_rows)
    r.filt_one[...] = r.filter_one[...] * scale
    r.filt_two[...] = r.filter_two[...] * scale
    r.put(r.filt_one, r.filt_two)
    r.filt_near[...] = r.filt_one[...]
    store_pair(r.in_near, r.w_one_in[...])
    store_pair(r.out_near, r.w_one_out[...])
    r.phi_own[...] = projected(r.embedding[...], r.in_near, r.out_near)
    r.put(r.phi_own)
    r.acc[...] = jnp.zeros_like(r.acc)
    first_messages(
        r.acc,
        r.geo_own,
        r.osc_own,
        r.state,
        r.work,
        r.gs,
        r.gv,
        r.phi_own,
        r.filt_one,
        own_rows,
        chunks,
    )
    r.put(r.acc)
    sent = jnp.concatenate([r.send_rows[...]] * (own_rows // ghosts), 1)
    atom = lax.broadcasted_iota(jnp.int32, (own_rows, own_rows), 0)
    place = jnp.where(atom == sent, 1.0, 0.0).astype(f32).T[:ghosts].astype(bf16)
    r.cols_sent[...] = picked(place, r.cols[...])
    r.emb_sent[...] = picked(place, r.embedding[...])
    fill_mask(r.wbox, r.mask_ghost[...])
    r.wbox_sent[...] = mxu(place, r.wbox[...].astype(bf16))
    for i in range(8):
        r.acc_sent[i * ghosts : (i + 1) * ghosts, :] = picked(
            place, r.acc[i * own_rows : (i + 1) * own_rows, :]
        )


def node_states(acc, embedding, maps, node, inner, w_left, w_right, w_two_in, w_two_out):
    rows = embedding.shape[0]
    top = 2 * rows
    half = 3 * rows
    ah, al = split(acc[top:, :])
    maps[0 : 2 * half, :] = three(ah, al, *split(w_left[...]))
    maps[2 * half :, :] = three(ah, al, *split(w_right[...]))
    total = embedding[...] + acc[0:rows, :]
    moved = acc[rows:top, :]
    for i in range(3):
        a, b = i * rows, (i + 1) * rows
        left, left_dot = maps[a:b, :], maps[half + a : half + b, :]
        right = maps[2 * half + a : 2 * half + b, :]
        right_dot = maps[3 * half + a : 3 * half + b, :]
        total = total + left * right
        moved = moved + left_dot * right + left * right_dot
    node[0:rows, :] = total
    node[rows:, :] = moved
    inner[...] = dot3(node[...], w_two_in)
    value, slope, _ = silu_parts(inner[0:rows, :])
    outer = dot3(jnp.concatenate([value, slope * inner[rows:, :]], 0), w_two_out)
    return outer[:rows], outer[rows:]


def first_sent_kernel(sizes, chunks, r):
    channels = r.emb_sent.shape[1]
    r.table[...] = jnp.zeros_like(r.table)
    members = r.table.shape[0]
    count = members // 8
    gap = lanes // count
    for number, target in enumerate(offsets):
        device, inside = neighbour_id(target, sizes)

        @pl.when(inside)
        def _():
            chunk = r.arrived[device]
            ends = chunk[:, count * channels :]
            for p in range(count):
                at_row = slice(number * count + p, number * count + p + 1)
                r.table[at_row, :channels] = chunk[:, p * channels : (p + 1) * channels]
                r.table[at_row, channels:] = pltpu.roll(ends, lanes - p * gap, 1) if p else ends

    r.coords_ghost[...] = r.table[:, channels:]
    r.put(r.coords_ghost)
    r.phi_ghost[...] = projected(r.table[:, :channels], r.in_near, r.out_near)
    r.put(r.phi_ghost)
    geometry_by_atom(
        r.geo, r.osc, r.cols_sent[...], ghost_lanes(r.coords_ghost), r.wbox_sent
    )
    first_messages(
        r.acc_sent,
        r.geo,
        r.osc,
        r.state,
        r.work,
        r.gs,
        r.gv,
        r.phi_ghost,
        r.filt_near,
        members,
        chunks,
    )
    r.need(r.w_left, r.w_right, r.w_two_in, r.w_two_out)
    plain, dotted = node_states(
        r.acc_sent,
        r.emb_sent,
        r.maps,
        r.node,
        r.inner,
        r.w_left,
        r.w_right,
        r.w_two_in,
        r.w_two_out,
    )
    r.stage[:, :channels] = plain
    r.stage[:, channels:] = dotted
    send_groups(r, r.stage, sizes)


def ghost_lanes(coords):
    members = coords.shape[0]
    return jnp.concatenate([coords[...]] * (lanes // members), 0).T[:, :members]


def second_own_kernel(chunks, ghost_chunks, r):
    own_rows = r.mask_own.shape[0]
    ghosts = r.mask_ghost.shape[0]
    channels = r.embedding.shape[1]
    r.need(r.cols, r.mask_ghost, r.coords_ghost)
    fill_mask(r.wbox, r.mask_ghost[...])
    geometry_by_atom(
        r.geo_ghost, r.osc_ghost, r.cols[...], ghost_lanes(r.coords_ghost), r.wbox
    )
    r.put(r.geo_ghost, r.osc_ghost)
    r.need(r.phi_ghost, r.filt_one, r.acc)
    first_messages(
        r.acc,
        r.geo_ghost,
        r.osc_ghost,
        r.state,
        r.work_one,
        r.gs,
        r.gv,
        r.phi_ghost,
        r.filt_one,
        ghosts,
        ghost_chunks,
    )
    r.need(r.w_left, r.w_right, r.w_two_in, r.w_two_out, r.embedding)
    plain, dotted = node_states(
        r.acc,
        r.embedding,
        r.maps,
        r.node,
        r.inner,
        r.w_left,
        r.w_right,
        r.w_two_in,
        r.w_two_out,
    )
    r.phi_two[:, :channels] = plain
    r.phi_two[:, channels:] = dotted
    r.put(r.node, r.maps, r.inner, r.phi_two)
    r.acc_two[...] = jnp.zeros_like(r.acc_two)
    r.need(r.geo_own, r.osc_own, r.filt_two)
    r.filt_near[...] = r.filt_two[...]
    start_state(r.state, r.osc_own, own_rows, own_rows)

    def own_basis(step, slot):
        kept = at(r.work, slot)
        plain_basis(kept, r.geo_own, r.osc_own, r.state, own_rows, step, own_rows)
        return kept

    second_messages(r.acc_two, own_basis, r.gs, r.gv, r.filt_two, r.phi_two, chunks)
    r.need(r.box)
    geometry_by_slot(r.geo, r.osc, r.coords_ghost[...], r.box[...], r.mask_ghost[...])
    start_state(r.state, r.osc, ghosts, own_rows)

    def slot_rows(step, slot):
        kept = at(r.work, slot)
        plain_basis(kept, r.geo, r.osc, r.state, own_rows, step, ghosts)
        for i in range(wide // lanes):
            part = slice(i * lanes, (i + 1) * lanes)
            order = step * (wide // lanes) + i
            for half, place in zip(kept, (slice(0, lanes), slice(lanes, wide))):
                r.at_plain[order, :, place] = half[0:ghosts, part]
                r.at_dot[order, :, place] = half[ghosts : 2 * ghosts, part]

    steps(chunks, own_rows, slot_rows)
    start_state(r.state, r.osc_ghost, own_rows, ghosts)
    steps(
        ghost_chunks,
        ghosts,
        lambda step, slot: plain_basis(
            at(r.a_ghost, step), r.geo_ghost, r.osc_ghost, r.state, ghosts, step, own_rows
        ),
    )


def ghost_cotangents(back, plain, dotted, filt, cot):
    orders, height, _ = plain.shape
    own_rows = cot.shape[0] // 2
    channels = cot.shape[1]
    beside = jnp.concatenate([cot[0:own_rows, :], cot[own_rows:, :]], 1)
    high, low = split(beside)
    both = jnp.concatenate([high, high], 0)
    rest = jnp.concatenate([low, jnp.zeros_like(low)], 0)
    together = orders // 4
    value = jnp.zeros((height, channels), f32)
    moved = jnp.zeros((height, channels), f32)
    for start in range(0, orders, together):
        rows = plain[start : start + together].reshape(together * height, wide)
        first = mxu(rows, both) + mxu(rows, rest)
        rows = dotted[start : start + together].reshape(together * height, wide)
        second = first[:, channels:] + (
            mxu(rows, both[:, :channels]) + mxu(rows, rest[:, :channels])
        )
        for i in range(together):
            weight = filt[start + i : start + i + 1, :]
            value = value + weight * first[i * height : (i + 1) * height, :channels]
            moved = moved + weight * second[i * height : (i + 1) * height, :]
    back[:, :channels] = value
    back[:, channels:] = moved


def second_ghost_kernel(sizes, ghost_chunks, r):
    own_rows = r.node.shape[0] // 2
    r.table[...] = jnp.zeros_like(r.table)
    receive(r, r.table, sizes)
    r.put(r.table)

    second_messages(
        r.acc_two,
        lambda step, slot: at(r.a_ghost, step),
        r.plain,
        r.dotted,
        r.filt_near,
        r.table,
        ghost_chunks,
    )
    r.need(r.node, r.w_hidden, r.w_energy)
    hidden = dot3(r.node[...] + r.acc_two[...], r.w_hidden)
    _, slope, bend = silu_parts(hidden[:own_rows])
    live = lax.broadcasted_iota(jnp.int32, (own_rows, 1), 0) < r.counts[0]
    weight = jnp.where(live, r.w_energy[...], 0.0)
    bars = jnp.concatenate([weight * slope, weight * bend * hidden[own_rows:]], 0)
    r.cot[...] = dot3(bars, r.w_hidden, nt_dims)
    r.put(r.cot)
    ghost_cotangents(r.back_ghost, r.at_plain, r.at_dot, r.filt_near, r.cot)
    send_groups(r, r.back_ghost, sizes)


def second_back_kernel(chunks, ghost_chunks, r):
    own_rows = r.mask_own.shape[0]
    r.need(r.box, r.cols, r.mask_own)
    geometry_by_slot(r.geo, r.osc, r.cols[...], r.box[...], r.mask_own[...])
    r.need(r.cot, r.filt_two)

    start_state(r.state, r.osc, own_rows, own_rows)

    def slot_basis(step, slot):
        kept = at(r.work, slot)
        plain_basis(kept, r.geo, r.osc, r.state, own_rows, step, own_rows)
        return kept

    table_cotangents(r.back, slot_basis, r.plain, r.dotted, r.filt_two, r.cot, chunks)
    split_cot = at(r.work, 0)
    put_split(split_cot, 0, r.cot[...])
    r.need(r.geo_own, r.osc_own, r.phi_two)

    start_state(r.state, r.osc_own, own_rows, own_rows)

    second_pairs(
        r.pair,
        r.pair_own,
        split_cot,
        lambda step: full_basis(r.geo_own, r.osc_own, r.state, own_rows, step),
        r.plain,
        r.dotted,
        r.filt_two,
        r.phi_two,
        chunks,
    )
    r.put(r.pair_own)
    r.need(r.table, r.geo_ghost, r.osc_ghost)
    ghosts = r.table.shape[0]
    start_state(r.state, r.osc_ghost, own_rows, ghosts)


    second_pairs(
        r.pair,
        r.pair_ghost,
        split_cot,
        lambda step: full_basis(r.geo_ghost, r.osc_ghost, r.state, ghosts, step),
        r.plain,
        r.dotted,
        r.filt_two,
        r.table,
        ghost_chunks,
    )


def pairs_again(r, geo, osc, phi, chunks):
    members = phi.shape[0]
    channels = phi.shape[1] // 2
    start_state(r.state, osc, geo.shape[1], members)

    def basis_at(step):
        return full_basis(geo, osc, r.state, members, step)

    def factors_at(step, slot):
        scaled_rows(r.gs, slot, step, r.filt_one, slice(0, channels), phi[:, :channels])
        scaled_rows(r.gv, slot, step, r.filt_one, slice(channels, None), phi[:, channels:])
        return at(r.gs, slot), at(r.gv, slot)

    first_pairs(r.pair, r.cots, r.bars, geo, basis_at, factors_at, members, chunks)


def first_back_ghost_kernel(sizes, chunks, r):
    own_rows = r.back.shape[0]
    channels = r.back.shape[1] // 2
    r.table[...] = jnp.zeros_like(r.table)
    receive(r, r.table, sizes)
    add_returned(r.back, r.table, r.send_rows[...])
    outer = dot3(
        jnp.concatenate([r.back[:, :channels], r.back[:, channels:]], 0), r.w_two_out, nt_dims
    )
    _, slope, bend = silu_parts(r.inner[:own_rows, :])
    pulled = jnp.concatenate(
        [
            outer[:own_rows] * slope,
            outer[own_rows:] * slope + outer[:own_rows] * bend * r.inner[own_rows:, :],
        ],
        0,
    )
    bars = r.cot[...] + dot3(pulled, r.w_two_in, nt_dims)
    put_split(r.bars, 0, bars)
    half = 3 * own_rows
    maps = r.maps
    bar, bar_dot = bars[0:own_rows], bars[own_rows:]
    r.need(r.w_left, r.w_right)
    for i in range(3):
        a, b = i * own_rows, (i + 1) * own_rows
        left, left_dot = maps[a:b, :], maps[half + a : half + b, :]
        right = maps[2 * half + a : 2 * half + b, :]
        right_dot = maps[3 * half + a : 3 * half + b, :]
        for_left = jnp.concatenate([bar * right, bar_dot * right + bar * right_dot], 0)
        for_right = jnp.concatenate([bar * left, bar_dot * left + bar * left_dot], 0)
        both = dot3(for_left, r.w_left, nt_dims) + dot3(for_right, r.w_right, nt_dims)
        put_split(r.bars, (2 + i) * own_rows, both[:own_rows])
        put_split(r.bars, (5 + i) * own_rows, both[own_rows:])
    r.put(r.bars)
    r.need(r.geo_ghost, r.osc_ghost, r.phi_ghost, r.filt_one)
    pairs_again(r, r.geo_ghost, r.osc_ghost, r.phi_ghost, chunks)
    members = r.table.shape[0]
    values = offset_gradients(r.geo_ghost, r.pair, r.pair_ghost, members)
    slot_sums(r.by_slot, values)

    def beside():
        atom_sums(r.by_atom, values, members)
        r.put(r.by_atom)

    send_chunks(r, lambda number: r.by_slot, sizes, beside)


def first_back_own_kernel(chunks, r):
    own_rows = r.by_atom.shape[0]
    r.need(r.phi_own, r.filt_one, r.geo_own, r.osc_own, r.bars)
    pairs_again(r, r.geo_own, r.osc_own, r.phi_own, chunks)
    r.need(r.pair_own, r.by_atom)
    values = offset_gradients(r.geo_own, r.pair, r.pair_own, own_rows)
    slot_sums(r.result, values)
    atom_sums(r.atoms, values, own_rows)
    r.result[...] += (r.atoms[...] + r.by_atom[...]).T[0:8, :]
    r.need(r.send_rows)
    r.send_near[...] = r.send_rows[...]


def finish_kernel(sizes, r):
    count = r.send_near.shape[1] // 8
    own_rows = r.result.shape[1]
    r.table[...] = jnp.zeros_like(r.table)
    receive(r, r.table, sizes)
    lane = lax.broadcasted_iota(jnp.int32, (1, lanes), 1)
    atom = lax.broadcasted_iota(jnp.int32, (own_rows, 8 * count), 0)
    place = jnp.where(atom == r.send_near[...], 1.0, 0.0).astype(bf16)
    rows = jnp.zeros((8, lanes), f32)
    for number in range(8):
        shift = ((2 * number - 7) * count) % lanes
        moved = r.table[8 * number : 8 * number + 8, :]
        if shift:
            moved = pltpu.roll(moved, shift, 1)
        mine = (lane >= number * count) & (lane < (number + 1) * count)
        rows = jnp.where(mine, moved, rows)
    value = rows[:, : 8 * count]
    high, low = split(value)
    rest = (value - high.astype(f32) - low.astype(f32)).astype(bf16)
    total = r.result[...] + mxu(high, place, nt_dims) + mxu(low, place, nt_dims)
    total = total + mxu(rest, place, nt_dims)
    r.forces[...] = -total[0:3, :]
    r.product[...] = -total[3:6, :]
    r.put(r.forces, r.product)


class Refs:
    def need(self, *buffers):
        for buffer in buffers:
            for copy in self.loads.pop(id(buffer), ()):
                copy.wait()

    def put(self, *buffers):
        for buffer in buffers:
            for copy in self.stores[id(buffer)]:
                copy.start()
                self.started.append(copy)

    def close(self):
        for copy in [copy for group in self.loads.values() for copy in group] + self.started:
            copy.wait()


def as_tuple(value):
    return value if isinstance(value, tuple) else (value,)


def flat(entry):
    if isinstance(entry, list):
        return entry
    return [(entry[0], kind) for kind in as_tuple(entry[1])]


class Slot:
    def __init__(self, name, value):
        self.name, self.arrays, self.near = name, as_tuple(value), False


class Slots:
    def __setattr__(self, name, value):
        object.__setattr__(self, name, Slot(name, value))


def call(kernel, v, loads, outs, scratch, index=(), raw=(), scalars=(), sent=(), near=None, carry=()):
    near = near or dict()
    raw = raw + tuple(slot for slot in loads if slot.near)
    loads = tuple(slot for slot in loads if not slot.near)
    args, kinds, shapes, buffers = [], [], [], []
    copied = [(slot, pltpu.VMEM) for slot in loads] + [(slot, pltpu.SMEM) for slot in index]
    copies = 0
    for slot, space in copied:
        for array in slot.arrays:
            args.append(pltpu.with_memory_space_constraint(array, pltpu.HBM))
            kinds.append(pl.BlockSpec(memory_space=pltpu.HBM))
            buffers.append(space(array.shape, array.dtype))
            copies += 1
    for slot in raw + scalars:
        for array in slot.arrays:
            args.append(array)
            kinds.append(pl.BlockSpec(memory_space=pltpu.VMEM if slot in raw else pltpu.SMEM))
    for shape, types in outs.values():
        for kind in as_tuple(types):
            shapes.append(pltpu.HBM(shape, kind))
            buffers.append(pltpu.VMEM(shape, kind))
            copies += 1
    places = [pltpu.HBM] * len(shapes)
    for slot in carry:
        array = slot.arrays[0]
        args.append(pltpu.with_memory_space_constraint(array, pltpu.HBM))
        kinds.append(pl.BlockSpec(memory_space=pltpu.HBM))
        shapes.append(jax.ShapeDtypeStruct(array.shape, array.dtype))
        places.append(pltpu.VMEM)
        copies += 1
    for entry in near.values():
        for shape, kind in flat(entry):
            shapes.append(jax.ShapeDtypeStruct(shape, kind))
            places.append(pltpu.VMEM)
    if sent:
        shapes.append(pltpu.HBM(sent, f32))
        places.append(pltpu.HBM)
    for entry in scratch.values():
        for shape, kind in flat(entry):
            buffers.append(pltpu.VMEM(shape, kind))
    buffers.append(pltpu.SemaphoreType.DMA((copies + 1,)))
    buffers.append(pltpu.SemaphoreType.DMA((8,)))

    def run(*refs):
        r = Refs()
        r.loads, r.stores, r.started = {}, {}, []
        ins, refs = refs[: len(args)], refs[len(args) :]
        targets, refs = refs[: len(shapes)], list(refs[len(shapes) :])
        ins, targets = list(ins), list(targets)
        r.moves = refs[-1]
        sems = [refs[-2].at[number] for number in range(copies)]

        def taken(name, number):
            group = tuple(refs.pop(0) for _ in range(number))
            value = group if number > 1 else group[0]
            setattr(r, name, value)
            return group, id(value)

        for slot, _ in copied:
            group, key = taken(slot.name, len(slot.arrays))
            r.loads[key] = []
            for buffer in group:
                copy = pltpu.make_async_copy(ins.pop(0), buffer, sems.pop(0))
                copy.start()
                r.loads[key].append(copy)
        for slot in raw + scalars:
            group = tuple(ins.pop(0) for _ in slot.arrays)
            setattr(r, slot.name, group if len(group) > 1 else group[0])
        for name, (shape, types) in outs.items():
            group, key = taken(name, len(as_tuple(types)))
            r.stores[key] = []
            for buffer in group:
                copy = pltpu.make_async_copy(buffer, targets.pop(0), sems.pop(0))
                r.stores[key].append(copy)
        for slot in carry:
            buffer = targets.pop(0)
            setattr(r, slot.name, buffer)
            copy = pltpu.make_async_copy(ins.pop(0), buffer, sems.pop(0))
            copy.start()
            r.loads[id(buffer)] = [copy]
        for name, entry in near.items():
            group = tuple(targets.pop(0) for _ in flat(entry))
            setattr(r, name, group if len(group) > 1 else group[0])
        if sent:
            r.out = targets.pop(0)
        for name, entry in scratch.items():
            taken(name, len(flat(entry)))
        kernel(r)
        r.close()

    results = pl.pallas_call(
        run,
        out_shape=shapes,
        in_specs=kinds,
        out_specs=[pl.BlockSpec(memory_space=place) for place in places],
        scratch_shapes=buffers,
        compiler_params=pltpu.CompilerParams(vmem_limit_bytes=20 * 1024 * 1024),
        name=kernel.func.__name__,
    )(*args)
    results = list(results)
    for name, (shape, types) in outs.items():
        group = tuple(results.pop(0) for _ in as_tuple(types))
        setattr(v, name, group)
    carried = Slots()
    for slot in carry:
        setattr(carried, slot.name, results.pop(0))
        getattr(carried, slot.name).near = True
    for name, entry in near.items():
        setattr(v, name, tuple(results.pop(0) for _ in flat(entry)))
        getattr(v, name).near = True
    if sent:
        v.arrived = exchanged(results.pop(0))
    return carried


def exchanged(buffer):
    return lax.all_to_all(buffer, ("bx", "by"), 0, 0)


def per_device(
    positions,
    tangent,
    embedding,
    counts,
    neighbours,
    send_rows,
    w_one_in,
    w_one_out,
    filter_one,
    w_left,
    w_right,
    w_two_in,
    w_two_out,
    filter_two,
    w_hidden,
    w_energy,
):
    w_energy = w_energy.reshape(1, w_energy.shape[0])
    v = Slots()
    for name, value in tuple(locals().items()):
        if value is not v:
            setattr(v, name, value)
    sizes = (lax.axis_size("bx"), lax.axis_size("by"))
    devices = sizes[0] * sizes[1]
    n = positions.shape[1]
    channels = embedding.shape[1]
    ghosts = send_rows.shape[1]
    orders = filter_one.shape[0]
    count = ghosts // 8
    scale = 1.0 / math.sqrt(neighbours.shape[0])
    part = functools.partial
    pair = (bf16, bf16)
    own_chunks, ghost_chunks = orders * n // wide, orders * ghosts // wide

    def factors(chunks):
        return ((chunks, wide, channels), pair)

    geometry = ((geo_slots, n, lanes), f32)
    osc = ((osc_slots, n, lanes), f32)
    state = [((2, n, wide), f32), ((2, n, lanes), f32)]
    wbox = ((n, lanes), f32)
    pairs = ((8, n, lanes), f32)
    cots = ((2, 8 * n, wide), f32)

    call(
        part(pack_kernel, sizes),
        v,
        (v.positions, v.tangent, v.embedding),
        dict(),
        dict(
            box=((n, n), f32),
            table=((n, channels + lanes), f32),
            stage=((8, 1, count * channels + lanes), f32),
        ),
        index=(v.send_rows,),
        sent=(devices, 1, count * channels + lanes),
    )
    call(
        part(first_own_kernel, scale, own_chunks),
        v,
        (v.positions, v.tangent, v.neighbours, v.w_one_in, v.w_one_out, v.embedding, v.filter_one, v.filter_two, v.send_rows),
        dict(
            box=((n, n), f32),
            cols=((n, n), f32),
            mask_own=((n, n), f32),
            mask_ghost=((ghosts, n), f32),
            filt_one=((orders, 2 * channels), f32),
            filt_two=((orders, channels), f32),
            geo_own=geometry,
            osc_own=osc,
            phi_own=((n, 2 * channels), f32),
            acc=((8 * n, channels), f32),
        ),
        dict(
            gs=factors(2),
            gv=factors(2),
            wbox=wbox,
            state=state,
            work=((2, 8 * n, wide), pair),
        ),
        near=dict(
            acc_sent=((8 * ghosts, channels), f32),
            cols_sent=((ghosts, n), f32),
            emb_sent=((ghosts, channels), f32),
            wbox_sent=((ghosts, lanes), f32),
            filt_near=((orders, 2 * channels), f32),
            in_near=((channels, channels), pair),
            out_near=((channels, 2 * channels), pair),
        ),
    )
    call(
        part(first_sent_kernel, sizes, ghost_chunks),
        v,
        (
            v.acc_sent,
            v.cols_sent,
            v.emb_sent,
            v.wbox_sent,
            v.filt_near,
            v.in_near,
            v.out_near,
            v.w_left,
            v.w_right,
            v.w_two_in,
            v.w_two_out,
        ),
        dict(
            phi_ghost=((ghosts, 2 * channels), f32),
            coords_ghost=((ghosts, lanes), f32),
        ),
        dict(
            geo=((geo_slots, ghosts, lanes), f32),
            osc=((osc_slots, ghosts, lanes), f32),
            gs=factors(2),
            gv=factors(2),
            state=[((2, ghosts, wide), f32), ((2, ghosts, lanes), f32)],
            work=((2, 8 * ghosts, wide), pair),
            node=((2 * ghosts, channels), f32),
            inner=((2 * ghosts, channels), f32),
            maps=((12 * ghosts, channels), f32),
            table=((ghosts, channels + lanes), f32),
            stage=((ghosts, 2 * channels), f32),
        ),
        raw=(v.arrived,),
        sent=(devices, count, 2 * channels),
    )
    call(
        part(second_own_kernel, own_chunks, ghost_chunks),
        v,
        (
            v.cols,
            v.mask_ghost,
            v.coords_ghost,
            v.phi_ghost,
            v.filt_one,
            v.acc,
            v.w_left,
            v.w_right,
            v.embedding,
            v.w_two_in,
            v.w_two_out,
            v.geo_own,
            v.osc_own,
            v.filt_two,
            v.box,
            v.mask_own,
        ),
        dict(
            geo_ghost=geometry,
            osc_ghost=osc,
            maps=((12 * n, channels), f32),
            node=((2 * n, channels), f32),
            inner=((2 * n, channels), f32),
            phi_two=((n, 2 * channels), f32),
        ),
        dict(
            geo=geometry,
            osc=osc,
            state=state,
            wbox=wbox,
            work_one=((2, 8 * n, wide), pair),
            work=((2, 2 * n, wide), pair),
            gs=factors(2),
            gv=factors(2),
        ),
        near=dict(
            acc_two=((2 * n, channels), f32),
            at_plain=((orders, ghosts, wide), bf16),
            at_dot=((orders, ghosts, wide), bf16),
            a_ghost=((ghost_chunks, 2 * n, wide), pair),
            filt_near=((orders, channels), f32),
        ),
    )
    call(
        part(second_ghost_kernel, sizes, ghost_chunks),
        v,
        (v.filt_near, v.acc_two, v.a_ghost, v.node, v.w_hidden, v.w_energy, v.at_plain, v.at_dot),
        dict(
            cot=((2 * n, channels), f32),
            table=((ghosts, 2 * channels), f32),
        ),
        dict(
            plain=factors(2),
            dotted=factors(2),
            back_ghost=((ghosts, 2 * channels), f32),
        ),
        raw=(v.arrived,),
        scalars=(v.counts,),
        sent=(devices, count, 2 * channels),
    )
    carried = call(
        part(second_back_kernel, own_chunks, ghost_chunks),
        v,
        (v.box, v.cols, v.mask_own, v.filt_two, v.geo_own, v.osc_own, v.phi_two, v.table, v.geo_ghost, v.osc_ghost),
        dict(
            pair_own=((2, n, lanes), f32),
        ),
        dict(
            geo=geometry,
            osc=osc,
            state=state,
            wbox=wbox,
            work=((2, 2 * n, wide), pair),
            plain=factors(2),
            dotted=factors(2),
            pair=((2, n, lanes), f32),
        ),
        near=dict(
            back=((n, 2 * channels), f32),
            pair_ghost=((2, n, lanes), f32),
        ),
        carry=(v.cot, v.send_rows, v.w_two_out, v.inner, v.w_two_in, v.maps),
    )
    call(
        part(first_back_ghost_kernel, sizes, ghost_chunks),
        v,
        (carried.send_rows, v.back, carried.w_two_out, carried.inner, carried.w_two_in, carried.cot, carried.maps, v.w_left, v.w_right, v.phi_ghost, v.filt_one, v.osc_ghost, v.geo_ghost, v.pair_ghost),
        dict(
            bars=((8 * n, channels), pair),
            by_atom=((n, lanes), f32),
        ),
        dict(
            table=((ghosts, 2 * channels), f32),
            by_slot=((8, lanes), f32),
            pair=pairs,
            cots=cots,
            state=state,
            gs=factors(2),
            gv=factors(2),
        ),
        raw=(v.arrived,),
        sent=(devices, 8, lanes),
    )
    call(
        part(first_back_own_kernel, own_chunks),
        v,
        (v.bars, v.phi_own, v.filt_one, v.geo_own, v.osc_own, v.pair_own, v.by_atom, v.send_rows),
        dict(),
        dict(
            atoms=((n, lanes), f32),
            pair=pairs,
            cots=cots,
            state=state,
            gs=factors(2),
            gv=factors(2),
        ),
        near=dict(result=((8, lanes), f32), send_near=((1, ghosts), jnp.int32)),
    )
    call(
        part(finish_kernel, sizes),
        v,
        (v.send_near, v.result),
        dict(forces=((3, n), f32), product=((3, n), f32)),
        dict(table=((64, lanes), f32)),
        raw=(v.arrived,),
    )
    return v.forces.arrays[0], v.product.arrays[0]


def solution(mesh):
    brick = ("bx", "by")
    placed = (
        P(None, brick),
        P(None, brick),
        P(brick, None),
        P(brick),
        P(None, brick),
        P(brick, None),
    ) + (P(),) * 10

    return jax.shard_map(
        per_device,
        mesh=mesh,
        in_specs=placed,
        out_specs=(P(None, brick), P(None, brick)),
        check_vma=False,
    )
```
